256 devices in a mesh: dp: 16 (over x_lo, z), ctx: 16 (over y, x_hi, core).
Axes of the slice: x: 4 (x_hi: 2, x_lo: 2; x = x_hi * 2 + x_lo), y: 4, z: 8, core: 2. Of those that a mesh axis runs over, the one named last changes fastest.
Arguments:
- queries: bfloat16 [32768, 3072], P(('dp', 'ctx')), may hold values from -6 to 6
- keys: bfloat16 [32768, 512], P(('dp', 'ctx')), may hold values from -6 to 6
- values: bfloat16 [32768, 512], P(('dp', 'ctx')), may hold values from -6 to 6
- d_out: bfloat16 [32768, 3072], P(('dp', 'ctx')), may hold values from -6 to 6
- features: bfloat16 [32768, 6144], P(('dp', 'ctx')), may hold values from -6 to 6
- doc_start: int32 [32768], P(('dp', 'ctx')), may hold values from 0 to 2047, as said below
- error: float32 [16, 6144, 512], P('dp', 'ctx'), may hold values from -6 to 6
- q_init: float32 [512, 128], replicated, may hold values from -6 to 6
Outputs:
- d_query: bfloat16 [32768, 3072], P(('dp', 'ctx'))
- d_key: bfloat16 [32768, 512], P(('dp', 'ctx'))
- d_value: bfloat16 [32768, 512], P(('dp', 'ctx'))
- compressed: float32 [6144, 512], P('ctx')
- q_factor: float32 [512, 128], replicated
- new_error: float32 [16, 6144, 512], P('dp', 'ctx')
The draws below stay inside these ranges and needn't reach their ends.
Inputs may be any that keep to these rules, and one draw needn't show every extreme that they name: Within each sequence doc_start never falls, equals the position at each document's first token and is at most the token's own position; the first document starts at 0. In the first sequence the last token begins a document of its own.
All inputs are finite; a program needn't handle non-finite values.
Results may differ from the reference program's by a relative error of at most 0.015.
Values may be sent and summed in bfloat16 or wider, within the bound.
No kernel may reach another device: no remote copies, remote signals or barrier semaphores. Data moves between devices by JAX's collectives and lax.ppermute only.
A program may use at most 128 MiB of HBM per device.

```python
import math
import jax
import jax.numpy as jnp
from jax import lax

D = 6144
Q_HEADS = 24
KV_HEADS = 4
HEAD_DIM = 128
RANK = 128
TOK_DEV = 128
SEQ_LEN = 2048
SEQS = 16
TOKENS = 32768
N_CTX = 16


def draw_queries(key, part):
    key = jax.random.fold_in(key, 1)
    first, second = jax.random.split(key)
    row_scale = jnp.exp(jax.random.uniform(first, (TOKENS, 1), minval=-0.7, maxval=0.7))
    result = jax.random.normal(second, (TOKENS, Q_HEADS * HEAD_DIM)) * row_scale
    return jnp.clip(result, -6.0, 6.0).astype(jnp.bfloat16)


def draw_keys(key, part):
    key = jax.random.fold_in(key, 2)
    first, second = jax.random.split(key)
    row_scale = jnp.exp(jax.random.uniform(first, (TOKENS, 1), minval=-1.15, maxval=1.15))
    result = jax.random.normal(second, (TOKENS, KV_HEADS * HEAD_DIM)) * row_scale
    return jnp.clip(result, -6.0, 6.0).astype(jnp.bfloat16)


def draw_doc_start(key, part):
    key = jax.random.fold_in(key, 5)
    cuts = jnp.sort(jax.random.randint(key, (SEQS, 2), SEQ_LEN // 2, SEQ_LEN), axis=1)
    position = jnp.arange(SEQ_LEN, dtype=jnp.int32)[None, :]
    sequence_id = jnp.arange(SEQS, dtype=jnp.int32)[:, None]
    first_cut = cuts[:, 0:1]
    second_cut = jnp.where(sequence_id == 0, SEQ_LEN - 1, cuts[:, 1:2])
    start = jnp.where(position >= second_cut, second_cut, jnp.where(position >= first_cut, first_cut, 0))
    return start.reshape(TOKENS).astype(jnp.int32)


def block_levels(key, shape, cuts, least, top_value):
    def one(axis_at, blocks):
        heights = jax.random.uniform(jax.random.fold_in(jax.random.fold_in(key, 6), axis_at), (blocks,), jnp.float32, least / len(cuts), top_value / len(cuts))
        return jnp.repeat(jnp.exp(heights), shape[axis_at] // blocks).reshape((-1,) + (1,) * (len(shape) - axis_at - 1))

    factor_of = one(*cuts[0])
    for cut in cuts[1:]:
        factor_of = factor_of * one(*cut)
    return factor_of


def scatter_about(rng, dims, scale, most, cuts=(), held_as=jnp.bfloat16):
    values = scale * jax.random.normal(rng, dims, jnp.float32)
    if cuts:
        values = values * block_levels(rng, dims, cuts, -0.22, 0.18)
    return jnp.clip(values, -most, most).astype(held_as)


def setup_inputs(seed: int = 0) -> dict:
    streams_of = jax.random.split(jax.random.key(seed), 9)
    queries = draw_queries(jax.random.fold_in(streams_of[8], 71), 0)
    keys = draw_keys(jax.random.fold_in(streams_of[8], 71), 0)
    values = scatter_about(streams_of[2], (TOKENS, KV_HEADS * HEAD_DIM), 1.0, 6.0, ((0, 256),))
    d_out = scatter_about(streams_of[3], (TOKENS, Q_HEADS * HEAD_DIM), 1.0, 6.0, ((0, 256),))
    features = scatter_about(streams_of[4], (TOKENS, D), 1.0, 6.0, ((0, 256),))
    doc_start = draw_doc_start(jax.random.fold_in(streams_of[8], 71), 0)
    error = scatter_about(streams_of[6], (SEQS, D, KV_HEADS * HEAD_DIM), 1.0, 6.0, ((0, 16), (1, 16)), jnp.float32)
    q_init = scatter_about(streams_of[7], (KV_HEADS * HEAD_DIM, RANK), 1.0, 6.0, (), jnp.float32)
    return {"queries": queries, "keys": keys, "values": values, "d_out": d_out, "features": features, "doc_start": doc_start, "error": error, "q_init": q_init}


NEG_FILL = -1e+30

def head_terms(head_id, q_seq, k_seq, v_seq, do_seq, start_seq):
    kv_id = head_id // (Q_HEADS // KV_HEADS)
    softmax_scale = 1.0 / math.sqrt(HEAD_DIM)
    q_head = lax.dynamic_slice_in_dim(q_seq, head_id * HEAD_DIM, HEAD_DIM, 1)
    do_head = lax.dynamic_slice_in_dim(do_seq, head_id * HEAD_DIM, HEAD_DIM, 1)
    k_head = lax.dynamic_slice_in_dim(k_seq, kv_id * HEAD_DIM, HEAD_DIM, 1)
    v_head = lax.dynamic_slice_in_dim(v_seq, kv_id * HEAD_DIM, HEAD_DIM, 1)
    position = jnp.arange(SEQ_LEN, dtype=jnp.int32)
    allowed = (position[None, :] <= position[:, None]) & (position[None, :] >= start_seq[:, None])
    scores = jnp.dot(q_head.astype(jnp.float32), k_head.T.astype(jnp.float32), preferred_element_type=jnp.float32) * softmax_scale
    scores = jnp.where(allowed, scores, NEG_FILL)
    top = lax.optimization_barrier(jnp.max(scores, axis=1, keepdims=True))
    expo = jnp.where(allowed, jnp.exp(scores - top), 0.0)
    probs = expo / lax.optimization_barrier(jnp.sum(expo, axis=1, keepdims=True))
    probs_low = probs.astype(jnp.bfloat16)
    dprob = jnp.dot(do_head.astype(jnp.float32), v_head.T.astype(jnp.float32), preferred_element_type=jnp.float32)
    mix = lax.optimization_barrier(jnp.sum(probs_low.astype(jnp.float32) * dprob, axis=1, keepdims=True))
    dscore = (probs * (dprob - mix)).astype(jnp.bfloat16)
    dq_head = jnp.dot(dscore.astype(jnp.float32), k_head.astype(jnp.float32), preferred_element_type=jnp.float32) * softmax_scale
    score_gradient_blocks = dscore.astype(jnp.float32).reshape(N_CTX, TOK_DEV, SEQ_LEN)
    probability_blocks = probs_low.astype(jnp.float32).reshape(N_CTX, TOK_DEV, SEQ_LEN)
    query_blocks = q_head.astype(jnp.float32).reshape(N_CTX, TOK_DEV, HEAD_DIM)
    output_gradient_blocks = do_head.astype(jnp.float32).reshape(N_CTX, TOK_DEV, HEAD_DIM)
    key_gradient_blocks = jnp.einsum('ozp,oze->ope', score_gradient_blocks, query_blocks) * softmax_scale
    value_gradient_blocks = jnp.einsum('ozp,oze->ope', probability_blocks, output_gradient_blocks)
    return (dq_head, key_gradient_blocks, value_gradient_blocks)

def block_total(parts):
    group_size = Q_HEADS // KV_HEADS
    summed = lax.optimization_barrier(jnp.sum(parts.reshape(KV_HEADS, group_size, N_CTX, SEQ_LEN, HEAD_DIM), axis=1))
    rounded = lax.optimization_barrier(summed.astype(jnp.bfloat16)).astype(jnp.float32)
    total = lax.optimization_barrier(jnp.sum(rounded, axis=1))
    return jnp.transpose(total, (1, 0, 2)).reshape(SEQ_LEN, KV_HEADS * HEAD_DIM)

def sequence_terms(pieces):
    q_seq, k_seq, v_seq, do_seq, start_seq = pieces

    def one_head(head_id):
        return head_terms(head_id, q_seq, k_seq, v_seq, do_seq, start_seq)
    dq_all, dk_all, dv_all = lax.map(one_head, jnp.arange(Q_HEADS, dtype=jnp.int32))
    d_query = jnp.transpose(dq_all, (1, 0, 2)).reshape(SEQ_LEN, Q_HEADS * HEAD_DIM)
    d_key = block_total(dk_all)
    d_value = block_total(dv_all)
    return (d_query.astype(jnp.bfloat16), d_key.astype(jnp.bfloat16), d_value.astype(jnp.bfloat16))

def seq_gradient(pair):
    return jnp.dot(pair[0].T.astype(jnp.float32), pair[1].astype(jnp.float32), preferred_element_type=jnp.float32)

def reference(queries, keys, values, d_out, features, doc_start, error, q_init):
    width_kv = KV_HEADS * HEAD_DIM
    highest = lax.Precision.HIGHEST
    pieces = (queries.reshape(SEQS, SEQ_LEN, Q_HEADS * HEAD_DIM), keys.reshape(SEQS, SEQ_LEN, width_kv), values.reshape(SEQS, SEQ_LEN, width_kv), d_out.reshape(SEQS, SEQ_LEN, Q_HEADS * HEAD_DIM), doc_start.reshape(SEQS, SEQ_LEN))
    d_query, d_key, d_value = lax.map(sequence_terms, pieces)
    grads = lax.map(seq_gradient, (features.reshape(SEQS, SEQ_LEN, D), d_key))
    combined = grads + error
    p_sum = jnp.einsum('rdk,kc->dc', combined, q_init, precision=highest)
    gram = jnp.dot(p_sum.T, p_sum, precision=highest)
    lower = jnp.linalg.cholesky(gram)
    p_hat = jax.scipy.linalg.solve_triangular(lower, p_sum.T, lower=True).T
    q_factor = jnp.einsum('rdk,dc->kc', combined, p_hat, precision=highest) / SEQS
    compressed = jnp.dot(p_hat, q_factor.T, precision=highest)
    new_error = combined - compressed[None]
    return (d_query.reshape(TOKENS, Q_HEADS * HEAD_DIM), d_key.reshape(TOKENS, width_kv), d_value.reshape(TOKENS, width_kv), compressed, q_factor, new_error)
```

```python
import math

import jax
import jax.numpy as jnp
from jax import lax
from jax.experimental import pallas as pl
from jax.experimental.pallas import tpu as pltpu
from jax.sharding import Mesh
from jax.sharding import PartitionSpec as P

HEAD = 128
NEG_FILL = -1e30
LOG2E = 1.4426950408889634
HIGHEST = lax.Precision.HIGHEST
TN = (((0,), (0,)), ((), ()))
NT = (((1,), (1,)), ((), ()))
HEADS_AT_ONCE = 2


def attention(where, queries, q_peer, d_out, do_peer, kv, doc, group_size):
    tokens = queries.shape[0]
    block = 2 * tokens
    length = kv.shape[0]
    slots = length // block
    width_kv = kv.shape[1] // 2
    heads = q_peer.shape[1] // HEAD
    steps = heads // HEADS_AT_ONCE
    per_group = group_size // HEADS_AT_ONCE
    groups = width_kv // HEAD
    wide = HEADS_AT_ONCE * HEAD
    columns = HEADS_AT_ONCE * block
    scale = 1.0 / math.sqrt(HEAD)
    power = scale * LOG2E

    def kernel(
        at, qo, qp, do, dp_, k_ref, v_ref, doc_ref, dqo, dqp, dk_ref, dv_ref,
        s_scr, d_scr, bias, k_turned, dq_acc, dk_acc, dv_acc,
    ):
        step = pl.program_id(0)
        core, chip = at[0], at[1]
        first = (jnp.min(doc_ref[...].astype(jnp.float32)).astype(jnp.int32)) // block

        def place(index):
            return jnp.where(index < tokens, index + core * tokens, index - core * tokens)

        @pl.when(step == 0)
        def _():
            q_pos = chip * block + place(lax.broadcasted_iota(jnp.int32, (block, block), 1))
            k_off = place(lax.broadcasted_iota(jnp.int32, (block, block), 0))
            start = doc_ref[...]

            def fill(j, _):
                slot = jnp.bitwise_xor(j, chip)
                k_pos = j * block + k_off
                ok = (k_pos <= q_pos) & (k_pos >= start)
                bias[pl.ds(pl.multiple_of(slot * block, block), block), :] = jnp.where(
                    ok, 0.0, NEG_FILL
                )
                return 0

            lax.fori_loop(first, chip + 1, fill, 0)

        @pl.when(lax.rem(step, per_group) == 0)
        def _():
            dk_acc[...] = jnp.zeros_like(dk_acc)
            dv_acc[...] = jnp.zeros_like(dv_acc)
            for slot in range(slots):
                k_turned[slot] = (
                    k_ref[slot * block : (slot + 1) * block, :].astype(jnp.float32).T
                ).astype(jnp.bfloat16)

        def rows_of(own, peer):
            parts = []
            for n in range(HEADS_AT_ONCE):
                parts.append(own[:, n * HEAD : (n + 1) * HEAD])
                parts.append(peer[:, n * HEAD : (n + 1) * HEAD])
            return jnp.concatenate(parts, axis=0)

        q = rows_of(qo, qp)
        g = rows_of(do, dp_)

        def fold(x):
            return x.reshape(block // 8, 8, columns)

        def here(j):
            slot = jnp.bitwise_xor(j, chip)
            return slot, pl.ds(pl.multiple_of(slot * block, block), block)

        def score_step(j, top):
            _, span = here(j)
            s = lax.dot_general(k_ref[span, :], q, NT, preferred_element_type=jnp.float32)
            b = bias[span, :]
            s = s + jnp.concatenate([b] * HEADS_AT_ONCE, axis=1)
            s_scr[span, :] = s
            return jnp.maximum(top, jnp.max(fold(s), axis=0))

        top = lax.fori_loop(
            first, chip + 1, score_step, jnp.full((8, columns), NEG_FILL, jnp.float32)
        )
        top = jnp.max(top, axis=0, keepdims=True)

        def prob_step(j, carry):
            total, mix = carry
            _, span = here(j)
            p = jnp.exp2((s_scr[span, :] - top) * power)
            d = lax.dot_general(v_ref[span, :], g, NT, preferred_element_type=jnp.float32)
            s_scr[span, :] = p
            d_scr[span, :] = d
            return (total + jnp.sum(fold(p), axis=0), mix + jnp.sum(fold(p * d), axis=0))

        zero = jnp.zeros((8, columns), jnp.float32)
        total, mix = lax.fori_loop(first, chip + 1, prob_step, (zero, zero))
        inverse = 1.0 / jnp.sum(total, axis=0, keepdims=True)
        mix = jnp.sum(mix, axis=0, keepdims=True) * inverse
        dq_acc[...] = jnp.zeros_like(dq_acc)

        def grad_step(j, _):
            slot, span = here(j)
            p = s_scr[span, :] * inverse
            ds = (p * (d_scr[span, :] - mix)).astype(jnp.bfloat16)
            low = p.astype(jnp.bfloat16)
            dv_acc[span, :] += jnp.dot(low, g, preferred_element_type=jnp.float32)
            dk_acc[span, :] += jnp.dot(ds, q, preferred_element_type=jnp.float32)
            dq_acc[...] += jnp.dot(k_turned[slot], ds, preferred_element_type=jnp.float32)
            return 0

        lax.fori_loop(first, chip + 1, grad_step, 0)
        dq = (dq_acc[...] * scale).T.astype(jnp.bfloat16)
        for n in range(HEADS_AT_ONCE):
            at_row = n * block
            dqo[:, n * HEAD : (n + 1) * HEAD] = dq[at_row : at_row + tokens]
            dqp[:, n * HEAD : (n + 1) * HEAD] = dq[at_row + tokens : at_row + block]

        @pl.when(lax.rem(step, per_group) == per_group - 1)
        def _():
            dk_ref[...] = (dk_acc[...] * scale).astype(jnp.bfloat16)
            dv_ref[...] = dv_acc[...].astype(jnp.bfloat16)

    own = pl.BlockSpec((tokens, wide), lambda s, at: (0, at[0] * steps + s))
    peer = pl.BlockSpec((tokens, wide), lambda s, at: (0, s))
    part = pl.BlockSpec((length, HEAD), lambda s, at: (0, s // per_group))
    flops = 5 * 2 * length * block * heads * HEAD
    return pl.pallas_call(
        kernel,
        grid_spec=pltpu.PrefetchScalarGridSpec(
            num_scalar_prefetch=1,
            grid=(steps,),
            in_specs=[
                own,
                peer,
                own,
                peer,
                part,
                pl.BlockSpec((length, HEAD), lambda s, at: (0, groups + s // per_group)),
                pl.BlockSpec((1, block), lambda s, at: (0, 0)),
            ],
            out_specs=[peer, peer, part, part],
            scratch_shapes=[
                pltpu.VMEM((length, columns), jnp.float32),
                pltpu.VMEM((length, columns), jnp.float32),
                pltpu.VMEM((length, block), jnp.float32),
                pltpu.VMEM((slots, HEAD, block), jnp.bfloat16),
                pltpu.VMEM((HEAD, columns), jnp.float32),
                pltpu.VMEM((length, HEAD), jnp.float32),
                pltpu.VMEM((length, HEAD), jnp.float32),
            ],
        ),
        out_shape=[
            jax.ShapeDtypeStruct((tokens, heads * HEAD), jnp.bfloat16),
            jax.ShapeDtypeStruct((tokens, heads * HEAD), jnp.bfloat16),
            jax.ShapeDtypeStruct((length, width_kv), jnp.bfloat16),
            jax.ShapeDtypeStruct((length, width_kv), jnp.bfloat16),
        ],
        compiler_params=pltpu.CompilerParams(
            dimension_semantics=("arbitrary",), vmem_limit_bytes=40 * 1024 * 1024
        ),
        cost_estimate=pl.CostEstimate(
            flops=4 * flops, bytes_accessed=8 * 1024 * 1024, transcendentals=0
        ),
        name="attention",
    )(where, queries, q_peer, d_out, do_peer, kv, kv, doc)


def inverse_factor(gram):
    size = gram.shape[0]
    tiles = size // 8

    def kernel(g_ref, out_ref):
        sub = lax.broadcasted_iota(jnp.int32, (8, 1), 0)
        lane = lax.broadcasted_iota(jnp.int32, (8, size), 1)
        row8 = lax.broadcasted_iota(jnp.int32, (8, size), 0)
        left = [g_ref[8 * t : 8 * t + 8, :] for t in range(tiles)]
        right = [jnp.where(lane == row8 + 8 * t, 1.0, 0.0) for t in range(tiles)]
        for j in range(size):
            t0, r = j // 8, j % 8
            row_l = left[t0][r : r + 1, :]
            row_r = right[t0][r : r + 1, :]
            root = 1.0 / jnp.sqrt(row_l[:, j : j + 1])
            row_l = row_l * root
            row_r = row_r * root
            for t in range(t0, tiles):
                c = left[t][:, j : j + 1] * root
                if t == t0:
                    c = jnp.where(sub > r, c, 0.0)
                    hit = sub == r
                    left[t] = jnp.where(hit, row_l, left[t] - c * row_l)
                    right[t] = jnp.where(hit, row_r, right[t] - c * row_r)
                else:
                    left[t] = left[t] - c * row_l
                    right[t] = right[t] - c * row_r
        for t in range(tiles):
            out_ref[8 * t : 8 * t + 8, :] = right[t]

    return pl.pallas_call(
        kernel,
        out_shape=jax.ShapeDtypeStruct((size, size), jnp.float32),
        in_specs=[pl.BlockSpec(memory_space=pltpu.VMEM)],
        out_specs=pl.BlockSpec(memory_space=pltpu.VMEM),
        name="inverse_factor",
    )(gram)


def body(queries, keys, values, d_out, features, doc_start, error, q_init):
    tokens = queries.shape[0]
    width_kv = keys.shape[1]
    half_kv = width_kv // 2
    half_q = queries.shape[1] // 2
    group_size = queries.shape[1] // width_kv
    chips = lax.axis_size("chip")
    replicas = lax.axis_size("dp")
    core = lax.axis_index("core")
    chip = lax.axis_index("chip")
    other = 1 - core
    f32, bf16 = jnp.float32, jnp.bfloat16

    def swap(x):
        return lax.ppermute(x, "core", [(0, 1), (1, 0)])

    def piece(x, size, index, axis=1):
        return lax.dynamic_slice_in_dim(x, index * size, size, axis)

    def in_order(mine, theirs):
        return jnp.where(
            core == 0,
            jnp.concatenate([mine, theirs], axis=1),
            jnp.concatenate([theirs, mine], axis=1),
        )

    def send(x, k, keep=lambda i, j: True):
        pairs = [(i, i ^ k) for i in range(chips) if keep(i, i ^ k)]
        return lax.ppermute(x, "chip", pairs)

    kv_peer = swap(
        jnp.concatenate([piece(keys, half_kv, other), piece(values, half_kv, other)], axis=1)
    )
    kv_mine = jnp.concatenate([piece(keys, half_kv, core), piece(values, half_kv, core)], axis=1)
    kv_chip = jnp.concatenate([kv_mine, kv_peer], axis=0)
    kv = jnp.concatenate(
        [kv_chip] + [send(kv_chip, k, lambda i, j: i < j) for k in range(1, chips)], axis=0
    )
    q_peer = swap(piece(queries, half_q, other))
    do_peer = swap(piece(d_out, half_q, other))
    doc = jnp.concatenate([doc_start, swap(doc_start)])[None, :]
    where = jnp.stack([core, chip]).astype(jnp.int32)

    kv, features = lax.optimization_barrier((kv, features))
    rows2 = features.shape[1] // chips
    rows = rows2 // 2
    blocks = [piece(features, rows2, chip)]
    for k in range(1, chips):
        blocks.append(send(piece(features, rows2, jnp.bitwise_xor(chip, k)), k))

    dq_own, dq_peer, dk, dv = attention(
        where, queries, q_peer, d_out, do_peer, kv, doc, group_size
    )

    block = 2 * tokens

    def gather_sum(x):
        total = x[:block].astype(f32)
        for k in range(1, chips):
            part = send(x[k * block : (k + 1) * block], k, lambda i, j: i > j)
            total = total + part.astype(f32)
        return total.astype(bf16)

    dk_half = gather_sum(dk)
    dk_mine = jnp.stack([dk_half] + [send(dk_half, k) for k in range(1, chips)])
    dk_theirs = swap(dk_mine)
    d_key = in_order(dk_half[:tokens], dk_theirs[0, tokens:])

    feat = jnp.concatenate(blocks, axis=0)
    feat_own = piece(feat, rows, core)
    feat_peer = swap(piece(feat, rows, other))
    feat = jnp.concatenate([feat_own, feat_peer], axis=0)
    by_token = jnp.concatenate(
        [
            jnp.concatenate([dk_mine[:, :tokens], dk_mine[:, tokens:]], axis=0),
            jnp.concatenate([dk_theirs[:, tokens:], dk_theirs[:, :tokens]], axis=0),
        ],
        axis=2,
    ).reshape(2 * chips * tokens, width_kv)
    grad = lax.dot_general(feat, by_token, TN, preferred_element_type=f32)
    grad = jnp.where(core == 0, grad, jnp.roll(grad, half_kv, axis=1))
    combined = grad + error.reshape(rows, width_kv)

    shares = combined.astype(bf16).reshape(replicas, rows // replicas, width_kv)
    shares = lax.all_to_all(shares, "dp", 0, 0)
    share = jnp.sum(shares.astype(f32), axis=0).astype(bf16)
    total = lax.all_to_all(jnp.broadcast_to(share[None], (replicas,) + share.shape), "dp", 0, 0)
    total = total.reshape(rows, width_kv).astype(f32)

    p_sum = jnp.dot(total, q_init, precision=HIGHEST)
    both = lax.dot_general(
        jnp.concatenate([total, p_sum], axis=1), p_sum, TN, precision=HIGHEST
    )
    rank = q_init.shape[1]
    size = both.shape[0] // 2
    part = piece(both, size, core, 0) + swap(piece(both, size, other, 0))
    part = lax.all_to_all(part.reshape(chips, size // chips, rank), "chip", 0, 0)
    part = jnp.sum(part, axis=0)
    part = lax.all_to_all(jnp.broadcast_to(part[None], (chips,) + part.shape), "chip", 0, 0)
    part = part.reshape(size, rank)
    their = swap(part)
    both = jnp.where(
        core == 0, jnp.concatenate([part, their]), jnp.concatenate([their, part])
    )
    inverse = inverse_factor(both[width_kv:])
    p_hat = lax.dot_general(p_sum, inverse, NT, precision=HIGHEST)
    q_factor = lax.dot_general(both[:width_kv], inverse, NT, precision=HIGHEST) / replicas
    compressed = lax.dot_general(p_hat, q_factor, NT, precision=HIGHEST)
    new_error = (combined - compressed).reshape(1, rows, width_kv)

    dv_half = gather_sum(dv)
    d_value = in_order(dv_half[:tokens], swap(dv_half[tokens:]))
    d_query = in_order(dq_own, swap(dq_peer))
    return (d_query, d_key, d_value, compressed, q_factor, new_error)


def solution(mesh):
    replicas, ctx = mesh.devices.shape
    parts = Mesh(mesh.devices.reshape(replicas, ctx // 2, 2), ("dp", "chip", "core"))
    everywhere = ("dp", "chip", "core")
    tokens = P(everywhere, None)
    in_specs = (
        tokens, tokens, tokens, tokens, tokens, P(everywhere), P("dp", ("chip", "core"), None), P(),
    )
    out_specs = (
        tokens, tokens, tokens, P(("chip", "core"), None), P(), P("dp", ("chip", "core"), None),
    )
    return jax.shard_map(body, mesh=parts, in_specs=in_specs, out_specs=out_specs, check_vma=False)
```

```python
import math

import jax
import jax.numpy as jnp
from jax import lax
from jax.experimental import pallas as pl
from jax.experimental.pallas import tpu as pltpu
from jax.sharding import Mesh
from jax.sharding import PartitionSpec as P

HEAD = 128
NEG_FILL = -1e30
LOG2E = 1.4426950408889634
HIGHEST = lax.Precision.HIGHEST
TN = (((0,), (0,)), ((), ()))
NT = (((1,), (1,)), ((), ()))
HEADS_AT_ONCE = 2


def attention(where, qg, kv):
    devices, padded, _ = kv.shape
    tokens = HEAD
    block = 2 * tokens
    chips = devices // 2
    length = devices * tokens
    heads = qg.shape[1] // (2 * HEAD)
    steps = heads // HEADS_AT_ONCE
    wide = HEADS_AT_ONCE * HEAD
    columns = HEADS_AT_ONCE * block
    scale = 1.0 / math.sqrt(HEAD)
    power = scale * LOG2E

    def kernel(
        at, q_ref, g_ref, k_ref, v_ref, dq_ref, dk_ref, dv_ref,
        s_scr, d_scr, bias, k_turned, dq_acc, dk_acc, dv_acc,
    ):
        step = pl.program_id(0)
        core = at[0]
        chip = at[1 + step // steps]

        def place(index):
            return jnp.where(index < tokens, index + core * tokens, index - core * tokens)

        def starts(device):
            high = k_ref[device, tokens : tokens + 1, :].astype(jnp.float32)
            low = v_ref[device, tokens : tokens + 1, :].astype(jnp.float32)
            return high * 64.0 + low

        start = jnp.concatenate(
            [starts(2 * chip + core), starts(2 * chip + 1 - core)], axis=1
        )
        first = jnp.min(start).astype(jnp.int32) // block

        def span_of(j):
            return pl.ds(pl.multiple_of(j * block, block), block)

        def rows_of(ref, j):
            return ref[pl.ds(2 * j, 2), :tokens, :].reshape(block, HEAD)

        @pl.when(lax.rem(step, steps) == 0)
        def _():
            q_pos = chip * block + place(lax.broadcasted_iota(jnp.int32, (block, block), 1))
            k_off = lax.broadcasted_iota(jnp.int32, (block, block), 0)
            begin = start.astype(jnp.int32)

            def fill(j, _):
                k_pos = j * block + k_off
                ok = (k_pos <= q_pos) & (k_pos >= begin)
                bias[span_of(j), :] = jnp.where(ok, 0.0, NEG_FILL)
                return 0

            lax.fori_loop(first, chip + 1, fill, 0)

        @pl.when(step == 0)
        def _():
            dk_acc[...] = jnp.zeros_like(dk_acc)
            dv_acc[...] = jnp.zeros_like(dv_acc)
            for j in range(chips):
                k_turned[j] = (
                    k_ref[2 * j : 2 * j + 2, :tokens, :].reshape(block, HEAD).astype(jnp.float32).T
                ).astype(jnp.bfloat16)

        def stacked(ref):
            x = ref[...]
            return jnp.concatenate(
                [x[:, n * HEAD : (n + 1) * HEAD] for n in range(HEADS_AT_ONCE)], axis=0
            )

        q = stacked(q_ref)
        g = stacked(g_ref)

        def fold(x):
            return x.reshape(block // 8, 8, columns)

        def score_step(j, top):
            s = lax.dot_general(rows_of(k_ref, j), q, NT, preferred_element_type=jnp.float32)
            b = bias[span_of(j), :]
            s = s + jnp.concatenate([b] * HEADS_AT_ONCE, axis=1)
            s_scr[span_of(j), :] = s
            return jnp.maximum(top, jnp.max(fold(s), axis=0))

        top = lax.fori_loop(
            first, chip + 1, score_step, jnp.full((8, columns), NEG_FILL, jnp.float32)
        )
        top = jnp.max(top, axis=0, keepdims=True)

        def prob_step(j, carry):
            total, mix = carry
            span = span_of(j)
            p = jnp.exp2((s_scr[span, :] - top) * power)
            d = lax.dot_general(rows_of(v_ref, j), g, NT, preferred_element_type=jnp.float32)
            s_scr[span, :] = p
            d_scr[span, :] = d
            return (total + jnp.sum(fold(p), axis=0), mix + jnp.sum(fold(p * d), axis=0))

        zero = jnp.zeros((8, columns), jnp.float32)
        total, mix = lax.fori_loop(first, chip + 1, prob_step, (zero, zero))
        inverse = 1.0 / jnp.sum(total, axis=0, keepdims=True)
        mix = jnp.sum(mix, axis=0, keepdims=True) * inverse
        dq_acc[...] = jnp.zeros_like(dq_acc)

        def grad_step(j, _):
            span = span_of(j)
            p = s_scr[span, :] * inverse
            ds = (p * (d_scr[span, :] - mix)).astype(jnp.bfloat16)
            low = p.astype(jnp.bfloat16)
            dv_acc[span, :] += jnp.dot(low, g, preferred_element_type=jnp.float32)
            dk_acc[span, :] += jnp.dot(ds, q, preferred_element_type=jnp.float32)
            dq_acc[...] += jnp.dot(k_turned[j], ds, preferred_element_type=jnp.float32)
            return 0

        lax.fori_loop(first, chip + 1, grad_step, 0)
        dq = (dq_acc[...] * scale).T.astype(jnp.bfloat16)
        for n in range(HEADS_AT_ONCE):
            dq_ref[:, n * HEAD : (n + 1) * HEAD] = dq[n * block : (n + 1) * block]

        @pl.when(step == 2 * steps - 1)
        def _():
            dk_ref[...] = (dk_acc[...] * scale).astype(jnp.bfloat16)
            dv_ref[...] = dv_acc[...].astype(jnp.bfloat16)

    whole = pl.BlockSpec((length, HEAD), lambda s, at: (0, 0))
    queries_at = pl.BlockSpec((block, wide), lambda s, at: (s // steps, s % steps))
    flops = 5 * 2 * length * block * heads * HEAD
    return pl.pallas_call(
        kernel,
        grid_spec=pltpu.PrefetchScalarGridSpec(
            num_scalar_prefetch=1,
            grid=(2 * steps,),
            in_specs=[
                queries_at,
                pl.BlockSpec((block, wide), lambda s, at: (s // steps, steps + s % steps)),
                pl.BlockSpec((devices, padded, HEAD), lambda s, at: (0, 0, 0)),
                pl.BlockSpec((devices, padded, HEAD), lambda s, at: (0, 0, 1)),
            ],
            out_specs=[queries_at, whole, whole],
            scratch_shapes=[
                pltpu.VMEM((length, columns), jnp.float32),
                pltpu.VMEM((length, columns), jnp.float32),
                pltpu.VMEM((length, block), jnp.float32),
                pltpu.VMEM((chips, HEAD, block), jnp.bfloat16),
                pltpu.VMEM((HEAD, columns), jnp.float32),
                pltpu.VMEM((length, HEAD), jnp.float32),
                pltpu.VMEM((length, HEAD), jnp.float32),
            ],
        ),
        out_shape=[
            jax.ShapeDtypeStruct((2 * block, heads * HEAD), jnp.bfloat16),
            jax.ShapeDtypeStruct((length, HEAD), jnp.bfloat16),
            jax.ShapeDtypeStruct((length, HEAD), jnp.bfloat16),
        ],
        compiler_params=pltpu.CompilerParams(
            dimension_semantics=("arbitrary",), vmem_limit_bytes=40 * 1024 * 1024
        ),
        cost_estimate=pl.CostEstimate(
            flops=8 * flops, bytes_accessed=8 * 1024 * 1024, transcendentals=0
        ),
        name="attention",
    )(where, qg, qg, kv, kv)


def inverse_factor(gram):
    size = gram.shape[0]
    tiles = size // 8

    def kernel(g_ref, out_ref):
        sub = lax.broadcasted_iota(jnp.int32, (8, 1), 0)
        lane = lax.broadcasted_iota(jnp.int32, (8, size), 1)
        row8 = lax.broadcasted_iota(jnp.int32, (8, size), 0)
        left = [g_ref[8 * t : 8 * t + 8, :] for t in range(tiles)]
        right = [jnp.where(lane == row8 + 8 * t, 1.0, 0.0) for t in range(tiles)]
        for j in range(size):
            t0, r = j // 8, j % 8
            row_l = left[t0][r : r + 1, :]
            row_r = right[t0][r : r + 1, :]
            root = 1.0 / jnp.sqrt(row_l[:, j : j + 1])
            row_l = row_l * root
            row_r = row_r * root
            for t in range(t0, tiles):
                c = left[t][:, j : j + 1] * root
                if t == t0:
                    c = jnp.where(sub > r, c, 0.0)
                    hit = sub == r
                    left[t] = jnp.where(hit, row_l, left[t] - c * row_l)
                    right[t] = jnp.where(hit, row_r, right[t] - c * row_r)
                else:
                    left[t] = left[t] - c * row_l
                    right[t] = right[t] - c * row_r
        for t in range(tiles):
            out_ref[8 * t : 8 * t + 8, :] = right[t]

    return pl.pallas_call(
        kernel,
        out_shape=jax.ShapeDtypeStruct((size, size), jnp.float32),
        in_specs=[pl.BlockSpec(memory_space=pltpu.VMEM)],
        out_specs=pl.BlockSpec(memory_space=pltpu.VMEM),
        name="inverse_factor",
    )(gram)


def body(queries, keys, values, d_out, features, doc_start, error, q_init):
    tokens = queries.shape[0]
    width_kv = keys.shape[1]
    group = queries.shape[1] // (width_kv // HEAD)
    chips = lax.axis_size("chip")
    devices = 2 * chips
    replicas = lax.axis_size("dp")
    core = lax.axis_index("core")
    chip = lax.axis_index("chip")
    upper = (chip >= chips // 2).astype(jnp.int32)
    f32, bf16 = jnp.float32, jnp.bfloat16
    ctx = ("chip", "core")

    def swap(x):
        return lax.ppermute(x, "core", [(0, 1), (1, 0)])

    def piece(x, size, index, axis=1):
        return lax.dynamic_slice_in_dim(x, index * size, size, axis)

    def move(x, cross, turn):
        pairs = []
        for c in range(chips):
            for h in range(2):
                to = (chips - 1 - c if cross else c) * 2 + (1 - h if turn else h)
                pairs.append((2 * c + h, to))
        return lax.ppermute(x, ctx, pairs)

    def exchange(x, axis):
        return lax.all_to_all(x, axis, 0, 0)

    def spread(x, axis, size):
        return exchange(jnp.broadcast_to(x[None], (size,) + x.shape), axis)

    def head_of(cross, turn):
        return 2 * (1 - core if turn else core) + (1 - upper if cross else upper)

    ways = [(False, False), (False, True), (True, False), (True, True)]
    start_row = jnp.concatenate([doc_start // 64, doc_start % 64]).astype(bf16)[None, :]
    start_rows = jnp.concatenate([start_row, jnp.zeros((15, 2 * tokens), bf16)], axis=0)
    per_head = [
        jnp.concatenate(
            [
                jnp.concatenate(
                    [keys[:, h * HEAD : (h + 1) * HEAD], values[:, h * HEAD : (h + 1) * HEAD]],
                    axis=1,
                ),
                start_rows,
            ],
            axis=0,
        )
        for h in range(width_kv // HEAD)
    ]
    per_half = [jnp.stack([per_head[u], per_head[2 + u]]) for u in range(2)]
    kv_send = jnp.concatenate([per_half[0]] * (chips // 2) + [per_half[1]] * (chips // 2), axis=0)
    kv = exchange(kv_send, ctx)

    def both_of(head):
        return jnp.concatenate([piece(queries, group, head), piece(d_out, group, head)], axis=1)

    qg = [both_of(head_of(False, False))]
    for cross, turn in ways[1:]:
        qg.append(move(both_of(head_of(cross, turn)), cross, turn))
    qg = jnp.concatenate(qg, axis=0)

    rows = features.shape[1] // devices
    feat_send = jnp.transpose(features.reshape(tokens, devices, rows), (1, 0, 2))
    kv, feat_send = lax.optimization_barrier((kv, feat_send))
    feat = exchange(feat_send, ctx)

    where = jnp.stack([core, chip, chips - 1 - chip]).astype(jnp.int32)
    dq, dk, dv = attention(where, qg, kv)
    dk, feat = lax.optimization_barrier((dk, feat))

    def to_owner(x):
        x = exchange(x.reshape(devices, tokens, HEAD), ctx)
        x = x.reshape(2, chips // 2, 2, tokens, HEAD).astype(f32)
        x = jnp.sum(x, axis=1).astype(bf16)
        return jnp.concatenate([x[0, 0], x[1, 0], x[0, 1], x[1, 1]], axis=1)

    d_key = to_owner(dk)
    dk_mine = spread(d_key, "chip", chips)
    dk_theirs = swap(dk_mine)
    by_token = jnp.where(
        core == 0,
        jnp.stack([dk_mine, dk_theirs], axis=1),
        jnp.stack([dk_theirs, dk_mine], axis=1),
    ).reshape(devices * tokens, width_kv)
    grad = lax.dot_general(
        feat.reshape(devices * tokens, rows), by_token, TN, preferred_element_type=f32
    )
    combined = grad + error.reshape(rows, width_kv)

    shares = combined.astype(bf16).reshape(replicas, rows // replicas, width_kv)
    shares, dv, dq = lax.optimization_barrier((shares, dv, dq))
    shares = exchange(shares, "dp")
    d_value = to_owner(dv)
    share = jnp.sum(shares.astype(f32), axis=0).astype(bf16)
    total = spread(share, "dp", replicas).reshape(rows, width_kv).astype(f32)

    d_query = jnp.zeros((tokens, queries.shape[1]), bf16)
    for n, (cross, turn) in enumerate(ways):
        back = dq[n * tokens : (n + 1) * tokens]
        if n:
            back = move(back, cross, turn)
        d_query = lax.dynamic_update_slice_in_dim(d_query, back, head_of(cross, turn) * group, 1)

    p_sum = jnp.dot(total, q_init, precision=HIGHEST)
    gram = lax.dot_general(p_sum, p_sum, TN, precision=HIGHEST)
    gram = jnp.sum(spread(gram + swap(gram), "chip", chips), axis=0)
    moment = lax.dot_general(total, p_sum, TN, precision=HIGHEST)
    size = width_kv // 2
    moment = piece(moment, size, core, 0) + swap(piece(moment, size, 1 - core, 0))
    moment, gram = lax.optimization_barrier((moment.astype(bf16), gram))
    moment = jnp.sum(spread(moment, "chip", chips).astype(f32), axis=0)
    inverse = inverse_factor(gram)
    q_mine = lax.dot_general(moment, inverse, NT, precision=HIGHEST) / replicas
    q_theirs = swap(q_mine)
    q_factor = jnp.where(
        core == 0, jnp.concatenate([q_mine, q_theirs]), jnp.concatenate([q_theirs, q_mine])
    )
    p_hat = lax.dot_general(p_sum, inverse, NT, precision=HIGHEST)
    compressed = lax.dot_general(p_hat, q_factor, NT, precision=HIGHEST)
    new_error = (combined - compressed).reshape(1, rows, width_kv)
    return (d_query, d_key, d_value, compressed, q_factor, new_error)


def solution(mesh):
    replicas, ctx = mesh.devices.shape
    parts = Mesh(mesh.devices.reshape(replicas, ctx // 2, 2), ("dp", "chip", "core"))
    everywhere = ("dp", "chip", "core")
    tokens = P(everywhere, None)
    in_specs = (
        tokens, tokens, tokens, tokens, tokens, P(everywhere), P("dp", ("chip", "core"), None), P(),
    )
    out_specs = (
        tokens, tokens, tokens, P(("chip", "core"), None), P(), P("dp", ("chip", "core"), None),
    )
    return jax.shard_map(body, mesh=parts, in_specs=in_specs, out_specs=out_specs, check_vma=False)
```

```python
import math

import jax
import jax.numpy as jnp
from jax import lax
from jax.experimental import pallas as pl
from jax.experimental.pallas import tpu as pltpu
from jax.sharding import Mesh
from jax.sharding import PartitionSpec as P

HEAD = 128
NEG_FILL = -1e30
LOG2E = 1.4426950408889634
HIGHEST = lax.Precision.HIGHEST
TN = (((0,), (0,)), ((), ()))
NT = (((1,), (1,)), ((), ()))
HEADS_AT_ONCE = 2


def attention(where, parts, kv):
    devices, padded, _ = kv.shape
    tokens = HEAD
    block = 2 * tokens
    chips = devices // 2
    length = devices * tokens
    heads = parts[0].shape[1] // (2 * HEAD)
    steps = heads // HEADS_AT_ONCE
    wide = HEADS_AT_ONCE * HEAD
    columns = HEADS_AT_ONCE * block
    scale = 1.0 / math.sqrt(HEAD)
    power = scale * LOG2E

    def kernel(
        at, q0, q1, q2, q3, g0, g1, g2, g3, k_ref, v_ref, dq_ref, dk_ref, dv_ref,
        s_scr, d_scr, bias, k_turned, dq_acc, dk_acc, dv_acc,
    ):
        step = pl.program_id(0)
        core = at[0]
        chip = at[1 + step // steps]

        def place(index):
            return jnp.where(index < tokens, index + core * tokens, index - core * tokens)

        def starts(device):
            high = k_ref[device, tokens : tokens + 1, :].astype(jnp.float32)
            low = v_ref[device, tokens : tokens + 1, :].astype(jnp.float32)
            return high * 64.0 + low

        start = jnp.concatenate(
            [starts(2 * chip + core), starts(2 * chip + 1 - core)], axis=1
        )
        first = jnp.min(start).astype(jnp.int32) // block

        def span_of(j):
            return pl.ds(pl.multiple_of(j * block, block), block)

        def rows_of(ref, j):
            return ref[pl.ds(2 * j, 2), :tokens, :].reshape(block, HEAD)

        @pl.when(lax.rem(step, steps) == 0)
        def _():
            q_pos = chip * block + place(lax.broadcasted_iota(jnp.int32, (block, block), 1))
            k_off = lax.broadcasted_iota(jnp.int32, (block, block), 0)
            begin = start.astype(jnp.int32)

            def fill(j, _):
                k_pos = j * block + k_off
                ok = (k_pos <= q_pos) & (k_pos >= begin)
                bias[span_of(j), :] = jnp.where(ok, 0.0, NEG_FILL)
                return 0

            lax.fori_loop(first, chip + 1, fill, 0)

        @pl.when(step == 0)
        def _():
            dk_acc[...] = jnp.zeros_like(dk_acc)
            dv_acc[...] = jnp.zeros_like(dv_acc)
            for j in range(chips):
                k_turned[j] = (
                    k_ref[2 * j : 2 * j + 2, :tokens, :].reshape(block, HEAD).astype(jnp.float32).T
                ).astype(jnp.bfloat16)

        def stacked(a, b, c, d):
            x = jnp.where(step < steps, a[...], c[...])
            y = jnp.where(step < steps, b[...], d[...])
            rows = []
            for n in range(HEADS_AT_ONCE):
                rows += [x[:, n * HEAD : (n + 1) * HEAD], y[:, n * HEAD : (n + 1) * HEAD]]
            return jnp.concatenate(rows, axis=0)

        q = stacked(q0, q1, q2, q3)
        g = stacked(g0, g1, g2, g3)

        def fold(x):
            return x.reshape(block // 8, 8, columns)

        def score_step(j, top):
            s = lax.dot_general(rows_of(k_ref, j), q, NT, preferred_element_type=jnp.float32)
            b = bias[span_of(j), :]
            s = s + jnp.concatenate([b] * HEADS_AT_ONCE, axis=1)
            s_scr[span_of(j), :] = s
            return jnp.maximum(top, jnp.max(fold(s), axis=0))

        top = lax.fori_loop(
            first, chip + 1, score_step, jnp.full((8, columns), NEG_FILL, jnp.float32)
        )
        top = jnp.max(top, axis=0, keepdims=True)

        def prob_step(j, carry):
            total, mix = carry
            span = span_of(j)
            p = jnp.exp2((s_scr[span, :] - top) * power)
            d = lax.dot_general(rows_of(v_ref, j), g, NT, preferred_element_type=jnp.float32)
            s_scr[span, :] = p
            d_scr[span, :] = d
            return (total + jnp.sum(fold(p), axis=0), mix + jnp.sum(fold(p * d), axis=0))

        zero = jnp.zeros((8, columns), jnp.float32)
        total, mix = lax.fori_loop(first, chip + 1, prob_step, (zero, zero))
        inverse = 1.0 / jnp.sum(total, axis=0, keepdims=True)
        mix = jnp.sum(mix, axis=0, keepdims=True) * inverse
        dq_acc[...] = jnp.zeros_like(dq_acc)

        def grad_step(j, _):
            span = span_of(j)
            p = s_scr[span, :] * inverse
            ds = (p * (d_scr[span, :] - mix)).astype(jnp.bfloat16)
            low = p.astype(jnp.bfloat16)
            dv_acc[span, :] += jnp.dot(low, g, preferred_element_type=jnp.float32)
            dk_acc[span, :] += jnp.dot(ds, q, preferred_element_type=jnp.float32)
            dq_acc[...] += jnp.dot(k_turned[j], ds, preferred_element_type=jnp.float32)
            return 0

        lax.fori_loop(first, chip + 1, grad_step, 0)
        dq = (dq_acc[...] * scale).T.astype(jnp.bfloat16)
        for n in range(HEADS_AT_ONCE):
            dq_ref[:, n * HEAD : (n + 1) * HEAD] = dq[n * block : (n + 1) * block]

        @pl.when(step == 2 * steps - 1)
        def _():
            dk_ref[...] = (dk_acc[...] * scale).astype(jnp.bfloat16)
            dv_ref[...] = dv_acc[...].astype(jnp.bfloat16)

    whole = pl.BlockSpec((length, HEAD), lambda s, at: (0, 0))
    queries_at = pl.BlockSpec((block, wide), lambda s, at: (s // steps, s % steps))
    flops = 5 * 2 * length * block * heads * HEAD
    return pl.pallas_call(
        kernel,
        grid_spec=pltpu.PrefetchScalarGridSpec(
            num_scalar_prefetch=1,
            grid=(2 * steps,),
            in_specs=[
                *[pl.BlockSpec((tokens, wide), lambda s, at: (0, s % steps))] * 4,
                *[pl.BlockSpec((tokens, wide), lambda s, at: (0, steps + s % steps))] * 4,
                pl.BlockSpec((devices, padded, HEAD), lambda s, at: (0, 0, 0)),
                pl.BlockSpec((devices, padded, HEAD), lambda s, at: (0, 0, 1)),
            ],
            out_specs=[queries_at, whole, whole],
            scratch_shapes=[
                pltpu.VMEM((length, columns), jnp.float32),
                pltpu.VMEM((length, columns), jnp.float32),
                pltpu.VMEM((length, block), jnp.float32),
                pltpu.VMEM((chips, HEAD, block), jnp.bfloat16),
                pltpu.VMEM((HEAD, columns), jnp.float32),
                pltpu.VMEM((length, HEAD), jnp.float32),
                pltpu.VMEM((length, HEAD), jnp.float32),
            ],
        ),
        out_shape=[
            jax.ShapeDtypeStruct((2 * block, heads * HEAD), jnp.bfloat16),
            jax.ShapeDtypeStruct((length, HEAD), jnp.bfloat16),
            jax.ShapeDtypeStruct((length, HEAD), jnp.bfloat16),
        ],
        compiler_params=pltpu.CompilerParams(
            dimension_semantics=("arbitrary",), vmem_limit_bytes=40 * 1024 * 1024
        ),
        cost_estimate=pl.CostEstimate(
            flops=8 * flops, bytes_accessed=8 * 1024 * 1024, transcendentals=0
        ),
        name="attention",
    )(where, *parts, *parts, kv, kv)


VMEM = pl.BlockSpec(memory_space=pltpu.VMEM)
SMEM = pl.BlockSpec(memory_space=pltpu.SMEM)


def pack_keys(keys, values, starts, devices):
    tokens = keys.shape[0]

    def kernel(k_ref, v_ref, s_ref, out_ref):
        start = s_ref[...]
        high = jnp.right_shift(start, 6).astype(jnp.float32)
        low = jnp.bitwise_and(start, 63).astype(jnp.float32)
        row = jnp.concatenate([high, low], axis=1)
        first = lax.broadcasted_iota(jnp.int32, (16, 2 * tokens), 0) == 0
        extra = jnp.where(first, row, 0.0).astype(jnp.bfloat16)
        for n in range(devices):
            h = 2 * (n % 2) + (n >= devices // 2)
            out_ref[n, :tokens, :HEAD] = k_ref[:, h * HEAD : (h + 1) * HEAD]
            out_ref[n, :tokens, HEAD:] = v_ref[:, h * HEAD : (h + 1) * HEAD]
            out_ref[n, tokens:, :] = extra

    return pl.pallas_call(
        kernel,
        out_shape=jax.ShapeDtypeStruct((devices, tokens + 16, 2 * HEAD), jnp.bfloat16),
        in_specs=[VMEM] * 3,
        out_specs=VMEM,
        name="pack_keys",
    )(keys, values, starts)


def pack_queries(heads, queries, d_out, group):
    tokens = queries.shape[0]

    def kernel(h_ref, q_ref, g_ref, *outs):
        for n, out in enumerate(outs):
            span = pl.ds(pl.multiple_of(h_ref[n] * group, group), group)
            out[:, :group] = q_ref[:, span]
            out[:, group:] = g_ref[:, span]

    return pl.pallas_call(
        kernel,
        out_shape=[jax.ShapeDtypeStruct((tokens, 2 * group), jnp.bfloat16)] * 4,
        in_specs=[SMEM, VMEM, VMEM],
        out_specs=[VMEM] * 4,
        name="pack_queries",
    )(heads, queries, d_out)


def unpack_queries(heads, parts, group):
    tokens = parts[0].shape[0]

    def kernel(h_ref, *refs):
        for n in range(4):
            span = pl.ds(pl.multiple_of(h_ref[n] * group, group), group)
            refs[4][:, span] = refs[n][...]

    return pl.pallas_call(
        kernel,
        out_shape=jax.ShapeDtypeStruct((tokens, 4 * group), jnp.bfloat16),
        in_specs=[SMEM] + [VMEM] * 4,
        out_specs=VMEM,
        name="unpack_queries",
    )(heads, *parts)


def gradient(where, turned, mine, theirs, error):
    devices, rows, tokens = turned.shape
    width = mine.shape[2]

    def kernel(at, f_ref, m_ref, t_ref, e_ref, out_ref, low_ref):
        core = at[0]
        total = e_ref[...]
        for c in range(devices // 2):
            total = total + jnp.dot(
                f_ref[2 * c + core], m_ref[c], preferred_element_type=jnp.float32
            )
            total = total + jnp.dot(
                f_ref[2 * c + 1 - core], t_ref[c], preferred_element_type=jnp.float32
            )
        out_ref[...] = total
        low_ref[...] = total.astype(jnp.bfloat16)

    return pl.pallas_call(
        kernel,
        out_shape=[
            jax.ShapeDtypeStruct((rows, width), jnp.float32),
            jax.ShapeDtypeStruct((rows, width), jnp.bfloat16),
        ],
        in_specs=[SMEM] + [VMEM] * 4,
        out_specs=[VMEM] * 2,
        compiler_params=pltpu.CompilerParams(vmem_limit_bytes=32 * 1024 * 1024),
        name="gradient",
    )(where, turned, mine, theirs, error)


def inverse_factor(parts):
    count, size, _ = parts.shape
    tiles = size // 8

    def kernel(g_ref, out_ref):
        sub = lax.broadcasted_iota(jnp.int32, (8, 1), 0)
        lane = lax.broadcasted_iota(jnp.int32, (8, size), 1)
        row8 = lax.broadcasted_iota(jnp.int32, (8, size), 0)
        left, right = [], []
        for t in range(tiles):
            total = g_ref[0, 8 * t : 8 * t + 8, :]
            for n in range(1, count):
                total = total + g_ref[n, 8 * t : 8 * t + 8, :]
            left.append(total)
            right.append(jnp.where(lane == row8 + 8 * t, 1.0, 0.0))
        for j in range(0, size, 2):
            t0, r = j // 8, j % 8
            l0, l1 = left[t0][r : r + 1, :], left[t0][r + 1 : r + 2, :]
            r0, r1 = right[t0][r : r + 1, :], right[t0][r + 1 : r + 2, :]
            a, b, c = l0[:, j : j + 1], l0[:, j + 1 : j + 2], l1[:, j + 1 : j + 2]
            det = a * c - b * b
            inv = 1.0 / det
            ai, bi, ci = a * inv, b * inv, c * inv
            ul, vl = ci * l0 - bi * l1, ai * l1 - bi * l0
            ur, vr = ci * r0 - bi * r1, ai * r1 - bi * r0
            over = 1.0 / a
            out_ref[j : j + 1, :] = r0 * jnp.sqrt(over)
            out_ref[j + 1 : j + 2, :] = (r1 - (b * over) * r0) * jnp.sqrt(ai)
            for t in range(t0, tiles):
                x, y = left[t][:, j : j + 1], left[t][:, j + 1 : j + 2]
                if t == t0:
                    if r == 6:
                        continue
                    x = jnp.where(sub > r + 1, x, 0.0)
                    y = jnp.where(sub > r + 1, y, 0.0)
                left[t] = left[t] - (x * ul + y * vl)
                right[t] = right[t] - (x * ur + y * vr)

    return pl.pallas_call(
        kernel,
        out_shape=jax.ShapeDtypeStruct((size, size), jnp.float32),
        in_specs=[VMEM],
        out_specs=VMEM,
        cost_estimate=pl.CostEstimate(
            flops=8 * 10**9, bytes_accessed=10**6, transcendentals=0
        ),
        name="inverse_factor",
    )(parts)


def finish(where, p_sum, inverse, moment, their_moment, combined, replicas):
    rows, width = combined.shape
    rank = p_sum.shape[1]
    half = moment.shape[0]

    def kernel(at, p_ref, i_ref, m_ref, t_ref, c_ref, comp_ref, q_ref, new_ref):
        core = at[0]
        inv = i_ref[...]

        def product(x, y):
            return lax.dot_general(
                x, y, NT, precision=HIGHEST, preferred_element_type=jnp.float32
            )

        q_ref[pl.ds(pl.multiple_of(core * half, half), half), :] = (
            product(m_ref[...], inv) * (1.0 / replicas)
        )
        q_ref[pl.ds(pl.multiple_of((1 - core) * half, half), half), :] = (
            product(t_ref[...], inv) * (1.0 / replicas)
        )
        p_hat = product(p_ref[...], inv)
        out = product(p_hat, q_ref[...])
        comp_ref[...] = out
        new_ref[0] = c_ref[...] - out

    return pl.pallas_call(
        kernel,
        out_shape=[
            jax.ShapeDtypeStruct((rows, width), jnp.float32),
            jax.ShapeDtypeStruct((width, rank), jnp.float32),
            jax.ShapeDtypeStruct((1, rows, width), jnp.float32),
        ],
        in_specs=[SMEM] + [VMEM] * 5,
        out_specs=[VMEM] * 3,
        compiler_params=pltpu.CompilerParams(vmem_limit_bytes=32 * 1024 * 1024),
        name="finish",
    )(where, p_sum, inverse, moment, their_moment, combined)


def body(queries, keys, values, d_out, features, doc_start, error, q_init):
    tokens = queries.shape[0]
    width_kv = keys.shape[1]
    group = queries.shape[1] // (width_kv // HEAD)
    chips = lax.axis_size("chip")
    devices = 2 * chips
    replicas = lax.axis_size("dp")
    core = lax.axis_index("core")
    chip = lax.axis_index("chip")
    upper = (chip >= chips // 2).astype(jnp.int32)
    f32, bf16 = jnp.float32, jnp.bfloat16
    ctx = ("chip", "core")

    def swap(x):
        return lax.ppermute(x, "core", [(0, 1), (1, 0)])

    def piece(x, size, index, axis=1):
        return lax.dynamic_slice_in_dim(x, index * size, size, axis)

    def move(x, cross, turn):
        pairs = []
        for c in range(chips):
            for h in range(2):
                to = (chips - 1 - c if cross else c) * 2 + (1 - h if turn else h)
                pairs.append((2 * c + h, to))
        return lax.ppermute(x, ctx, pairs)

    def exchange(x, axis):
        return lax.all_to_all(x, axis, 0, 0)

    def spread(x, axis, size):
        return exchange(jnp.broadcast_to(x[None], (size,) + x.shape), axis)

    def head_of(cross, turn):
        return 2 * (1 - core if turn else core) + (1 - upper if cross else upper)

    ways = [(False, False), (False, True), (True, False), (True, True)]
    heads = jnp.stack([head_of(*way) for way in ways]).astype(jnp.int32)
    kv = exchange(pack_keys(keys, values, doc_start[None, :], devices), ctx)
    parts = pack_queries(heads, queries, d_out, group)
    parts = [parts[0]] + [move(x, *way) for x, way in zip(parts[1:], ways[1:])]

    rows = features.shape[1] // devices
    feat = jnp.transpose(features).reshape(devices, rows, tokens)
    kv, feat = lax.optimization_barrier((kv, feat))
    feat = exchange(feat, ctx)

    where = jnp.stack([core, chip, chips - 1 - chip]).astype(jnp.int32)
    dq, dk, dv = attention(where, parts, kv)
    dk, feat = lax.optimization_barrier((dk, feat))

    def to_owner(x):
        x = exchange(x.reshape(devices, tokens, HEAD), ctx)
        x = x.reshape(2, chips // 2, 2, tokens, HEAD).astype(f32)
        x = jnp.sum(x, axis=1).astype(bf16)
        return jnp.concatenate([x[0, 0], x[1, 0], x[0, 1], x[1, 1]], axis=1)

    d_key = to_owner(dk)
    dk_mine = spread(d_key, "chip", chips)
    dk_theirs = swap(dk_mine)
    combined, low = gradient(where, feat, dk_mine, dk_theirs, error.reshape(rows, width_kv))

    shares = low.reshape(replicas, rows // replicas, width_kv)
    shares, dv, dq = lax.optimization_barrier((shares, dv, dq))
    shares = exchange(shares, "dp")
    dv = dv.reshape(chips, 2 * tokens, HEAD)
    sums = []
    for low_k in (0, chips // 2):
        total = None
        for k in range(low_k, low_k + chips // 2):
            x = piece(dv, 1, jnp.bitwise_xor(chip, k), 0)[0]
            if k:
                x = lax.ppermute(x, "chip", [(i, i ^ k) for i in range(chips)])
            x = x.astype(f32)
            total = x if total is None else total + x
        sums.append(total.astype(bf16))
    share = jnp.sum(shares.astype(f32), axis=0).astype(bf16)
    share, *sums = lax.optimization_barrier((share, *sums))
    total = spread(share, "dp", replicas).reshape(rows, width_kv)
    dv_half = jnp.where(
        upper == 0,
        jnp.concatenate(sums, axis=1),
        jnp.concatenate(sums[::-1], axis=1),
    )
    dv_mine = piece(dv_half, tokens, core, 0)
    dv_theirs = swap(piece(dv_half, tokens, 1 - core, 0))
    d_value = jnp.where(
        core == 0,
        jnp.concatenate([dv_mine, dv_theirs], axis=1),
        jnp.concatenate([dv_theirs, dv_mine], axis=1),
    )
    back = [dq[:tokens]] + [
        move(dq[n * tokens : (n + 1) * tokens], *ways[n]) for n in range(1, 4)
    ]
    total, *back = lax.optimization_barrier((total, *back))
    d_query = unpack_queries(heads, back, group)

    total = total.astype(f32)
    p_sum = jnp.dot(total, q_init, precision=HIGHEST)
    gram = lax.dot_general(p_sum, p_sum, TN, precision=HIGHEST)
    gram = spread(gram + swap(gram), "chip", chips)
    moment = lax.dot_general(total, p_sum, TN, precision=HIGHEST)
    size = width_kv // 2
    moment = piece(moment, size, core, 0) + swap(piece(moment, size, 1 - core, 0))
    moment, gram = lax.optimization_barrier((moment.astype(bf16), gram))
    moment = jnp.sum(spread(moment, "chip", chips).astype(f32), axis=0)
    their_moment = swap(moment)
    inverse = inverse_factor(gram)
    compressed, q_factor, new_error = finish(
        where, p_sum, inverse, moment, their_moment, combined, replicas
    )
    return (d_query, d_key, d_value, compressed, q_factor, new_error)


def solution(mesh):
    replicas, ctx = mesh.devices.shape
    parts = Mesh(mesh.devices.reshape(replicas, ctx // 2, 2), ("dp", "chip", "core"))
    everywhere = ("dp", "chip", "core")
    tokens = P(everywhere, None)
    in_specs = (
        tokens, tokens, tokens, tokens, tokens, P(everywhere), P("dp", ("chip", "core"), None), P(),
    )
    out_specs = (
        tokens, tokens, tokens, P(("chip", "core"), None), P(), P("dp", ("chip", "core"), None),
    )
    return jax.shard_map(body, mesh=parts, in_specs=in_specs, out_specs=out_specs, check_vma=False)
```

```python
import math

import jax
import jax.numpy as jnp
from jax import lax
from jax.experimental import pallas as pl
from jax.experimental.pallas import tpu as pltpu
from jax.sharding import Mesh
from jax.sharding import PartitionSpec as P

HEAD = 128
NEG_FILL = -1e30
LOG2E = 1.4426950408889634
HIGHEST = lax.Precision.HIGHEST
TN = (((0,), (0,)), ((), ()))
NT = (((1,), (1,)), ((), ()))
HEADS_AT_ONCE = 6


def attention(where, parts, kv):
    devices, padded, _ = kv.shape
    tokens = HEAD
    block = 2 * tokens
    chips = devices // 2
    length = devices * tokens
    heads = parts[0].shape[1] // (2 * HEAD)
    steps = heads // HEADS_AT_ONCE
    wide = HEADS_AT_ONCE * HEAD
    columns = HEADS_AT_ONCE * block
    scale = 1.0 / math.sqrt(HEAD)
    power = scale * LOG2E

    def kernel(
        at, q0, q1, q2, q3, g0, g1, g2, g3, k_ref, v_ref, dq_ref, dkv_ref,
        s_scr, d_scr, bias, k_turned, dq_acc, dk_acc, dv_acc,
    ):
        step = pl.program_id(0)
        core = at[0]
        chip = at[1 + step // steps]

        def place(index):
            return jnp.where(index < tokens, index + core * tokens, index - core * tokens)

        def starts(device):
            high = k_ref[device, tokens : tokens + 1, :].astype(jnp.float32)
            low = v_ref[device, tokens : tokens + 1, :].astype(jnp.float32)
            return high * 64.0 + low

        start = jnp.concatenate(
            [starts(2 * chip + core), starts(2 * chip + 1 - core)], axis=1
        )
        first = jnp.min(start).astype(jnp.int32) // block

        def span_of(j):
            return pl.ds(pl.multiple_of(j * block, block), block)

        def rows_of(ref, j):
            return ref[pl.ds(2 * j, 2), :tokens, :].reshape(block, HEAD)

        @pl.when(lax.rem(step, steps) == 0)
        def _():
            q_pos = chip * block + place(lax.broadcasted_iota(jnp.int32, (block, block), 1))
            k_off = lax.broadcasted_iota(jnp.int32, (block, block), 0)
            begin = start.astype(jnp.int32)

            def fill(j, _):
                k_pos = j * block + k_off
                ok = (k_pos <= q_pos) & (k_pos >= begin)
                bias[span_of(j), :] = jnp.where(ok, 0.0, NEG_FILL)
                return 0

            lax.fori_loop(first, chip + 1, fill, 0)

        @pl.when(step == 0)
        def _():
            dk_acc[...] = jnp.zeros_like(dk_acc)
            dv_acc[...] = jnp.zeros_like(dv_acc)
            for j in range(chips):
                k_turned[j] = (
                    k_ref[2 * j : 2 * j + 2, :tokens, :].reshape(block, HEAD).astype(jnp.float32).T
                ).astype(jnp.bfloat16)

        def stacked(a, b, c, d):
            x = jnp.where(step < steps, a[...], c[...])
            y = jnp.where(step < steps, b[...], d[...])
            rows = []
            for n in range(HEADS_AT_ONCE):
                rows += [x[:, n * HEAD : (n + 1) * HEAD], y[:, n * HEAD : (n + 1) * HEAD]]
            return jnp.concatenate(rows, axis=0)

        q = stacked(q0, q1, q2, q3)
        g = stacked(g0, g1, g2, g3)

        def fold(x):
            return x.reshape(block // 8, 8, columns)

        def score_step(j, top):
            s = lax.dot_general(rows_of(k_ref, j), q, NT, preferred_element_type=jnp.float32)
            b = bias[span_of(j), :]
            s = s + jnp.concatenate([b] * HEADS_AT_ONCE, axis=1)
            s_scr[span_of(j), :] = s
            return jnp.maximum(top, jnp.max(fold(s), axis=0))

        top = lax.fori_loop(
            first, chip + 1, score_step, jnp.full((8, columns), NEG_FILL, jnp.float32)
        )
        top = jnp.max(top, axis=0, keepdims=True)

        def prob_step(j, carry):
            total, mix = carry
            span = span_of(j)
            p = jnp.exp2((s_scr[span, :] - top) * power)
            d = lax.dot_general(rows_of(v_ref, j), g, NT, preferred_element_type=jnp.float32)
            s_scr[span, :] = p
            d_scr[span, :] = d
            return (total + jnp.sum(fold(p), axis=0), mix + jnp.sum(fold(p * d), axis=0))

        zero = jnp.zeros((8, columns), jnp.float32)
        total, mix = lax.fori_loop(first, chip + 1, prob_step, (zero, zero))
        inverse = 1.0 / jnp.sum(total, axis=0, keepdims=True)
        mix = jnp.sum(mix, axis=0, keepdims=True) * inverse
        dq_acc[...] = jnp.zeros_like(dq_acc)

        def grad_step(j, _):
            span = span_of(j)
            p = s_scr[span, :] * inverse
            ds = (p * (d_scr[span, :] - mix)).astype(jnp.bfloat16)
            low = p.astype(jnp.bfloat16)
            dv_acc[span, :] += jnp.dot(low, g, preferred_element_type=jnp.float32)
            dk_acc[span, :] += jnp.dot(ds, q, preferred_element_type=jnp.float32)
            dq_acc[...] += jnp.dot(k_turned[j], ds, preferred_element_type=jnp.float32)
            return 0

        lax.fori_loop(first, chip + 1, grad_step, 0)
        dq = (dq_acc[...] * scale).T.astype(jnp.bfloat16)
        for n in range(HEADS_AT_ONCE):
            dq_ref[:, n * HEAD : (n + 1) * HEAD] = dq[n * block : (n + 1) * block]

        @pl.when(step == 2 * steps - 1)
        def _():
            dkv_ref[:, :HEAD] = (dk_acc[...] * scale).astype(jnp.bfloat16)
            dkv_ref[:, HEAD:] = dv_acc[...].astype(jnp.bfloat16)

    whole = pl.BlockSpec((length, 2 * HEAD), lambda s, at: (0, 0))
    queries_at = pl.BlockSpec((block, wide), lambda s, at: (s // steps, s % steps))
    flops = 5 * 2 * length * block * heads * HEAD
    return pl.pallas_call(
        kernel,
        grid_spec=pltpu.PrefetchScalarGridSpec(
            num_scalar_prefetch=1,
            grid=(2 * steps,),
            in_specs=[
                *[pl.BlockSpec((tokens, wide), lambda s, at: (0, s % steps))] * 4,
                *[pl.BlockSpec((tokens, wide), lambda s, at: (0, steps + s % steps))] * 4,
                pl.BlockSpec((devices, padded, HEAD), lambda s, at: (0, 0, 0)),
                pl.BlockSpec((devices, padded, HEAD), lambda s, at: (0, 0, 1)),
            ],
            out_specs=[queries_at, whole],
            scratch_shapes=[
                pltpu.VMEM((length, columns), jnp.float32),
                pltpu.VMEM((length, columns), jnp.float32),
                pltpu.VMEM((length, block), jnp.float32),
                pltpu.VMEM((chips, HEAD, block), jnp.bfloat16),
                pltpu.VMEM((HEAD, columns), jnp.float32),
                pltpu.VMEM((length, HEAD), jnp.float32),
                pltpu.VMEM((length, HEAD), jnp.float32),
            ],
        ),
        out_shape=[
            jax.ShapeDtypeStruct((2 * block, heads * HEAD), jnp.bfloat16),
            jax.ShapeDtypeStruct((length, 2 * HEAD), jnp.bfloat16),
        ],
        compiler_params=pltpu.CompilerParams(
            dimension_semantics=("arbitrary",), vmem_limit_bytes=40 * 1024 * 1024
        ),
        cost_estimate=pl.CostEstimate(
            flops=8 * flops, bytes_accessed=8 * 1024 * 1024, transcendentals=0
        ),
        name="attention",
    )(where, *parts, *parts, kv, kv)


VMEM = pl.BlockSpec(memory_space=pltpu.VMEM)
SMEM = pl.BlockSpec(memory_space=pltpu.SMEM)


def pack_keys(keys, values, starts, devices):
    tokens = keys.shape[0]

    def kernel(k_ref, v_ref, s_ref, out_ref):
        start = s_ref[...]
        high = jnp.right_shift(start, 6).astype(jnp.float32)
        low = jnp.bitwise_and(start, 63).astype(jnp.float32)
        row = jnp.concatenate([high, low], axis=1)
        first = lax.broadcasted_iota(jnp.int32, (16, 2 * tokens), 0) == 0
        extra = jnp.where(first, row, 0.0).astype(jnp.bfloat16)
        for n in range(devices):
            h = 2 * (n % 2) + (n >= devices // 2)
            out_ref[n, :tokens, :HEAD] = k_ref[:, h * HEAD : (h + 1) * HEAD]
            out_ref[n, :tokens, HEAD:] = v_ref[:, h * HEAD : (h + 1) * HEAD]
            out_ref[n, tokens:, :] = extra

    return pl.pallas_call(
        kernel,
        out_shape=jax.ShapeDtypeStruct((devices, tokens + 16, 2 * HEAD), jnp.bfloat16),
        in_specs=[VMEM] * 3,
        out_specs=VMEM,
        name="pack_keys",
    )(keys, values, starts)


def pack_queries(heads, queries, d_out, group):
    tokens = queries.shape[0]

    def kernel(h_ref, q_ref, g_ref, *outs):
        for n, out in enumerate(outs):
            span = pl.ds(pl.multiple_of(h_ref[n] * group, group), group)
            out[:, :group] = q_ref[:, span]
            out[:, group:] = g_ref[:, span]

    return pl.pallas_call(
        kernel,
        out_shape=[jax.ShapeDtypeStruct((tokens, 2 * group), jnp.bfloat16)] * 4,
        in_specs=[SMEM, VMEM, VMEM],
        out_specs=[VMEM] * 4,
        name="pack_queries",
    )(heads, queries, d_out)


def unpack_queries(heads, parts, group):
    tokens = parts[0].shape[0]

    def kernel(h_ref, *refs):
        for n in range(4):
            span = pl.ds(pl.multiple_of(h_ref[n] * group, group), group)
            refs[4][:, span] = refs[n][...]

    return pl.pallas_call(
        kernel,
        out_shape=jax.ShapeDtypeStruct((tokens, 4 * group), jnp.bfloat16),
        in_specs=[SMEM] + [VMEM] * 4,
        out_specs=VMEM,
        name="unpack_queries",
    )(heads, *parts)


def gradient(where, turned, mine, theirs, error):
    devices, rows, tokens = turned.shape
    width = mine.shape[2]

    def kernel(at, f_ref, m_ref, t_ref, e_ref, out_ref, low_ref):
        core = at[0]
        total = e_ref[...]
        for c in range(devices // 2):
            total = total + jnp.dot(
                f_ref[2 * c + core], m_ref[c], preferred_element_type=jnp.float32
            )
            total = total + jnp.dot(
                f_ref[2 * c + 1 - core], t_ref[c], preferred_element_type=jnp.float32
            )
        out_ref[...] = total
        low_ref[...] = total.astype(jnp.bfloat16)

    return pl.pallas_call(
        kernel,
        out_shape=[
            jax.ShapeDtypeStruct((rows, width), jnp.float32),
            jax.ShapeDtypeStruct((rows, width), jnp.bfloat16),
        ],
        in_specs=[SMEM] + [VMEM] * 4,
        out_specs=[VMEM] * 2,
        compiler_params=pltpu.CompilerParams(vmem_limit_bytes=32 * 1024 * 1024),
        name="gradient",
    )(where, turned, mine, theirs, error)


def inverse_factor(parts):
    count, size, _ = parts.shape
    tiles = size // 8
    shape = (8, size)

    def kernel(g_ref, out_ref):
        lane = lax.broadcasted_iota(jnp.int32, shape, 1)
        sub = lax.broadcasted_iota(jnp.int32, shape, 0)
        left, right = [], []
        for t in range(tiles):
            total = g_ref[0, 8 * t : 8 * t + 8, :]
            for n in range(1, count):
                total = total + g_ref[n, 8 * t : 8 * t + 8, :]
            left.append(total)
            right.append(jnp.where(lane == sub + 8 * t, 1.0, 0.0))

        def row(x, r):
            return jnp.broadcast_to(x[r : r + 1, :], shape)

        for p in range(tiles):
            spread = [
                [
                    jnp.broadcast_to(left[t][:, 8 * p + k : 8 * p + k + 1], shape)
                    for k in range(8)
                ]
                for t in range(p, tiles)
            ]
            for k in range(8):
                pivot = spread[0][k]
                root = lax.rsqrt(row(pivot, k))
                row_l = row(left[p], k) * root
                row_r = row(right[p], k) * root
                out_ref[8 * p + k : 8 * p + k + 1, :] = row_r[0:1]
                factors = [row(pivot, m) * root for m in range(k + 1, 8)]
                for t in range(p, tiles):
                    x = spread[t - p][k] * root
                    for m in range(k + 1, 8):
                        spread[t - p][m] = spread[t - p][m] - x * factors[m - k - 1]
                    left[t] = left[t] - x * row_l
                    right[t] = right[t] - x * row_r

    return pl.pallas_call(
        kernel,
        out_shape=jax.ShapeDtypeStruct((size, size), jnp.float32),
        in_specs=[VMEM],
        out_specs=VMEM,
        cost_estimate=pl.CostEstimate(
            flops=8 * 10**9, bytes_accessed=10**6, transcendentals=0
        ),
        name="inverse_factor",
    )(parts)


def finish(p_sum, inverse, q_factor, combined):
    rows, width = combined.shape

    def kernel(p_ref, i_ref, q_ref, c_ref, comp_ref, new_ref):
        def product(x, y):
            return lax.dot_general(
                x, y, NT, precision=HIGHEST, preferred_element_type=jnp.float32
            )

        out = product(product(p_ref[...], i_ref[...]), q_ref[...])
        comp_ref[...] = out
        new_ref[0] = c_ref[...] - out

    return pl.pallas_call(
        kernel,
        out_shape=[
            jax.ShapeDtypeStruct((rows, width), jnp.float32),
            jax.ShapeDtypeStruct((1, rows, width), jnp.float32),
        ],
        in_specs=[VMEM] * 4,
        out_specs=[VMEM] * 2,
        compiler_params=pltpu.CompilerParams(vmem_limit_bytes=32 * 1024 * 1024),
        name="finish",
    )(p_sum, inverse, q_factor, combined)


def body(queries, keys, values, d_out, features, doc_start, error, q_init):
    tokens = queries.shape[0]
    width_kv = keys.shape[1]
    group = queries.shape[1] // (width_kv // HEAD)
    chips = lax.axis_size("chip")
    devices = 2 * chips
    replicas = lax.axis_size("dp")
    core = lax.axis_index("core")
    chip = lax.axis_index("chip")
    upper = (chip >= chips // 2).astype(jnp.int32)
    f32, bf16 = jnp.float32, jnp.bfloat16
    ctx = ("chip", "core")

    def swap(x):
        return lax.ppermute(x, "core", [(0, 1), (1, 0)])

    def piece(x, size, index, axis=1):
        return lax.dynamic_slice_in_dim(x, index * size, size, axis)

    def move(x, cross, turn):
        pairs = []
        for c in range(chips):
            for h in range(2):
                to = (chips - 1 - c if cross else c) * 2 + (1 - h if turn else h)
                pairs.append((2 * c + h, to))
        return lax.ppermute(x, ctx, pairs)

    def exchange(x, axis):
        return lax.all_to_all(x, axis, 0, 0)

    def spread(x, axis, size):
        return exchange(jnp.broadcast_to(x[None], (size,) + x.shape), axis)

    def head_of(cross, turn):
        return 2 * (1 - core if turn else core) + (1 - upper if cross else upper)

    ways = [(False, False), (False, True), (True, False), (True, True)]
    heads = jnp.stack([head_of(*way) for way in ways]).astype(jnp.int32)
    kv = exchange(pack_keys(keys, values, doc_start[None, :], devices), ctx)
    parts = pack_queries(heads, queries, d_out, group)
    parts = [parts[0]] + [move(x, *way) for x, way in zip(parts[1:], ways[1:])]

    rows = features.shape[1] // devices
    feat = jnp.transpose(features).reshape(devices, rows, tokens)
    kv, feat = lax.optimization_barrier((kv, feat))
    feat = exchange(feat, ctx)

    where = jnp.stack([core, chip, chips - 1 - chip]).astype(jnp.int32)
    dq, dkv = attention(where, parts, kv)
    dkv, feat = lax.optimization_barrier((dkv, feat))

    home = exchange(dkv.reshape(devices, tokens, 2 * HEAD), ctx)
    home = home.reshape(2, chips // 2, 2, tokens, 2 * HEAD).astype(f32)
    home = jnp.sum(home, axis=1).astype(bf16)
    home = [home[0, 0], home[1, 0], home[0, 1], home[1, 1]]
    d_key = jnp.concatenate([x[:, :HEAD] for x in home], axis=1)
    d_value = jnp.concatenate([x[:, HEAD:] for x in home], axis=1)
    dk_mine = spread(d_key, "chip", chips)
    dk_theirs = swap(dk_mine)
    combined, low = gradient(where, feat, dk_mine, dk_theirs, error.reshape(rows, width_kv))

    shares = exchange(low.reshape(replicas, rows // replicas, width_kv), "dp")
    share = jnp.sum(shares.astype(f32), axis=0).astype(bf16)
    total = spread(share, "dp", replicas).reshape(rows, width_kv)

    back = [dq[:tokens]] + [
        move(dq[n * tokens : (n + 1) * tokens], *ways[n]) for n in range(1, 4)
    ]
    d_query = unpack_queries(heads, back, group)

    total = total.astype(f32)
    p_sum = jnp.dot(total, q_init, precision=HIGHEST)
    gram = lax.dot_general(p_sum, p_sum, TN, precision=HIGHEST)
    gram = spread(gram + swap(gram), "chip", chips)
    moment = lax.dot_general(total, p_sum, TN, precision=HIGHEST)
    size = width_kv // 2
    moment = piece(moment, size, core, 0) + swap(piece(moment, size, 1 - core, 0))
    moment, gram = lax.optimization_barrier((moment.astype(bf16), gram))
    moment = jnp.sum(spread(moment, "chip", chips).astype(f32), axis=0)
    inverse = inverse_factor(gram)
    q_mine = lax.dot_general(moment, inverse, NT, precision=HIGHEST) / replicas
    q_theirs = swap(q_mine)
    q_factor = jnp.where(
        core == 0, jnp.concatenate([q_mine, q_theirs]), jnp.concatenate([q_theirs, q_mine])
    )
    compressed, new_error = finish(p_sum, inverse, q_factor, combined)
    return (d_query, d_key, d_value, compressed, q_factor, new_error)


def solution(mesh):
    replicas, ctx = mesh.devices.shape
    parts = Mesh(mesh.devices.reshape(replicas, ctx // 2, 2), ("dp", "chip", "core"))
    everywhere = ("dp", "chip", "core")
    tokens = P(everywhere, None)
    in_specs = (
        tokens, tokens, tokens, tokens, tokens, P(everywhere), P("dp", ("chip", "core"), None), P(),
    )
    out_specs = (
        tokens, tokens, tokens, P(("chip", "core"), None), P(), P("dp", ("chip", "core"), None),
    )
    return jax.shard_map(body, mesh=parts, in_specs=in_specs, out_specs=out_specs, check_vma=False)
```

```python
import math

import jax
import jax.numpy as jnp
from jax import lax
from jax.experimental import pallas as pl
from jax.experimental.pallas import tpu as pltpu
from jax.sharding import Mesh
from jax.sharding import PartitionSpec as P

HEAD = 128
NEG_FILL = -1e30
LOG2E = 1.4426950408889634
HIGHEST = lax.Precision.HIGHEST
TN = (((0,), (0,)), ((), ()))
NT = (((1,), (1,)), ((), ()))
HEADS_AT_ONCE = 6
EARLY = 160


def attention(where, parts, kv, extra):
    devices, padded, _ = kv.shape
    tokens = HEAD
    block = 2 * tokens
    chips = devices // 2
    length = devices * tokens
    heads = parts[0].shape[1] // (2 * HEAD)
    steps = heads // HEADS_AT_ONCE
    wide = HEADS_AT_ONCE * HEAD
    columns = HEADS_AT_ONCE * block
    scale = 1.0 / math.sqrt(HEAD)
    power = scale * LOG2E

    def kernel(
        at, q0, q1, q2, q3, g0, g1, g2, g3, k_ref, v_ref, e_ref, dq_ref, out_ref,
        s_scr, d_scr, bias, k_turned, dq_acc, dk_acc, dv_acc,
    ):
        step = pl.program_id(0)
        core = at[0]
        chip = at[1 + step // steps]

        def place(index):
            return jnp.where(index < tokens, index + core * tokens, index - core * tokens)

        def starts(device):
            high = k_ref[device, tokens : tokens + 1, :].astype(jnp.float32)
            low = v_ref[device, tokens : tokens + 1, :].astype(jnp.float32)
            return high * 64.0 + low

        start = jnp.concatenate(
            [starts(2 * chip + core), starts(2 * chip + 1 - core)], axis=1
        )
        first = jnp.min(start).astype(jnp.int32) // block

        def span_of(j):
            return pl.ds(pl.multiple_of(j * block, block), block)

        def rows_of(ref, j):
            return ref[pl.ds(2 * j, 2), :tokens, :].reshape(block, HEAD)

        @pl.when(lax.rem(step, steps) == 0)
        def _():
            q_pos = chip * block + place(lax.broadcasted_iota(jnp.int32, (block, block), 1))
            k_off = lax.broadcasted_iota(jnp.int32, (block, block), 0)
            begin = start.astype(jnp.int32)

            def fill(j, _):
                k_pos = j * block + k_off
                ok = (k_pos <= q_pos) & (k_pos >= begin)
                bias[span_of(j), :] = jnp.where(ok, 0.0, NEG_FILL)
                return 0

            lax.fori_loop(first, chip + 1, fill, 0)

        @pl.when(step == 0)
        def _():
            dk_acc[...] = jnp.zeros_like(dk_acc)
            dv_acc[...] = jnp.zeros_like(dv_acc)
            for j in range(chips):
                k_turned[j] = (
                    k_ref[2 * j : 2 * j + 2, :tokens, :].reshape(block, HEAD).astype(jnp.float32).T
                ).astype(jnp.bfloat16)

        def stacked(a, b, c, d):
            x = jnp.where(step < steps, a[...], c[...])
            y = jnp.where(step < steps, b[...], d[...])
            rows = []
            for n in range(HEADS_AT_ONCE):
                rows += [x[:, n * HEAD : (n + 1) * HEAD], y[:, n * HEAD : (n + 1) * HEAD]]
            return jnp.concatenate(rows, axis=0)

        q = stacked(q0, q1, q2, q3)
        g = stacked(g0, g1, g2, g3)

        def fold(x):
            return x.reshape(block // 8, 8, columns)

        def score_step(j, top):
            s = lax.dot_general(rows_of(k_ref, j), q, NT, preferred_element_type=jnp.float32)
            b = bias[span_of(j), :]
            s = s + jnp.concatenate([b] * HEADS_AT_ONCE, axis=1)
            s_scr[span_of(j), :] = s
            return jnp.maximum(top, jnp.max(fold(s), axis=0))

        top = lax.fori_loop(
            first, chip + 1, score_step, jnp.full((8, columns), NEG_FILL, jnp.float32)
        )
        top = jnp.max(top, axis=0, keepdims=True)

        def prob_step(j, carry):
            total, mix = carry
            span = span_of(j)
            p = jnp.exp2((s_scr[span, :] - top) * power)
            d = lax.dot_general(rows_of(v_ref, j), g, NT, preferred_element_type=jnp.float32)
            s_scr[span, :] = p
            d_scr[span, :] = d
            return (total + jnp.sum(fold(p), axis=0), mix + jnp.sum(fold(p * d), axis=0))

        zero = jnp.zeros((8, columns), jnp.float32)
        total, mix = lax.fori_loop(first, chip + 1, prob_step, (zero, zero))
        inverse = 1.0 / jnp.sum(total, axis=0, keepdims=True)
        mix = jnp.sum(mix, axis=0, keepdims=True) * inverse
        dq_acc[...] = jnp.zeros_like(dq_acc)

        def grad_step(j, _):
            span = span_of(j)
            p = s_scr[span, :] * inverse
            ds = (p * (d_scr[span, :] - mix)).astype(jnp.bfloat16)
            low = p.astype(jnp.bfloat16)
            dv_acc[span, :] += jnp.dot(low, g, preferred_element_type=jnp.float32)
            dk_acc[span, :] += jnp.dot(ds, q, preferred_element_type=jnp.float32)
            dq_acc[...] += jnp.dot(k_turned[j], ds, preferred_element_type=jnp.float32)
            return 0

        lax.fori_loop(first, chip + 1, grad_step, 0)
        dq = (dq_acc[...] * scale).T.astype(jnp.bfloat16)
        for n in range(HEADS_AT_ONCE):
            dq_ref[:, n * HEAD : (n + 1) * HEAD] = dq[n * block : (n + 1) * block]

        @pl.when(step == 2 * steps - 1)
        def _():
            dk = (dk_acc[...] * scale).astype(jnp.bfloat16)
            out_ref[:, :tokens, :] = dk.reshape(devices, tokens, HEAD)
            dv = dv_acc[...].astype(jnp.bfloat16)
            out_ref[:, tokens:block, :] = dv.reshape(devices, tokens, HEAD)
            out_ref[:, block:, :] = e_ref[...]

    more = extra.shape[1]
    whole = pl.BlockSpec((devices, block + more, HEAD), lambda s, at: (0, 0, 0))
    queries_at = pl.BlockSpec((block, wide), lambda s, at: (s // steps, s % steps))
    flops = 5 * 2 * length * block * heads * HEAD
    return pl.pallas_call(
        kernel,
        grid_spec=pltpu.PrefetchScalarGridSpec(
            num_scalar_prefetch=1,
            grid=(2 * steps,),
            in_specs=[
                *[pl.BlockSpec((tokens, wide), lambda s, at: (0, s % steps))] * 4,
                *[pl.BlockSpec((tokens, wide), lambda s, at: (0, steps + s % steps))] * 4,
                pl.BlockSpec((devices, padded, HEAD), lambda s, at: (0, 0, 0)),
                pl.BlockSpec((devices, padded, HEAD), lambda s, at: (0, 0, 1)),
                pl.BlockSpec((devices, more, HEAD), lambda s, at: (0, 0, 0)),
            ],
            out_specs=[queries_at, whole],
            scratch_shapes=[
                pltpu.VMEM((length, columns), jnp.float32),
                pltpu.VMEM((length, columns), jnp.float32),
                pltpu.VMEM((length, block), jnp.float32),
                pltpu.VMEM((chips, HEAD, block), jnp.bfloat16),
                pltpu.VMEM((HEAD, columns), jnp.float32),
                pltpu.VMEM((length, HEAD), jnp.float32),
                pltpu.VMEM((length, HEAD), jnp.float32),
            ],
        ),
        out_shape=[
            jax.ShapeDtypeStruct((2 * block, heads * HEAD), jnp.bfloat16),
            jax.ShapeDtypeStruct((devices, block + more, HEAD), jnp.bfloat16),
        ],
        compiler_params=pltpu.CompilerParams(
            dimension_semantics=("arbitrary",), vmem_limit_bytes=44 * 1024 * 1024
        ),
        cost_estimate=pl.CostEstimate(
            flops=8 * flops, bytes_accessed=8 * 1024 * 1024, transcendentals=0
        ),
        name="attention",
    )(where, *parts, *parts, kv, kv, extra)


VMEM = pl.BlockSpec(memory_space=pltpu.VMEM)
SMEM = pl.BlockSpec(memory_space=pltpu.SMEM)


def pack_keys(keys, values, starts, devices):
    tokens = keys.shape[0]

    def kernel(k_ref, v_ref, s_ref, out_ref):
        start = s_ref[...]
        high = jnp.right_shift(start, 6).astype(jnp.float32)
        low = jnp.bitwise_and(start, 63).astype(jnp.float32)
        row = jnp.concatenate([high, low], axis=1)
        first = lax.broadcasted_iota(jnp.int32, (16, 2 * tokens), 0) == 0
        extra = jnp.where(first, row, 0.0).astype(jnp.bfloat16)
        for n in range(devices):
            h = 2 * (n % 2) + (n >= devices // 2)
            out_ref[n, :tokens, :HEAD] = k_ref[:, h * HEAD : (h + 1) * HEAD]
            out_ref[n, :tokens, HEAD:] = v_ref[:, h * HEAD : (h + 1) * HEAD]
            out_ref[n, tokens:, :] = extra

    return pl.pallas_call(
        kernel,
        out_shape=jax.ShapeDtypeStruct((devices, tokens + 16, 2 * HEAD), jnp.bfloat16),
        in_specs=[VMEM] * 3,
        out_specs=VMEM,
        name="pack_keys",
    )(keys, values, starts)


def pack_queries(heads, queries, d_out, group):
    tokens = queries.shape[0]

    def kernel(h_ref, q_ref, g_ref, *outs):
        for n, out in enumerate(outs):
            span = pl.ds(pl.multiple_of(h_ref[n] * group, group), group)
            out[:, :group] = q_ref[:, span]
            out[:, group:] = g_ref[:, span]

    return pl.pallas_call(
        kernel,
        out_shape=[jax.ShapeDtypeStruct((tokens, 2 * group), jnp.bfloat16)] * 4,
        in_specs=[SMEM, VMEM, VMEM],
        out_specs=[VMEM] * 4,
        name="pack_queries",
    )(heads, queries, d_out)


def unpack_queries(heads, parts, group):
    tokens = parts[0].shape[0]

    def kernel(h_ref, *refs):
        for n in range(4):
            span = pl.ds(pl.multiple_of(h_ref[n] * group, group), group)
            refs[4][:, span] = refs[n][...]

    return pl.pallas_call(
        kernel,
        out_shape=jax.ShapeDtypeStruct((tokens, 4 * group), jnp.bfloat16),
        in_specs=[SMEM] + [VMEM] * 4,
        out_specs=VMEM,
        name="unpack_queries",
    )(heads, *parts)


def gradient(where, first, later, skip, mine, theirs, error):
    devices, early, _ = first.shape
    rows, width = error.shape

    def kernel(at, f_ref, l_ref, m_ref, t_ref, e_ref, out_ref, low_ref):
        core = at[0]
        top, rest = e_ref[:early, :], e_ref[early:, :]
        for c in range(devices // 2):
            for n, d_ref in ((2 * c + core, m_ref), (2 * c + 1 - core, t_ref)):
                d = d_ref[c]
                top = top + jnp.dot(f_ref[n], d, preferred_element_type=jnp.float32)
                rest = rest + jnp.dot(
                    l_ref[n, skip:, :], d, preferred_element_type=jnp.float32
                )
        out_ref[:early, :] = top
        out_ref[early:, :] = rest
        low_ref[:early, :] = top.astype(jnp.bfloat16)
        low_ref[early:, :] = rest.astype(jnp.bfloat16)

    return pl.pallas_call(
        kernel,
        out_shape=[
            jax.ShapeDtypeStruct((rows, width), jnp.float32),
            jax.ShapeDtypeStruct((rows, width), jnp.bfloat16),
        ],
        in_specs=[SMEM] + [VMEM] * 5,
        out_specs=[VMEM] * 2,
        compiler_params=pltpu.CompilerParams(vmem_limit_bytes=32 * 1024 * 1024),
        name="gradient",
    )(where, first, later, mine, theirs, error)


def moments(where, total, q_init):
    rows, width = total.shape
    rank = q_init.shape[1]
    half, part = width // 2, rank // 2

    def kernel(at, t_ref, q_ref, p_ref, mine_ref, other_ref, all_ref, gram_ref):
        core = at[0]
        x = t_ref[...].astype(jnp.float32)
        p = jnp.dot(x, q_ref[...], precision=HIGHEST, preferred_element_type=jnp.float32)
        p_ref[...] = p
        p_turned = p.T
        gram_ref[...] = jnp.dot(
            p_turned, p, precision=HIGHEST, preferred_element_type=jnp.float32
        )
        all_ref[...] = jnp.dot(
            p_turned, x, precision=HIGHEST, preferred_element_type=jnp.float32
        ).T
        for out, who in ((mine_ref, core), (other_ref, 1 - core)):
            out[:half, :] = all_ref[pl.ds(pl.multiple_of(who * half, half), half), :]
            out[half:, :] = gram_ref[pl.ds(pl.multiple_of(who * part, part), part), :]

    return pl.pallas_call(
        kernel,
        out_shape=[
            jax.ShapeDtypeStruct((rows, rank), jnp.float32),
            jax.ShapeDtypeStruct((half + part, rank), jnp.float32),
            jax.ShapeDtypeStruct((half + part, rank), jnp.float32),
        ],
        in_specs=[SMEM, VMEM, VMEM],
        out_specs=[VMEM] * 3,
        scratch_shapes=[
            pltpu.VMEM((width, rank), jnp.float32),
            pltpu.VMEM((rank, rank), jnp.float32),
        ],
        name="moments",
    )(where, total, q_init)


def pack_moments(mine, theirs, copies, half):
    count, rank = mine.shape
    part = count - half

    def kernel(m_ref, t_ref, out_ref):
        total = m_ref[...] + t_ref[...]
        gram = total[half:, :]
        high = gram.astype(jnp.bfloat16)
        gram = gram - high.astype(jnp.float32)
        mid = gram.astype(jnp.bfloat16)
        low = (gram - mid.astype(jnp.float32)).astype(jnp.bfloat16)
        whole = jnp.concatenate([total[:half, :].astype(jnp.bfloat16), high, mid, low], axis=0)
        for n in range(copies):
            out_ref[n] = whole

    return pl.pallas_call(
        kernel,
        out_shape=jax.ShapeDtypeStruct((copies, half + 3 * part, rank), jnp.bfloat16),
        in_specs=[VMEM] * 2,
        out_specs=VMEM,
        name="pack_moments",
    )(mine, theirs)


def sum_moments(parts, half):
    copies, count, rank = parts.shape
    part = (count - half) // 3

    def kernel(x_ref, out_ref):
        total = x_ref[0].astype(jnp.float32)
        for n in range(1, copies):
            total = total + x_ref[n].astype(jnp.float32)
        out_ref[:half, :] = total[:half, :]
        out_ref[half:, :] = (
            total[half : half + part, :]
            + total[half + part : half + 2 * part, :]
            + total[half + 2 * part :, :]
        )

    return pl.pallas_call(
        kernel,
        out_shape=jax.ShapeDtypeStruct((half + part, rank), jnp.float32),
        in_specs=[VMEM],
        out_specs=VMEM,
        name="sum_moments",
    )(parts)


def finish(where, p_sum, mine, theirs, combined, replicas):
    rows, width = combined.shape
    size = p_sum.shape[1]
    half, part = width // 2, size // 2
    tiles = size // 8
    shape = (8, size)

    def kernel(at, p_ref, m_ref, t_ref, c_ref, comp_ref, q_ref, new_ref, gram_ref, inv_ref, all_ref):
        core = at[0]
        for x, who in ((m_ref, core), (t_ref, 1 - core)):
            all_ref[pl.ds(pl.multiple_of(who * half, half), half), :] = x[:half, :]
            gram_ref[pl.ds(pl.multiple_of(who * part, part), part), :] = x[half:, :]
        lane = lax.broadcasted_iota(jnp.int32, shape, 1)
        sub = lax.broadcasted_iota(jnp.int32, shape, 0)
        left = [gram_ref[8 * t : 8 * t + 8, :] for t in range(tiles)]
        right = [jnp.where(lane == sub + 8 * t, 1.0, 0.0) for t in range(tiles)]
        def row(x, r):
            return jnp.broadcast_to(x[r : r + 1, :], shape)

        for p in range(tiles):
            spread = [
                [
                    jnp.broadcast_to(left[t][:, 8 * p + k : 8 * p + k + 1], shape)
                    for k in range(8)
                ]
                for t in range(p, tiles)
            ]
            for k in range(8):
                pivot = spread[0][k]
                root = lax.rsqrt(row(pivot, k))
                row_l = row(left[p], k) * root
                row_r = row(right[p], k) * root
                inv_ref[8 * p + k : 8 * p + k + 1, :] = row_r[0:1]
                factors = [row(pivot, m) * root for m in range(k + 1, 8)]
                for t in range(p, tiles):
                    x = spread[t - p][k] * root
                    for m in range(k + 1, 8):
                        spread[t - p][m] = spread[t - p][m] - x * factors[m - k - 1]
                    left[t] = left[t] - x * row_l
                    right[t] = right[t] - x * row_r

        def product(x, y):
            return lax.dot_general(
                x, y, NT, precision=HIGHEST, preferred_element_type=jnp.float32
            )

        inv = inv_ref[...]
        q = product(all_ref[...], inv) * (1.0 / replicas)
        q_ref[...] = q
        out = product(product(p_ref[...], inv), q)
        comp_ref[...] = out
        new_ref[0] = c_ref[...] - out

    return pl.pallas_call(
        kernel,
        out_shape=[
            jax.ShapeDtypeStruct((rows, width), jnp.float32),
            jax.ShapeDtypeStruct((width, size), jnp.float32),
            jax.ShapeDtypeStruct((1, rows, width), jnp.float32),
        ],
        in_specs=[SMEM] + [VMEM] * 4,
        out_specs=[VMEM] * 3,
        scratch_shapes=[
            pltpu.VMEM((size, size), jnp.float32),
            pltpu.VMEM((size, size), jnp.float32),
            pltpu.VMEM((width, size), jnp.float32),
        ],
        compiler_params=pltpu.CompilerParams(vmem_limit_bytes=32 * 1024 * 1024),
        name="finish",
    )(where, p_sum, mine, theirs, combined)


def body(queries, keys, values, d_out, features, doc_start, error, q_init):
    tokens = queries.shape[0]
    width_kv = keys.shape[1]
    group = queries.shape[1] // (width_kv // HEAD)
    chips = lax.axis_size("chip")
    devices = 2 * chips
    replicas = lax.axis_size("dp")
    core = lax.axis_index("core")
    chip = lax.axis_index("chip")
    upper = (chip >= chips // 2).astype(jnp.int32)
    f32, bf16 = jnp.float32, jnp.bfloat16
    ctx = ("chip", "core")

    def swap(x):
        return lax.ppermute(x, "core", [(0, 1), (1, 0)])

    def piece(x, size, index, axis=1):
        return lax.dynamic_slice_in_dim(x, index * size, size, axis)

    def move(x, cross, turn):
        pairs = []
        for c in range(chips):
            for h in range(2):
                to = (chips - 1 - c if cross else c) * 2 + (1 - h if turn else h)
                pairs.append((2 * c + h, to))
        return lax.ppermute(x, ctx, pairs)

    def exchange(x, axis):
        return lax.all_to_all(x, axis, 0, 0)

    def spread(x, axis, size):
        return exchange(jnp.broadcast_to(x[None], (size,) + x.shape), axis)

    def head_of(cross, turn):
        return 2 * (1 - core if turn else core) + (1 - upper if cross else upper)

    ways = [(False, False), (False, True), (True, False), (True, True)]
    heads = jnp.stack([head_of(*way) for way in ways]).astype(jnp.int32)
    kv = exchange(pack_keys(keys, values, doc_start[None, :], devices), ctx)
    parts = pack_queries(heads, queries, d_out, group)
    parts = [parts[0]] + [move(x, *way) for x, way in zip(parts[1:], ways[1:])]

    rows = features.shape[1] // devices
    turned = jnp.transpose(features).reshape(devices, rows, tokens)
    first, later = turned[:, :EARLY], turned[:, EARLY:]
    kv, first = lax.optimization_barrier((kv, first))
    first = exchange(first, ctx)

    where = jnp.stack([core, chip, chips - 1 - chip]).astype(jnp.int32)
    dq, home = attention(where, parts, kv, later)
    home, first = lax.optimization_barrier((home, first))

    later = exchange(home, ctx)
    home = later[:, : 2 * tokens, :]
    home = home.reshape(2, chips // 2, 2, 2 * tokens, HEAD).astype(f32)
    home = jnp.sum(home, axis=1).astype(bf16)
    home = [home[0, 0], home[1, 0], home[0, 1], home[1, 1]]
    d_key = jnp.concatenate([x[:tokens] for x in home], axis=1)
    d_value = jnp.concatenate([x[tokens:] for x in home], axis=1)
    dk_mine = spread(d_key, "chip", chips)
    dk_theirs = swap(dk_mine)
    combined, low = gradient(
        where, first, later, 2 * tokens, dk_mine, dk_theirs, error.reshape(rows, width_kv)
    )

    shares = exchange(low.reshape(replicas, rows // replicas, width_kv), "dp")
    share = jnp.sum(shares.astype(f32), axis=0).astype(bf16)
    total = spread(share, "dp", replicas).reshape(rows, width_kv)

    back = [dq[:tokens]] + [
        move(dq[n * tokens : (n + 1) * tokens], *ways[n]) for n in range(1, 4)
    ]
    d_query = unpack_queries(heads, back, group)

    half = width_kv // 2
    p_sum, mine, other = moments(where, total, q_init)
    part = sum_moments(exchange(pack_moments(mine, swap(other), chips, half), "chip"), half)
    compressed, q_factor, new_error = finish(where, p_sum, part, swap(part), combined, replicas)
    return (d_query, d_key, d_value, compressed, q_factor, new_error)


def solution(mesh):
    replicas, ctx = mesh.devices.shape
    parts = Mesh(mesh.devices.reshape(replicas, ctx // 2, 2), ("dp", "chip", "core"))
    everywhere = ("dp", "chip", "core")
    tokens = P(everywhere, None)
    in_specs = (
        tokens, tokens, tokens, tokens, tokens, P(everywhere), P("dp", ("chip", "core"), None), P(),
    )
    out_specs = (
        tokens, tokens, tokens, P(("chip", "core"), None), P(), P("dp", ("chip", "core"), None),
    )
    return jax.shard_map(body, mesh=parts, in_specs=in_specs, out_specs=out_specs, check_vma=False)
```

```python
import math

import jax
import jax.numpy as jnp
from jax import lax
from jax.experimental import pallas as pl
from jax.experimental.pallas import tpu as pltpu
from jax.sharding import Mesh
from jax.sharding import PartitionSpec as P

HEAD = 128
NEG_FILL = -1e30
LOG2E = 1.4426950408889634
HIGHEST = lax.Precision.HIGHEST
TN = (((0,), (0,)), ((), ()))
NT = (((1,), (1,)), ((), ()))
HEADS_AT_ONCE = 6


def attention(where, parts, kv):
    devices, padded, _ = kv.shape
    tokens = HEAD
    block = 2 * tokens
    chips = devices // 2
    length = devices * tokens
    heads = parts[0].shape[1] // (2 * HEAD)
    steps = heads // HEADS_AT_ONCE
    wide = HEADS_AT_ONCE * HEAD
    columns = HEADS_AT_ONCE * block
    scale = 1.0 / math.sqrt(HEAD)
    power = scale * LOG2E

    def kernel(
        at, q0, q1, q2, q3, g0, g1, g2, g3, k_ref, v_ref, dq_ref, dkv_ref,
        s_scr, d_scr, bias, k_turned, dq_acc, dk_acc, dv_acc,
    ):
        step = pl.program_id(0)
        core = at[0]
        chip = at[1 + step // steps]

        def place(index):
            return jnp.where(index < tokens, index + core * tokens, index - core * tokens)

        def starts(device):
            high = k_ref[device, tokens : tokens + 1, :].astype(jnp.float32)
            low = v_ref[device, tokens : tokens + 1, :].astype(jnp.float32)
            return high * 64.0 + low

        start = jnp.concatenate(
            [starts(2 * chip + core), starts(2 * chip + 1 - core)], axis=1
        )
        first = jnp.min(start).astype(jnp.int32) // block

        def span_of(j):
            return pl.ds(pl.multiple_of(j * block, block), block)

        def rows_of(ref, j):
            return ref[pl.ds(2 * j, 2), :tokens, :].reshape(block, HEAD)

        @pl.when(lax.rem(step, steps) == 0)
        def _():
            q_pos = chip * block + place(lax.broadcasted_iota(jnp.int32, (block, block), 1))
            k_off = lax.broadcasted_iota(jnp.int32, (block, block), 0)
            begin = start.astype(jnp.int32)

            def fill(j, _):
                k_pos = j * block + k_off
                ok = (k_pos <= q_pos) & (k_pos >= begin)
                bias[span_of(j), :] = jnp.where(ok, 0.0, NEG_FILL)
                return 0

            lax.fori_loop(first, chip + 1, fill, 0)

        @pl.when(step == 0)
        def _():
            dk_acc[...] = jnp.zeros_like(dk_acc)
            dv_acc[...] = jnp.zeros_like(dv_acc)
            for j in range(chips):
                k_turned[j] = (
                    k_ref[2 * j : 2 * j + 2, :tokens, :].reshape(block, HEAD).astype(jnp.float32).T
                ).astype(jnp.bfloat16)

        def stacked(a, b, c, d):
            x = jnp.where(step < steps, a[...], c[...])
            y = jnp.where(step < steps, b[...], d[...])
            rows = []
            for n in range(HEADS_AT_ONCE):
                rows += [x[:, n * HEAD : (n + 1) * HEAD], y[:, n * HEAD : (n + 1) * HEAD]]
            return jnp.concatenate(rows, axis=0)

        q = stacked(q0, q1, q2, q3)
        g = stacked(g0, g1, g2, g3)

        def fold(x):
            return x.reshape(block // 8, 8, columns)

        def score_step(j, top):
            s = lax.dot_general(rows_of(k_ref, j), q, NT, preferred_element_type=jnp.float32)
            b = bias[span_of(j), :]
            s = s + jnp.concatenate([b] * HEADS_AT_ONCE, axis=1)
            s_scr[span_of(j), :] = s
            return jnp.maximum(top, jnp.max(fold(s), axis=0))

        top = lax.fori_loop(
            first, chip + 1, score_step, jnp.full((8, columns), NEG_FILL, jnp.float32)
        )
        top = jnp.max(top, axis=0, keepdims=True)

        def prob_step(j, carry):
            total, mix = carry
            span = span_of(j)
            p = jnp.exp2((s_scr[span, :] - top) * power)
            d = lax.dot_general(rows_of(v_ref, j), g, NT, preferred_element_type=jnp.float32)
            s_scr[span, :] = p
            d_scr[span, :] = d
            return (total + jnp.sum(fold(p), axis=0), mix + jnp.sum(fold(p * d), axis=0))

        zero = jnp.zeros((8, columns), jnp.float32)
        total, mix = lax.fori_loop(first, chip + 1, prob_step, (zero, zero))
        inverse = 1.0 / jnp.sum(total, axis=0, keepdims=True)
        mix = jnp.sum(mix, axis=0, keepdims=True) * inverse
        dq_acc[...] = jnp.zeros_like(dq_acc)

        def grad_step(j, _):
            span = span_of(j)
            p = s_scr[span, :] * inverse
            ds = (p * (d_scr[span, :] - mix)).astype(jnp.bfloat16)
            low = p.astype(jnp.bfloat16)
            dv_acc[span, :] += jnp.dot(low, g, preferred_element_type=jnp.float32)
            dk_acc[span, :] += jnp.dot(ds, q, preferred_element_type=jnp.float32)
            dq_acc[...] += jnp.dot(k_turned[j], ds, preferred_element_type=jnp.float32)
            return 0

        lax.fori_loop(first, chip + 1, grad_step, 0)
        dq = (dq_acc[...] * scale).T.astype(jnp.bfloat16)
        for n in range(HEADS_AT_ONCE):
            dq_ref[:, n * HEAD : (n + 1) * HEAD] = dq[n * block : (n + 1) * block]

        @pl.when(step == 2 * steps - 1)
        def _():
            dkv_ref[:, :HEAD] = (dk_acc[...] * scale).astype(jnp.bfloat16)
            dkv_ref[:, HEAD:] = dv_acc[...].astype(jnp.bfloat16)

    whole = pl.BlockSpec((length, 2 * HEAD), lambda s, at: (0, 0))
    queries_at = pl.BlockSpec((block, wide), lambda s, at: (s // steps, s % steps))
    flops = 5 * 2 * length * block * heads * HEAD
    return pl.pallas_call(
        kernel,
        grid_spec=pltpu.PrefetchScalarGridSpec(
            num_scalar_prefetch=1,
            grid=(2 * steps,),
            in_specs=[
                *[pl.BlockSpec((tokens, wide), lambda s, at: (0, s % steps))] * 4,
                *[pl.BlockSpec((tokens, wide), lambda s, at: (0, steps + s % steps))] * 4,
                pl.BlockSpec((devices, padded, HEAD), lambda s, at: (0, 0, 0)),
                pl.BlockSpec((devices, padded, HEAD), lambda s, at: (0, 0, 1)),
            ],
            out_specs=[queries_at, whole],
            scratch_shapes=[
                pltpu.VMEM((length, columns), jnp.float32),
                pltpu.VMEM((length, columns), jnp.float32),
                pltpu.VMEM((length, block), jnp.float32),
                pltpu.VMEM((chips, HEAD, block), jnp.bfloat16),
                pltpu.VMEM((HEAD, columns), jnp.float32),
                pltpu.VMEM((length, HEAD), jnp.float32),
                pltpu.VMEM((length, HEAD), jnp.float32),
            ],
        ),
        out_shape=[
            jax.ShapeDtypeStruct((2 * block, heads * HEAD), jnp.bfloat16),
            jax.ShapeDtypeStruct((length, 2 * HEAD), jnp.bfloat16),
        ],
        compiler_params=pltpu.CompilerParams(
            dimension_semantics=("arbitrary",), vmem_limit_bytes=58 * 1024 * 1024
        ),
        cost_estimate=pl.CostEstimate(
            flops=8 * flops, bytes_accessed=8 * 1024 * 1024, transcendentals=0
        ),
        name="attention",
    )(where, *parts, *parts, kv, kv)


VMEM = pl.BlockSpec(memory_space=pltpu.VMEM)
SMEM = pl.BlockSpec(memory_space=pltpu.SMEM)


def pack_keys(keys, values, starts, devices):
    tokens = keys.shape[0]

    def kernel(k_ref, v_ref, s_ref, out_ref):
        start = s_ref[...]
        high = jnp.right_shift(start, 6).astype(jnp.float32)
        low = jnp.bitwise_and(start, 63).astype(jnp.float32)
        row = jnp.concatenate([high, low], axis=1)
        first = lax.broadcasted_iota(jnp.int32, (16, 2 * tokens), 0) == 0
        extra = jnp.where(first, row, 0.0).astype(jnp.bfloat16)
        for n in range(devices):
            h = 2 * (n % 2) + (n >= devices // 2)
            out_ref[n, :tokens, :HEAD] = k_ref[:, h * HEAD : (h + 1) * HEAD]
            out_ref[n, :tokens, HEAD:] = v_ref[:, h * HEAD : (h + 1) * HEAD]
            out_ref[n, tokens:, :] = extra

    return pl.pallas_call(
        kernel,
        out_shape=jax.ShapeDtypeStruct((devices, tokens + 16, 2 * HEAD), jnp.bfloat16),
        in_specs=[VMEM] * 3,
        out_specs=VMEM,
        name="pack_keys",
    )(keys, values, starts)


def pack_queries(heads, queries, d_out, group):
    tokens = queries.shape[0]

    def kernel(h_ref, q_ref, g_ref, *outs):
        for n, out in enumerate(outs):
            span = pl.ds(pl.multiple_of(h_ref[n] * group, group), group)
            out[:, :group] = q_ref[:, span]
            out[:, group:] = g_ref[:, span]

    return pl.pallas_call(
        kernel,
        out_shape=[jax.ShapeDtypeStruct((tokens, 2 * group), jnp.bfloat16)] * 4,
        in_specs=[SMEM, VMEM, VMEM],
        out_specs=[VMEM] * 4,
        name="pack_queries",
    )(heads, queries, d_out)


def unpack_queries(heads, parts, group):
    tokens = parts[0].shape[0]

    def kernel(h_ref, *refs):
        for n in range(4):
            span = pl.ds(pl.multiple_of(h_ref[n] * group, group), group)
            refs[4][:, span] = refs[n][...]

    return pl.pallas_call(
        kernel,
        out_shape=jax.ShapeDtypeStruct((tokens, 4 * group), jnp.bfloat16),
        in_specs=[SMEM] + [VMEM] * 4,
        out_specs=VMEM,
        name="unpack_queries",
    )(heads, *parts)


def gradient(where, turned, mine, theirs, error):
    devices, rows, tokens = turned.shape
    width = mine.shape[2]

    def kernel(at, f_ref, m_ref, t_ref, e_ref, out_ref, low_ref):
        core = at[0]
        total = e_ref[...]
        for c in range(devices // 2):
            total = total + jnp.dot(
                f_ref[2 * c + core], m_ref[c], preferred_element_type=jnp.float32
            )
            total = total + jnp.dot(
                f_ref[2 * c + 1 - core], t_ref[c], preferred_element_type=jnp.float32
            )
        out_ref[...] = total
        low_ref[...] = total.astype(jnp.bfloat16)

    return pl.pallas_call(
        kernel,
        out_shape=[
            jax.ShapeDtypeStruct((rows, width), jnp.float32),
            jax.ShapeDtypeStruct((rows, width), jnp.bfloat16),
        ],
        in_specs=[SMEM] + [VMEM] * 4,
        out_specs=[VMEM] * 2,
        compiler_params=pltpu.CompilerParams(vmem_limit_bytes=32 * 1024 * 1024),
        name="gradient",
    )(where, turned, mine, theirs, error)


def finish(where, p_sum, mine, theirs, combined, replicas):
    rows, width = combined.shape
    size = p_sum.shape[1]
    half, part = width // 2, size // 2
    tiles = size // 8
    shape = (8, size)

    def kernel(at, p_ref, m_ref, t_ref, c_ref, comp_ref, q_ref, new_ref, gram_ref, inv_ref, all_ref):
        core = at[0]
        for x, who in ((m_ref, core), (t_ref, 1 - core)):
            all_ref[pl.ds(pl.multiple_of(who * half, half), half), :] = x[:half, :]
            gram_ref[pl.ds(pl.multiple_of(who * part, part), part), :] = (
                x[half : half + part, :]
                + x[half + part : half + 2 * part, :]
                + x[half + 2 * part :, :]
            )
        lane = lax.broadcasted_iota(jnp.int32, shape, 1)
        sub = lax.broadcasted_iota(jnp.int32, shape, 0)
        left = [gram_ref[8 * t : 8 * t + 8, :] for t in range(tiles)]
        right = [jnp.where(lane == sub + 8 * t, 1.0, 0.0) for t in range(tiles)]
        def row(x, r):
            return jnp.broadcast_to(x[r : r + 1, :], shape)

        for p in range(tiles):
            spread = [
                [
                    jnp.broadcast_to(left[t][:, 8 * p + k : 8 * p + k + 1], shape)
                    for k in range(8)
                ]
                for t in range(p, tiles)
            ]
            for k in range(8):
                pivot = spread[0][k]
                root = lax.rsqrt(row(pivot, k))
                row_l = row(left[p], k) * root
                row_r = row(right[p], k) * root
                inv_ref[8 * p + k : 8 * p + k + 1, :] = row_r[0:1]
                factors = [row(pivot, m) * root for m in range(k + 1, 8)]
                for t in range(p, tiles):
                    x = spread[t - p][k] * root
                    for m in range(k + 1, 8):
                        spread[t - p][m] = spread[t - p][m] - x * factors[m - k - 1]
                    left[t] = left[t] - x * row_l
                    right[t] = right[t] - x * row_r

        def product(x, y):
            return lax.dot_general(
                x, y, NT, precision=HIGHEST, preferred_element_type=jnp.float32
            )

        inv = inv_ref[...]
        q = product(all_ref[...], inv) * (1.0 / replicas)
        q_ref[...] = q
        out = product(product(p_ref[...], inv), q)
        comp_ref[...] = out
        new_ref[0] = c_ref[...] - out

    return pl.pallas_call(
        kernel,
        out_shape=[
            jax.ShapeDtypeStruct((rows, width), jnp.float32),
            jax.ShapeDtypeStruct((width, size), jnp.float32),
            jax.ShapeDtypeStruct((1, rows, width), jnp.float32),
        ],
        in_specs=[SMEM] + [VMEM] * 4,
        out_specs=[VMEM] * 3,
        scratch_shapes=[
            pltpu.VMEM((size, size), jnp.float32),
            pltpu.VMEM((size, size), jnp.float32),
            pltpu.VMEM((width, size), jnp.float32),
        ],
        compiler_params=pltpu.CompilerParams(vmem_limit_bytes=32 * 1024 * 1024),
        name="finish",
    )(where, p_sum, mine, theirs, combined)


def body(queries, keys, values, d_out, features, doc_start, error, q_init):
    tokens = queries.shape[0]
    width_kv = keys.shape[1]
    group = queries.shape[1] // (width_kv // HEAD)
    chips = lax.axis_size("chip")
    devices = 2 * chips
    replicas = lax.axis_size("dp")
    core = lax.axis_index("core")
    chip = lax.axis_index("chip")
    upper = (chip >= chips // 2).astype(jnp.int32)
    f32, bf16 = jnp.float32, jnp.bfloat16
    ctx = ("chip", "core")

    def swap(x):
        return lax.ppermute(x, "core", [(0, 1), (1, 0)])

    def piece(x, size, index, axis=1):
        return lax.dynamic_slice_in_dim(x, index * size, size, axis)

    def move(x, cross, turn):
        pairs = []
        for c in range(chips):
            for h in range(2):
                to = (chips - 1 - c if cross else c) * 2 + (1 - h if turn else h)
                pairs.append((2 * c + h, to))
        return lax.ppermute(x, ctx, pairs)

    def exchange(x, axis):
        return lax.all_to_all(x, axis, 0, 0)

    def spread(x, axis, size):
        return exchange(jnp.broadcast_to(x[None], (size,) + x.shape), axis)

    def head_of(cross, turn):
        return 2 * (1 - core if turn else core) + (1 - upper if cross else upper)

    ways = [(False, False), (False, True), (True, False), (True, True)]
    heads = jnp.stack([head_of(*way) for way in ways]).astype(jnp.int32)
    kv = exchange(pack_keys(keys, values, doc_start[None, :], devices), ctx)
    parts = pack_queries(heads, queries, d_out, group)
    parts = [parts[0]] + [move(x, *way) for x, way in zip(parts[1:], ways[1:])]

    rows = features.shape[1] // devices
    feat = jnp.transpose(features).reshape(devices, rows, tokens)
    kv, feat = lax.optimization_barrier((kv, feat))
    feat = exchange(feat, ctx)

    where = jnp.stack([core, chip, chips - 1 - chip]).astype(jnp.int32)
    dq, dkv = attention(where, parts, kv)
    dkv, feat = lax.optimization_barrier((dkv, feat))

    home = exchange(dkv.reshape(devices, tokens, 2 * HEAD), ctx)
    home = home.reshape(2, chips // 2, 2, tokens, 2 * HEAD).astype(f32)
    home = jnp.sum(home, axis=1).astype(bf16)
    home = [home[0, 0], home[1, 0], home[0, 1], home[1, 1]]
    d_key = jnp.concatenate([x[:, :HEAD] for x in home], axis=1)
    d_value = jnp.concatenate([x[:, HEAD:] for x in home], axis=1)
    dk_mine = spread(d_key, "chip", chips)
    dk_theirs = swap(dk_mine)
    combined, low = gradient(where, feat, dk_mine, dk_theirs, error.reshape(rows, width_kv))

    shares = exchange(low.reshape(replicas, rows // replicas, width_kv), "dp")
    share = jnp.sum(shares.astype(f32), axis=0).astype(bf16)
    total = spread(share, "dp", replicas).reshape(rows, width_kv)

    back = [dq[:tokens]] + [
        move(dq[n * tokens : (n + 1) * tokens], *ways[n]) for n in range(1, 4)
    ]
    d_query = unpack_queries(heads, back, group)

    total = total.astype(f32)
    p_sum = jnp.dot(total, q_init, precision=HIGHEST)
    gram = lax.dot_general(p_sum, p_sum, TN, precision=HIGHEST)
    moment = lax.dot_general(total, p_sum, TN, precision=HIGHEST)
    half, part = width_kv // 2, q_init.shape[1] // 2

    def share_of(who):
        return jnp.concatenate([piece(moment, half, who, 0), piece(gram, part, who, 0)], axis=0)

    sums = share_of(core) + swap(share_of(1 - core))
    gram = sums[half:]
    high = lax.reduce_precision(gram, 8, 7)
    mid = lax.reduce_precision(gram - high, 8, 7)
    low = gram - high - mid
    sums = jnp.concatenate([sums[:half], high, mid, low], axis=0).astype(bf16)
    sums = jnp.sum(spread(sums, "chip", chips).astype(f32), axis=0)
    compressed, q_factor, new_error = finish(where, p_sum, sums, swap(sums), combined, replicas)
    return (d_query, d_key, d_value, compressed, q_factor, new_error)


def solution(mesh):
    replicas, ctx = mesh.devices.shape
    parts = Mesh(mesh.devices.reshape(replicas, ctx // 2, 2), ("dp", "chip", "core"))
    everywhere = ("dp", "chip", "core")
    tokens = P(everywhere, None)
    in_specs = (
        tokens, tokens, tokens, tokens, tokens, P(everywhere), P("dp", ("chip", "core"), None), P(),
    )
    out_specs = (
        tokens, tokens, tokens, P(("chip", "core"), None), P(), P("dp", ("chip", "core"), None),
    )
    return jax.shard_map(body, mesh=parts, in_specs=in_specs, out_specs=out_specs, check_vma=False)
```

```python
import math

import jax
import jax.numpy as jnp
from jax import lax
from jax.experimental import pallas as pl
from jax.experimental.pallas import tpu as pltpu
from jax.sharding import Mesh
from jax.sharding import PartitionSpec as P

HEAD = 128
NEG_FILL = -1e30
LOG2E = 1.4426950408889634
HIGHEST = lax.Precision.HIGHEST
TN = (((0,), (0,)), ((), ()))
NT = (((1,), (1,)), ((), ()))
HEADS_AT_ONCE = 6


def attention(where, parts, kv):
    devices, padded, _ = kv.shape
    tokens = HEAD
    block = 2 * tokens
    chips = devices // 2
    length = devices * tokens
    heads = parts[0].shape[1] // (2 * HEAD)
    steps = heads // HEADS_AT_ONCE
    wide = HEADS_AT_ONCE * HEAD
    columns = HEADS_AT_ONCE * block
    scale = 1.0 / math.sqrt(HEAD)
    power = scale * LOG2E

    def kernel(
        at, q0, q1, q2, q3, g0, g1, g2, g3, k_ref, v_ref, dq_ref, dkv_ref,
        s_scr, d_scr, bias, k_turned, dq_acc, dk_acc, dv_acc,
    ):
        step = pl.program_id(0)
        core = at[0]
        chip = at[1 + step // steps]

        def place(index):
            return jnp.where(index < tokens, index + core * tokens, index - core * tokens)

        def starts(device):
            high = k_ref[device, tokens : tokens + 1, :].astype(jnp.float32)
            low = v_ref[device, tokens : tokens + 1, :].astype(jnp.float32)
            return high * 64.0 + low

        start = jnp.concatenate(
            [starts(2 * chip + core), starts(2 * chip + 1 - core)], axis=1
        )
        first = jnp.min(start).astype(jnp.int32) // block

        def span_of(j):
            return pl.ds(pl.multiple_of(j * block, block), block)

        def rows_of(ref, j):
            return ref[pl.ds(2 * j, 2), :tokens, :].reshape(block, HEAD)

        @pl.when(lax.rem(step, steps) == 0)
        def _():
            q_pos = chip * block + place(lax.broadcasted_iota(jnp.int32, (block, block), 1))
            k_off = lax.broadcasted_iota(jnp.int32, (block, block), 0)
            begin = start.astype(jnp.int32)

            def fill(j, _):
                k_pos = j * block + k_off
                ok = (k_pos <= q_pos) & (k_pos >= begin)
                bias[span_of(j), :] = jnp.where(ok, 0.0, NEG_FILL)
                return 0

            lax.fori_loop(first, chip + 1, fill, 0)

        @pl.when(step == 0)
        def _():
            dk_acc[...] = jnp.zeros_like(dk_acc)
            dv_acc[...] = jnp.zeros_like(dv_acc)
            for j in range(chips):
                k_turned[j] = (
                    k_ref[2 * j : 2 * j + 2, :tokens, :].reshape(block, HEAD).astype(jnp.float32).T
                ).astype(jnp.bfloat16)

        def stacked(a, b, c, d):
            x = jnp.where(step < steps, a[...], c[...])
            y = jnp.where(step < steps, b[...], d[...])
            rows = []
            for n in range(HEADS_AT_ONCE):
                rows += [x[:, n * HEAD : (n + 1) * HEAD], y[:, n * HEAD : (n + 1) * HEAD]]
            return jnp.concatenate(rows, axis=0)

        q = stacked(q0, q1, q2, q3)
        g = stacked(g0, g1, g2, g3)

        def fold(x):
            return x.reshape(block // 8, 8, columns)

        def score_step(j, top):
            s = lax.dot_general(rows_of(k_ref, j), q, NT, preferred_element_type=jnp.float32)
            b = bias[span_of(j), :]
            s = s + jnp.concatenate([b] * HEADS_AT_ONCE, axis=1)
            s_scr[span_of(j), :] = s
            return jnp.maximum(top, jnp.max(fold(s), axis=0))

        top = lax.fori_loop(
            first, chip + 1, score_step, jnp.full((8, columns), NEG_FILL, jnp.float32)
        )
        top = jnp.max(top, axis=0, keepdims=True)

        def prob_step(j, carry):
            total, mix = carry
            span = span_of(j)
            p = jnp.exp2((s_scr[span, :] - top) * power)
            d = lax.dot_general(rows_of(v_ref, j), g, NT, preferred_element_type=jnp.float32)
            s_scr[span, :] = p
            d_scr[span, :] = d
            return (total + jnp.sum(fold(p), axis=0), mix + jnp.sum(fold(p * d), axis=0))

        zero = jnp.zeros((8, columns), jnp.float32)
        total, mix = lax.fori_loop(first, chip + 1, prob_step, (zero, zero))
        inverse = 1.0 / jnp.sum(total, axis=0, keepdims=True)
        mix = jnp.sum(mix, axis=0, keepdims=True) * inverse
        dq_acc[...] = jnp.zeros_like(dq_acc)

        def grad_step(j, _):
            span = span_of(j)
            p = s_scr[span, :] * inverse
            ds = (p * (d_scr[span, :] - mix)).astype(jnp.bfloat16)
            low = p.astype(jnp.bfloat16)
            dv_acc[span, :] += jnp.dot(low, g, preferred_element_type=jnp.float32)
            dk_acc[span, :] += jnp.dot(ds, q, preferred_element_type=jnp.float32)
            dq_acc[...] += jnp.dot(k_turned[j], ds, preferred_element_type=jnp.float32)
            return 0

        lax.fori_loop(first, chip + 1, grad_step, 0)
        dq = (dq_acc[...] * scale).T.astype(jnp.bfloat16)
        for n in range(HEADS_AT_ONCE):
            dq_ref[:, n * HEAD : (n + 1) * HEAD] = dq[n * block : (n + 1) * block]

        @pl.when(step == 2 * steps - 1)
        def _():
            dkv_ref[:, :HEAD] = (dk_acc[...] * scale).astype(jnp.bfloat16)
            dkv_ref[:, HEAD:] = dv_acc[...].astype(jnp.bfloat16)

    whole = pl.BlockSpec((length, 2 * HEAD), lambda s, at: (0, 0))
    queries_at = pl.BlockSpec((block, wide), lambda s, at: (s // steps, s % steps))
    flops = 5 * 2 * length * block * heads * HEAD
    return pl.pallas_call(
        kernel,
        grid_spec=pltpu.PrefetchScalarGridSpec(
            num_scalar_prefetch=1,
            grid=(2 * steps,),
            in_specs=[
                *[pl.BlockSpec((tokens, wide), lambda s, at: (0, s % steps))] * 4,
                *[pl.BlockSpec((tokens, wide), lambda s, at: (0, steps + s % steps))] * 4,
                pl.BlockSpec((devices, padded, HEAD), lambda s, at: (0, 0, 0)),
                pl.BlockSpec((devices, padded, HEAD), lambda s, at: (0, 0, 1)),
            ],
            out_specs=[queries_at, whole],
            scratch_shapes=[
                pltpu.VMEM((length, columns), jnp.float32),
                pltpu.VMEM((length, columns), jnp.float32),
                pltpu.VMEM((length, block), jnp.float32),
                pltpu.VMEM((chips, HEAD, block), jnp.bfloat16),
                pltpu.VMEM((HEAD, columns), jnp.float32),
                pltpu.VMEM((length, HEAD), jnp.float32),
                pltpu.VMEM((length, HEAD), jnp.float32),
            ],
        ),
        out_shape=[
            jax.ShapeDtypeStruct((2 * block, heads * HEAD), jnp.bfloat16),
            jax.ShapeDtypeStruct((length, 2 * HEAD), jnp.bfloat16),
        ],
        compiler_params=pltpu.CompilerParams(
            dimension_semantics=("arbitrary",), vmem_limit_bytes=40 * 1024 * 1024
        ),
        cost_estimate=pl.CostEstimate(
            flops=8 * flops, bytes_accessed=8 * 1024 * 1024, transcendentals=0
        ),
        name="attention",
    )(where, *parts, *parts, kv, kv)


VMEM = pl.BlockSpec(memory_space=pltpu.VMEM)
SMEM = pl.BlockSpec(memory_space=pltpu.SMEM)


def pack_keys(keys, values, starts, devices):
    tokens = keys.shape[0]

    def kernel(k_ref, v_ref, s_ref, out_ref):
        start = s_ref[...]
        high = jnp.right_shift(start, 6).astype(jnp.float32)
        low = jnp.bitwise_and(start, 63).astype(jnp.float32)
        row = jnp.concatenate([high, low], axis=1)
        first = lax.broadcasted_iota(jnp.int32, (16, 2 * tokens), 0) == 0
        extra = jnp.where(first, row, 0.0).astype(jnp.bfloat16)
        for n in range(devices):
            h = 2 * (n % 2) + (n >= devices // 2)
            out_ref[n, :tokens, :HEAD] = k_ref[:, h * HEAD : (h + 1) * HEAD]
            out_ref[n, :tokens, HEAD:] = v_ref[:, h * HEAD : (h + 1) * HEAD]
            out_ref[n, tokens:, :] = extra

    return pl.pallas_call(
        kernel,
        out_shape=jax.ShapeDtypeStruct((devices, tokens + 16, 2 * HEAD), jnp.bfloat16),
        in_specs=[VMEM] * 3,
        out_specs=VMEM,
        name="pack_keys",
    )(keys, values, starts)


def pack_queries(heads, queries, d_out, group):
    tokens = queries.shape[0]

    def kernel(h_ref, q_ref, g_ref, *outs):
        for n, out in enumerate(outs):
            span = pl.ds(pl.multiple_of(h_ref[n] * group, group), group)
            out[:, :group] = q_ref[:, span]
            out[:, group:] = g_ref[:, span]

    return pl.pallas_call(
        kernel,
        out_shape=[jax.ShapeDtypeStruct((tokens, 2 * group), jnp.bfloat16)] * 4,
        in_specs=[SMEM, VMEM, VMEM],
        out_specs=[VMEM] * 4,
        name="pack_queries",
    )(heads, queries, d_out)


def unpack_queries(heads, parts, group):
    tokens = parts[0].shape[0]

    def kernel(h_ref, *refs):
        for n in range(4):
            span = pl.ds(pl.multiple_of(h_ref[n] * group, group), group)
            refs[4][:, span] = refs[n][...]

    return pl.pallas_call(
        kernel,
        out_shape=jax.ShapeDtypeStruct((tokens, 4 * group), jnp.bfloat16),
        in_specs=[SMEM] + [VMEM] * 4,
        out_specs=VMEM,
        name="unpack_queries",
    )(heads, *parts)


def gradient(where, turned, mine, theirs, error):
    devices, rows, tokens = turned.shape
    width = mine.shape[2]

    def kernel(at, f_ref, m_ref, t_ref, e_ref, out_ref, low_ref):
        core = at[0]
        total = e_ref[...]
        for c in range(devices // 2):
            total = total + jnp.dot(
                f_ref[2 * c + core], m_ref[c], preferred_element_type=jnp.float32
            )
            total = total + jnp.dot(
                f_ref[2 * c + 1 - core], t_ref[c], preferred_element_type=jnp.float32
            )
        out_ref[...] = total
        low_ref[...] = total.astype(jnp.bfloat16)

    return pl.pallas_call(
        kernel,
        out_shape=[
            jax.ShapeDtypeStruct((rows, width), jnp.float32),
            jax.ShapeDtypeStruct((rows, width), jnp.bfloat16),
        ],
        in_specs=[SMEM] + [VMEM] * 4,
        out_specs=[VMEM] * 2,
        compiler_params=pltpu.CompilerParams(vmem_limit_bytes=32 * 1024 * 1024),
        name="gradient",
    )(where, turned, mine, theirs, error)


def finish(where, p_sum, mine, theirs, combined, replicas):
    rows, width = combined.shape
    size = p_sum.shape[1]
    half, part = width // 2, size // 2
    tiles = size // 8
    shape = (8, size)

    def kernel(at, p_ref, m_ref, t_ref, c_ref, comp_ref, q_ref, new_ref, gram_ref, inv_ref, all_ref):
        core = at[0]
        for x, who in ((m_ref, core), (t_ref, 1 - core)):
            all_ref[pl.ds(pl.multiple_of(who * half, half), half), :] = x[:half, :]
            gram_ref[pl.ds(pl.multiple_of(who * part, part), part), :] = (
                x[half : half + part, :]
                + x[half + part : half + 2 * part, :]
                + x[half + 2 * part :, :]
            )
        lane = lax.broadcasted_iota(jnp.int32, shape, 1)
        sub = lax.broadcasted_iota(jnp.int32, shape, 0)
        left = [gram_ref[8 * t : 8 * t + 8, :] for t in range(tiles)]
        right = [jnp.where(lane == sub + 8 * t, 1.0, 0.0) for t in range(tiles)]
        def row(x, r):
            return jnp.broadcast_to(x[r : r + 1, :], shape)

        for p in range(tiles):
            spread = [
                [
                    jnp.broadcast_to(left[t][:, 8 * p + k : 8 * p + k + 1], shape)
                    for k in range(8)
                ]
                for t in range(p, tiles)
            ]
            for k in range(8):
                pivot = spread[0][k]
                root = lax.rsqrt(row(pivot, k))
                row_l = row(left[p], k) * root
                row_r = row(right[p], k) * root
                inv_ref[8 * p + k : 8 * p + k + 1, :] = row_r[0:1]
                factors = [row(pivot, m) * root for m in range(k + 1, 8)]
                for t in range(p, tiles):
                    x = spread[t - p][k] * root
                    for m in range(k + 1, 8):
                        spread[t - p][m] = spread[t - p][m] - x * factors[m - k - 1]
                    left[t] = left[t] - x * row_l
                    right[t] = right[t] - x * row_r

        def product(x, y):
            return lax.dot_general(
                x, y, NT, precision=HIGHEST, preferred_element_type=jnp.float32
            )

        inv = inv_ref[...]
        q = product(all_ref[...], inv) * (1.0 / replicas)
        q_ref[...] = q
        out = product(product(p_ref[...], inv), q)
        comp_ref[...] = out
        new_ref[0] = c_ref[...] - out

    return pl.pallas_call(
        kernel,
        out_shape=[
            jax.ShapeDtypeStruct((rows, width), jnp.float32),
            jax.ShapeDtypeStruct((width, size), jnp.float32),
            jax.ShapeDtypeStruct((1, rows, width), jnp.float32),
        ],
        in_specs=[SMEM] + [VMEM] * 4,
        out_specs=[VMEM] * 3,
        scratch_shapes=[
            pltpu.VMEM((size, size), jnp.float32),
            pltpu.VMEM((size, size), jnp.float32),
            pltpu.VMEM((width, size), jnp.float32),
        ],
        compiler_params=pltpu.CompilerParams(vmem_limit_bytes=32 * 1024 * 1024),
        name="finish",
    )(where, p_sum, mine, theirs, combined)


def body(queries, keys, values, d_out, features, doc_start, error, q_init):
    tokens = queries.shape[0]
    width_kv = keys.shape[1]
    group = queries.shape[1] // (width_kv // HEAD)
    chips = lax.axis_size("chip")
    devices = 2 * chips
    replicas = lax.axis_size("dp")
    core = lax.axis_index("core")
    chip = lax.axis_index("chip")
    upper = (chip >= chips // 2).astype(jnp.int32)
    f32, bf16 = jnp.float32, jnp.bfloat16
    ctx = ("chip", "core")

    def swap(x):
        return lax.ppermute(x, "core", [(0, 1), (1, 0)])

    def piece(x, size, index, axis=1):
        return lax.dynamic_slice_in_dim(x, index * size, size, axis)

    def move(x, cross, turn):
        pairs = []
        for c in range(chips):
            for h in range(2):
                to = (chips - 1 - c if cross else c) * 2 + (1 - h if turn else h)
                pairs.append((2 * c + h, to))
        return lax.ppermute(x, ctx, pairs)

    def exchange(x, axis):
        return lax.all_to_all(x, axis, 0, 0)

    def spread(x, axis, size):
        return exchange(jnp.broadcast_to(x[None], (size,) + x.shape), axis)

    def head_of(cross, turn):
        return 2 * (1 - core if turn else core) + (1 - upper if cross else upper)

    ways = [(False, False), (False, True), (True, False), (True, True)]
    heads = jnp.stack([head_of(*way) for way in ways]).astype(jnp.int32)
    kv = exchange(pack_keys(keys, values, doc_start[None, :], devices), ctx)
    parts = pack_queries(heads, queries, d_out, group)
    parts = [parts[0]] + [move(x, *way) for x, way in zip(parts[1:], ways[1:])]

    rows = features.shape[1] // devices
    feat = jnp.transpose(features).reshape(devices, rows, tokens)
    kv, feat = lax.optimization_barrier((kv, feat))
    feat = exchange(feat, ctx)

    where = jnp.stack([core, chip, chips - 1 - chip]).astype(jnp.int32)
    dq, dkv = attention(where, parts, kv)
    dkv, feat = lax.optimization_barrier((dkv, feat))

    home = exchange(dkv.reshape(devices, tokens, 2 * HEAD), ctx)
    home = home.reshape(2, chips // 2, 2, tokens, 2 * HEAD).astype(f32)
    home = jnp.sum(home, axis=1).astype(bf16)
    home = [home[0, 0], home[1, 0], home[0, 1], home[1, 1]]
    d_key = jnp.concatenate([x[:, :HEAD] for x in home], axis=1)
    d_value = jnp.concatenate([x[:, HEAD:] for x in home], axis=1)
    dk_mine = spread(d_key, "chip", chips)
    dk_theirs = swap(dk_mine)
    combined, low = gradient(where, feat, dk_mine, dk_theirs, error.reshape(rows, width_kv))

    shares = exchange(low.reshape(replicas, rows // replicas, width_kv), "dp")
    share = jnp.sum(shares.astype(f32), axis=0).astype(bf16)
    total = spread(share, "dp", replicas).reshape(rows, width_kv)

    total = total.astype(f32)
    p_sum = jnp.dot(total, q_init, precision=HIGHEST)
    gram = lax.dot_general(p_sum, p_sum, TN, precision=HIGHEST)
    moment = lax.dot_general(total, p_sum, TN, precision=HIGHEST)
    half, part = width_kv // 2, q_init.shape[1] // 2

    def share_of(who):
        return jnp.concatenate([piece(moment, half, who, 0), piece(gram, part, who, 0)], axis=0)

    sums = share_of(core) + swap(share_of(1 - core))
    gram = sums[half:]
    high = lax.reduce_precision(gram, 8, 7)
    mid = lax.reduce_precision(gram - high, 8, 7)
    low = gram - high - mid
    sums = jnp.concatenate([sums[:half], high, mid, low], axis=0).astype(bf16)
    sums = jnp.sum(spread(sums, "chip", chips).astype(f32), axis=0)
    compressed, q_factor, new_error = finish(where, p_sum, sums, swap(sums), combined, replicas)

    back = [dq[:tokens]] + [
        move(dq[n * tokens : (n + 1) * tokens], *ways[n]) for n in range(1, 4)
    ]
    compressed, *back = lax.optimization_barrier((compressed, *back))
    d_query = unpack_queries(heads, back, group)
    return (d_query, d_key, d_value, compressed, q_factor, new_error)


def solution(mesh):
    replicas, ctx = mesh.devices.shape
    parts = Mesh(mesh.devices.reshape(replicas, ctx // 2, 2), ("dp", "chip", "core"))
    everywhere = ("dp", "chip", "core")
    tokens = P(everywhere, None)
    in_specs = (
        tokens, tokens, tokens, tokens, tokens, P(everywhere), P("dp", ("chip", "core"), None), P(),
    )
    out_specs = (
        tokens, tokens, tokens, P(("chip", "core"), None), P(), P("dp", ("chip", "core"), None),
    )
    return jax.shard_map(body, mesh=parts, in_specs=in_specs, out_specs=out_specs, check_vma=False)
```

```python
import math

import jax
import jax.numpy as jnp
from jax import lax
from jax.experimental import pallas as pl
from jax.experimental.pallas import tpu as pltpu
from jax.sharding import Mesh
from jax.sharding import PartitionSpec as P

HEAD = 128
NEG_FILL = -1e30
LOG2E = 1.4426950408889634
HIGHEST = lax.Precision.HIGHEST
TN = (((0,), (0,)), ((), ()))
NT = (((1,), (1,)), ((), ()))
HEADS_AT_ONCE = 6


def attention(where, parts, kv):
    devices, padded, _ = kv.shape
    tokens = HEAD
    block = 2 * tokens
    chips = devices // 2
    length = devices * tokens
    heads = parts[0].shape[1] // (2 * HEAD)
    steps = heads // HEADS_AT_ONCE
    wide = HEADS_AT_ONCE * HEAD
    columns = HEADS_AT_ONCE * block
    scale = 1.0 / math.sqrt(HEAD)
    power = scale * LOG2E

    def kernel(
        at, q0, q1, q2, q3, g0, g1, g2, g3, k_ref, v_ref, dq_ref, dkv_ref,
        s_scr, d_scr, bias, k_turned, dq_acc, dk_acc, dv_acc,
    ):
        step = pl.program_id(0)
        core = at[0]
        chip = at[1 + step // steps]

        def place(index):
            return jnp.where(index < tokens, index + core * tokens, index - core * tokens)

        def starts(device):
            high = k_ref[device, tokens : tokens + 1, :].astype(jnp.float32)
            low = v_ref[device, tokens : tokens + 1, :].astype(jnp.float32)
            return high * 64.0 + low

        start = jnp.concatenate(
            [starts(2 * chip + core), starts(2 * chip + 1 - core)], axis=1
        )
        first = jnp.min(start).astype(jnp.int32) // block

        def span_of(j):
            return pl.ds(pl.multiple_of(j * block, block), block)

        def rows_of(ref, j):
            return ref[pl.ds(2 * j, 2), :tokens, :].reshape(block, HEAD)

        @pl.when(lax.rem(step, steps) == 0)
        def _():
            q_pos = chip * block + place(lax.broadcasted_iota(jnp.int32, (block, block), 1))
            k_off = lax.broadcasted_iota(jnp.int32, (block, block), 0)
            begin = start.astype(jnp.int32)

            def fill(j, _):
                k_pos = j * block + k_off
                ok = (k_pos <= q_pos) & (k_pos >= begin)
                bias[span_of(j), :] = jnp.where(ok, 0.0, NEG_FILL)
                return 0

            lax.fori_loop(first, chip + 1, fill, 0)

        @pl.when(step == 0)
        def _():
            dk_acc[...] = jnp.zeros_like(dk_acc)
            dv_acc[...] = jnp.zeros_like(dv_acc)
            for j in range(chips):
                k_turned[j] = (
                    k_ref[2 * j : 2 * j + 2, :tokens, :].reshape(block, HEAD).astype(jnp.float32).T
                ).astype(jnp.bfloat16)

        def stacked(a, b, c, d):
            x = jnp.where(step < steps, a[...], c[...])
            y = jnp.where(step < steps, b[...], d[...])
            rows = []
            for n in range(HEADS_AT_ONCE):
                rows += [x[:, n * HEAD : (n + 1) * HEAD], y[:, n * HEAD : (n + 1) * HEAD]]
            return jnp.concatenate(rows, axis=0)

        q = stacked(q0, q1, q2, q3)
        g = stacked(g0, g1, g2, g3)

        def fold(x):
            return x.reshape(block // 8, 8, columns)

        def score_step(j, top):
            s = lax.dot_general(rows_of(k_ref, j), q, NT, preferred_element_type=jnp.float32)
            b = bias[span_of(j), :]
            s = s + jnp.concatenate([b] * HEADS_AT_ONCE, axis=1)
            s_scr[span_of(j), :] = s
            return jnp.maximum(top, jnp.max(fold(s), axis=0))

        top = lax.fori_loop(
            first, chip + 1, score_step, jnp.full((8, columns), NEG_FILL, jnp.float32)
        )
        top = jnp.max(top, axis=0, keepdims=True)

        def prob_step(j, carry):
            total, mix = carry
            span = span_of(j)
            p = jnp.exp2((s_scr[span, :] - top) * power)
            d = lax.dot_general(rows_of(v_ref, j), g, NT, preferred_element_type=jnp.float32)
            s_scr[span, :] = p
            d_scr[span, :] = d
            return (total + jnp.sum(fold(p), axis=0), mix + jnp.sum(fold(p * d), axis=0))

        zero = jnp.zeros((8, columns), jnp.float32)
        total, mix = lax.fori_loop(first, chip + 1, prob_step, (zero, zero))
        inverse = 1.0 / jnp.sum(total, axis=0, keepdims=True)
        mix = jnp.sum(mix, axis=0, keepdims=True) * inverse
        dq_acc[...] = jnp.zeros_like(dq_acc)

        def grad_step(j, _):
            span = span_of(j)
            p = s_scr[span, :] * inverse
            ds = (p * (d_scr[span, :] - mix)).astype(jnp.bfloat16)
            low = p.astype(jnp.bfloat16)
            dv_acc[span, :] += jnp.dot(low, g, preferred_element_type=jnp.float32)
            dk_acc[span, :] += jnp.dot(ds, q, preferred_element_type=jnp.float32)
            dq_acc[...] += jnp.dot(k_turned[j], ds, preferred_element_type=jnp.float32)
            return 0

        lax.fori_loop(first, chip + 1, grad_step, 0)
        dq = (dq_acc[...] * scale).T.astype(jnp.bfloat16)
        for n in range(HEADS_AT_ONCE):
            dq_ref[:, n * HEAD : (n + 1) * HEAD] = dq[n * block : (n + 1) * block]

        @pl.when(step == 2 * steps - 1)
        def _():
            dkv_ref[:, :HEAD] = (dk_acc[...] * scale).astype(jnp.bfloat16)
            dkv_ref[:, HEAD:] = dv_acc[...].astype(jnp.bfloat16)

    whole = pl.BlockSpec((length, 2 * HEAD), lambda s, at: (0, 0))
    queries_at = pl.BlockSpec((block, wide), lambda s, at: (s // steps, s % steps))
    flops = 5 * 2 * length * block * heads * HEAD
    return pl.pallas_call(
        kernel,
        grid_spec=pltpu.PrefetchScalarGridSpec(
            num_scalar_prefetch=1,
            grid=(2 * steps,),
            in_specs=[
                *[pl.BlockSpec((tokens, wide), lambda s, at: (0, s % steps))] * 4,
                *[pl.BlockSpec((tokens, wide), lambda s, at: (0, steps + s % steps))] * 4,
                pl.BlockSpec((devices, padded, HEAD), lambda s, at: (0, 0, 0)),
                pl.BlockSpec((devices, padded, HEAD), lambda s, at: (0, 0, 1)),
            ],
            out_specs=[queries_at, whole],
            scratch_shapes=[
                pltpu.VMEM((length, columns), jnp.float32),
                pltpu.VMEM((length, columns), jnp.float32),
                pltpu.VMEM((length, block), jnp.float32),
                pltpu.VMEM((chips, HEAD, block), jnp.bfloat16),
                pltpu.VMEM((HEAD, columns), jnp.float32),
                pltpu.VMEM((length, HEAD), jnp.float32),
                pltpu.VMEM((length, HEAD), jnp.float32),
            ],
        ),
        out_shape=[
            jax.ShapeDtypeStruct((2 * block, heads * HEAD), jnp.bfloat16),
            jax.ShapeDtypeStruct((length, 2 * HEAD), jnp.bfloat16),
        ],
        compiler_params=pltpu.CompilerParams(
            dimension_semantics=("arbitrary",), vmem_limit_bytes=40 * 1024 * 1024
        ),
        cost_estimate=pl.CostEstimate(
            flops=8 * flops, bytes_accessed=8 * 1024 * 1024, transcendentals=0
        ),
        name="attention",
    )(where, *parts, *parts, kv, kv)


VMEM = pl.BlockSpec(memory_space=pltpu.VMEM)
SMEM = pl.BlockSpec(memory_space=pltpu.SMEM)


def pack_keys(keys, values, starts, devices):
    tokens = keys.shape[0]

    def kernel(k_ref, v_ref, s_ref, out_ref):
        start = s_ref[...]
        high = jnp.right_shift(start, 6).astype(jnp.float32)
        low = jnp.bitwise_and(start, 63).astype(jnp.float32)
        row = jnp.concatenate([high, low], axis=1)
        first = lax.broadcasted_iota(jnp.int32, (16, 2 * tokens), 0) == 0
        extra = jnp.where(first, row, 0.0).astype(jnp.bfloat16)
        for n in range(devices):
            h = 2 * (n % 2) + (n >= devices // 2)
            out_ref[n, :tokens, :HEAD] = k_ref[:, h * HEAD : (h + 1) * HEAD]
            out_ref[n, :tokens, HEAD:] = v_ref[:, h * HEAD : (h + 1) * HEAD]
            out_ref[n, tokens:, :] = extra

    return pl.pallas_call(
        kernel,
        out_shape=jax.ShapeDtypeStruct((devices, tokens + 16, 2 * HEAD), jnp.bfloat16),
        in_specs=[VMEM] * 3,
        out_specs=VMEM,
        name="pack_keys",
    )(keys, values, starts)


def pack_queries(heads, queries, d_out, group):
    tokens = queries.shape[0]

    def kernel(h_ref, q_ref, g_ref, *outs):
        for n, out in enumerate(outs):
            span = pl.ds(pl.multiple_of(h_ref[n] * group, group), group)
            out[:, :group] = q_ref[:, span]
            out[:, group:] = g_ref[:, span]

    return pl.pallas_call(
        kernel,
        out_shape=[jax.ShapeDtypeStruct((tokens, 2 * group), jnp.bfloat16)] * 4,
        in_specs=[SMEM, VMEM, VMEM],
        out_specs=[VMEM] * 4,
        name="pack_queries",
    )(heads, queries, d_out)


def unpack_queries(heads, parts, group):
    tokens = parts[0].shape[0]

    def kernel(h_ref, *refs):
        for n in range(4):
            span = pl.ds(pl.multiple_of(h_ref[n] * group, group), group)
            refs[4][:, span] = refs[n][...]

    return pl.pallas_call(
        kernel,
        out_shape=jax.ShapeDtypeStruct((tokens, 4 * group), jnp.bfloat16),
        in_specs=[SMEM] + [VMEM] * 4,
        out_specs=VMEM,
        name="unpack_queries",
    )(heads, *parts)


def gradient(where, turned, mine, theirs, error):
    devices, rows, tokens = turned.shape
    width = mine.shape[2]

    def kernel(at, f_ref, m_ref, t_ref, e_ref, out_ref, low_ref):
        core = at[0]
        total = e_ref[...]
        for c in range(devices // 2):
            total = total + jnp.dot(
                f_ref[2 * c + core], m_ref[c], preferred_element_type=jnp.float32
            )
            total = total + jnp.dot(
                f_ref[2 * c + 1 - core], t_ref[c], preferred_element_type=jnp.float32
            )
        out_ref[...] = total
        low_ref[...] = total.astype(jnp.bfloat16)

    return pl.pallas_call(
        kernel,
        out_shape=[
            jax.ShapeDtypeStruct((rows, width), jnp.float32),
            jax.ShapeDtypeStruct((rows, width), jnp.bfloat16),
        ],
        in_specs=[SMEM] + [VMEM] * 4,
        out_specs=[VMEM] * 2,
        compiler_params=pltpu.CompilerParams(vmem_limit_bytes=32 * 1024 * 1024),
        name="gradient",
    )(where, turned, mine, theirs, error)


def finish(where, p_sum, mine, theirs, combined, replicas):
    rows, width = combined.shape
    size = p_sum.shape[1]
    half, part = width // 2, size // 2
    tiles = size // 8
    shape = (8, size)

    def kernel(at, p_ref, m_ref, t_ref, c_ref, comp_ref, q_ref, new_ref, gram_ref, inv_ref, all_ref):
        core = at[0]
        for x, who in ((m_ref, core), (t_ref, 1 - core)):
            all_ref[pl.ds(pl.multiple_of(who * half, half), half), :] = x[:half, :]
            gram_ref[pl.ds(pl.multiple_of(who * part, part), part), :] = (
                x[half : half + part, :]
                + x[half + part : half + 2 * part, :]
                + x[half + 2 * part :, :]
            )
        lane = lax.broadcasted_iota(jnp.int32, shape, 1)
        sub = lax.broadcasted_iota(jnp.int32, shape, 0)
        left = [gram_ref[8 * t : 8 * t + 8, :] for t in range(tiles)]
        right = [jnp.where(lane == sub + 8 * t, 1.0, 0.0) for t in range(tiles)]
        def row(x, r):
            return jnp.broadcast_to(x[r : r + 1, :], shape)

        for p in range(tiles):
            spread = [
                [
                    jnp.broadcast_to(left[t][:, 8 * p + k : 8 * p + k + 1], shape)
                    for k in range(8)
                ]
                for t in range(p, tiles)
            ]
            for k in range(8):
                pivot = spread[0][k]
                root = lax.rsqrt(row(pivot, k))
                row_l = row(left[p], k) * root
                row_r = row(right[p], k) * root
                inv_ref[8 * p + k : 8 * p + k + 1, :] = row_r[0:1]
                factors = [row(pivot, m) * root for m in range(k + 1, 8)]
                for t in range(p, tiles):
                    x = spread[t - p][k] * root
                    for m in range(k + 1, 8):
                        spread[t - p][m] = spread[t - p][m] - x * factors[m - k - 1]
                    left[t] = left[t] - x * row_l
                    right[t] = right[t] - x * row_r

        def product(x, y):
            return lax.dot_general(
                x, y, NT, precision=HIGHEST, preferred_element_type=jnp.float32
            )

        inv = inv_ref[...]
        q = product(all_ref[...], inv) * (1.0 / replicas)
        q_ref[...] = q
        out = product(product(p_ref[...], inv), q)
        comp_ref[...] = out
        new_ref[0] = c_ref[...] - out

    return pl.pallas_call(
        kernel,
        out_shape=[
            jax.ShapeDtypeStruct((rows, width), jnp.float32),
            jax.ShapeDtypeStruct((width, size), jnp.float32),
            jax.ShapeDtypeStruct((1, rows, width), jnp.float32),
        ],
        in_specs=[SMEM] + [VMEM] * 4,
        out_specs=[VMEM] * 3,
        scratch_shapes=[
            pltpu.VMEM((size, size), jnp.float32),
            pltpu.VMEM((size, size), jnp.float32),
            pltpu.VMEM((width, size), jnp.float32),
        ],
        compiler_params=pltpu.CompilerParams(vmem_limit_bytes=32 * 1024 * 1024),
        name="finish",
    )(where, p_sum, mine, theirs, combined)


def body(queries, keys, values, d_out, features, doc_start, error, q_init):
    tokens = queries.shape[0]
    width_kv = keys.shape[1]
    group = queries.shape[1] // (width_kv // HEAD)
    chips = lax.axis_size("chip")
    devices = 2 * chips
    replicas = lax.axis_size("dp")
    core = lax.axis_index("core")
    chip = lax.axis_index("chip")
    upper = (chip >= chips // 2).astype(jnp.int32)
    f32, bf16 = jnp.float32, jnp.bfloat16
    ctx = ("chip", "core")

    def swap(x):
        return lax.ppermute(x, "core", [(0, 1), (1, 0)])

    def piece(x, size, index, axis=1):
        return lax.dynamic_slice_in_dim(x, index * size, size, axis)

    def move(x, cross, turn):
        pairs = []
        for c in range(chips):
            for h in range(2):
                to = (chips - 1 - c if cross else c) * 2 + (1 - h if turn else h)
                pairs.append((2 * c + h, to))
        return lax.ppermute(x, ctx, pairs)

    def exchange(x, axis):
        return lax.all_to_all(x, axis, 0, 0)

    def spread(x, axis, size):
        return exchange(jnp.broadcast_to(x[None], (size,) + x.shape), axis)

    def head_of(cross, turn):
        return 2 * (1 - core if turn else core) + (1 - upper if cross else upper)

    ways = [(False, False), (False, True), (True, False), (True, True)]
    heads = jnp.stack([head_of(*way) for way in ways]).astype(jnp.int32)
    kv = exchange(pack_keys(keys, values, doc_start[None, :], devices), ctx)
    parts = pack_queries(heads, queries, d_out, group)
    parts = [parts[0]] + [move(x, *way) for x, way in zip(parts[1:], ways[1:])]

    rows = features.shape[1] // devices
    feat = jnp.transpose(features).reshape(devices, rows, tokens)
    kv, feat = lax.optimization_barrier((kv, feat))
    feat = exchange(feat, ctx)

    where = jnp.stack([core, chip, chips - 1 - chip]).astype(jnp.int32)
    dq, dkv = attention(where, parts, kv)
    dkv, feat = lax.optimization_barrier((dkv, feat))

    home = exchange(dkv.reshape(devices, tokens, 2 * HEAD), ctx)
    home = home.reshape(2, chips // 2, 2, tokens, 2 * HEAD).astype(f32)
    home = jnp.sum(home, axis=1).astype(bf16)
    home = [home[0, 0], home[1, 0], home[0, 1], home[1, 1]]
    d_key = jnp.concatenate([x[:, :HEAD] for x in home], axis=1)
    d_value = jnp.concatenate([x[:, HEAD:] for x in home], axis=1)
    dk_mine = spread(d_key, "chip", chips)
    dk_theirs = swap(dk_mine)
    combined, low = gradient(where, feat, dk_mine, dk_theirs, error.reshape(rows, width_kv))

    low, dq = lax.optimization_barrier((low, dq))
    shares = exchange(low.reshape(replicas, rows // replicas, width_kv), "dp")
    back = [dq[:tokens]] + [
        move(dq[n * tokens : (n + 1) * tokens], *ways[n]) for n in range(1, 4)
    ]
    share = jnp.sum(shares.astype(f32), axis=0).astype(bf16)
    share, *back = lax.optimization_barrier((share, *back))
    d_query = unpack_queries(heads, back, group)
    total = spread(share, "dp", replicas).reshape(rows, width_kv)

    total = total.astype(f32)
    p_sum = jnp.dot(total, q_init, precision=HIGHEST)
    gram = lax.dot_general(p_sum, p_sum, TN, precision=HIGHEST)
    moment = lax.dot_general(total, p_sum, TN, precision=HIGHEST)
    half, part = width_kv // 2, q_init.shape[1] // 2

    def share_of(who):
        return jnp.concatenate([piece(moment, half, who, 0), piece(gram, part, who, 0)], axis=0)

    sums = share_of(core) + swap(share_of(1 - core))
    gram = sums[half:]
    high = lax.reduce_precision(gram, 8, 7)
    mid = lax.reduce_precision(gram - high, 8, 7)
    low = gram - high - mid
    sums = jnp.concatenate([sums[:half], high, mid, low], axis=0).astype(bf16)
    sums = spread(sums, "chip", chips)
    sums, d_query, d_value = lax.optimization_barrier((sums, d_query, d_value))
    sums = jnp.sum(sums.astype(f32), axis=0)
    compressed, q_factor, new_error = finish(where, p_sum, sums, swap(sums), combined, replicas)
    return (d_query, d_key, d_value, compressed, q_factor, new_error)


def solution(mesh):
    replicas, ctx = mesh.devices.shape
    parts = Mesh(mesh.devices.reshape(replicas, ctx // 2, 2), ("dp", "chip", "core"))
    everywhere = ("dp", "chip", "core")
    tokens = P(everywhere, None)
    in_specs = (
        tokens, tokens, tokens, tokens, tokens, P(everywhere), P("dp", ("chip", "core"), None), P(),
    )
    out_specs = (
        tokens, tokens, tokens, P(("chip", "core"), None), P(), P("dp", ("chip", "core"), None),
    )
    return jax.shard_map(body, mesh=parts, in_specs=in_specs, out_specs=out_specs, check_vma=False)
```

```python
import math

import jax
import jax.numpy as jnp
from jax import lax
from jax.experimental import pallas as pl
from jax.experimental.pallas import tpu as pltpu
from jax.sharding import Mesh
from jax.sharding import PartitionSpec as P

HEAD = 128
NEG_FILL = -1e30
LOG2E = 1.4426950408889634
HIGHEST = lax.Precision.HIGHEST
TN = (((0,), (0,)), ((), ()))
NT = (((1,), (1,)), ((), ()))
HEADS_AT_ONCE = 6


def attention(where, parts, kv):
    devices, padded, _ = kv.shape
    tokens = HEAD
    block = 2 * tokens
    chips = devices // 2
    length = devices * tokens
    heads = parts[0].shape[1] // (2 * HEAD)
    steps = heads // HEADS_AT_ONCE
    wide = HEADS_AT_ONCE * HEAD
    columns = HEADS_AT_ONCE * block
    scale = 1.0 / math.sqrt(HEAD)
    power = scale * LOG2E

    def kernel(
        at, q0, q1, q2, q3, g0, g1, g2, g3, k_ref, v_ref, dq_ref, dkv_ref,
        s_scr, d_scr, bias, k_turned, dq_acc, dk_acc, dv_acc,
    ):
        step = pl.program_id(0)
        core = at[0]
        chip = at[1 + step // steps]

        def place(index):
            return jnp.where(index < tokens, index + core * tokens, index - core * tokens)

        def starts(device):
            high = k_ref[device, tokens : tokens + 1, :].astype(jnp.float32)
            low = v_ref[device, tokens : tokens + 1, :].astype(jnp.float32)
            return high * 64.0 + low

        start = jnp.concatenate(
            [starts(2 * chip + core), starts(2 * chip + 1 - core)], axis=1
        )
        first = jnp.min(start).astype(jnp.int32) // block

        def span_of(j):
            return pl.ds(pl.multiple_of(j * block, block), block)

        def rows_of(ref, j):
            return ref[pl.ds(2 * j, 2), :tokens, :].reshape(block, HEAD)

        @pl.when(lax.rem(step, steps) == 0)
        def _():
            q_pos = chip * block + place(lax.broadcasted_iota(jnp.int32, (block, block), 1))
            k_off = lax.broadcasted_iota(jnp.int32, (block, block), 0)
            begin = start.astype(jnp.int32)

            def fill(j, _):
                k_pos = j * block + k_off
                ok = (k_pos <= q_pos) & (k_pos >= begin)
                bias[span_of(j), :] = jnp.where(ok, 0.0, NEG_FILL)
                return 0

            lax.fori_loop(first, chip + 1, fill, 0)

        @pl.when(step == 0)
        def _():
            dk_acc[...] = jnp.zeros_like(dk_acc)
            dv_acc[...] = jnp.zeros_like(dv_acc)
            for j in range(chips):
                k_turned[j] = (
                    k_ref[2 * j : 2 * j + 2, :tokens, :].reshape(block, HEAD).astype(jnp.float32).T
                ).astype(jnp.bfloat16)

        def stacked(a, b, c, d):
            x = jnp.where(step < steps, a[...], c[...])
            y = jnp.where(step < steps, b[...], d[...])
            rows = []
            for n in range(HEADS_AT_ONCE):
                rows += [x[:, n * HEAD : (n + 1) * HEAD], y[:, n * HEAD : (n + 1) * HEAD]]
            return jnp.concatenate(rows, axis=0)

        q = stacked(q0, q1, q2, q3)
        g = stacked(g0, g1, g2, g3)

        def fold(x):
            return x.reshape(block // 8, 8, columns)

        def score_step(j, top):
            s = lax.dot_general(rows_of(k_ref, j), q, NT, preferred_element_type=jnp.float32)
            b = bias[span_of(j), :]
            s = s + jnp.concatenate([b] * HEADS_AT_ONCE, axis=1)
            s_scr[span_of(j), :] = s
            return jnp.maximum(top, jnp.max(fold(s), axis=0))

        top = lax.fori_loop(
            first, chip + 1, score_step, jnp.full((8, columns), NEG_FILL, jnp.float32)
        )
        top = jnp.max(top, axis=0, keepdims=True)

        def prob_step(j, carry):
            total, mix = carry
            span = span_of(j)
            p = jnp.exp2((s_scr[span, :] - top) * power)
            d = lax.dot_general(rows_of(v_ref, j), g, NT, preferred_element_type=jnp.float32)
            s_scr[span, :] = p
            d_scr[span, :] = d
            return (total + jnp.sum(fold(p), axis=0), mix + jnp.sum(fold(p * d), axis=0))

        zero = jnp.zeros((8, columns), jnp.float32)
        total, mix = lax.fori_loop(first, chip + 1, prob_step, (zero, zero))
        inverse = 1.0 / jnp.sum(total, axis=0, keepdims=True)
        mix = jnp.sum(mix, axis=0, keepdims=True) * inverse
        dq_acc[...] = jnp.zeros_like(dq_acc)

        def grad_step(j, _):
            span = span_of(j)
            p = s_scr[span, :] * inverse
            ds = (p * (d_scr[span, :] - mix)).astype(jnp.bfloat16)
            low = p.astype(jnp.bfloat16)
            dv_acc[span, :] += jnp.dot(low, g, preferred_element_type=jnp.float32)
            dk_acc[span, :] += jnp.dot(ds, q, preferred_element_type=jnp.float32)
            dq_acc[...] += jnp.dot(k_turned[j], ds, preferred_element_type=jnp.float32)
            return 0

        lax.fori_loop(first, chip + 1, grad_step, 0)
        dq = (dq_acc[...] * scale).T.astype(jnp.bfloat16)
        for n in range(HEADS_AT_ONCE):
            dq_ref[:, n * HEAD : (n + 1) * HEAD] = dq[n * block : (n + 1) * block]

        @pl.when(step == 2 * steps - 1)
        def _():
            dkv_ref[:, :HEAD] = (dk_acc[...] * scale).astype(jnp.bfloat16)
            dkv_ref[:, HEAD:] = dv_acc[...].astype(jnp.bfloat16)

    whole = pl.BlockSpec((length, 2 * HEAD), lambda s, at: (0, 0))
    queries_at = pl.BlockSpec((block, wide), lambda s, at: (s // steps, s % steps))
    flops = 5 * 2 * length * block * heads * HEAD
    return pl.pallas_call(
        kernel,
        grid_spec=pltpu.PrefetchScalarGridSpec(
            num_scalar_prefetch=1,
            grid=(2 * steps,),
            in_specs=[
                *[pl.BlockSpec((tokens, wide), lambda s, at: (0, s % steps))] * 4,
                *[pl.BlockSpec((tokens, wide), lambda s, at: (0, steps + s % steps))] * 4,
                pl.BlockSpec((devices, padded, HEAD), lambda s, at: (0, 0, 0)),
                pl.BlockSpec((devices, padded, HEAD), lambda s, at: (0, 0, 1)),
            ],
            out_specs=[queries_at, whole],
            scratch_shapes=[
                pltpu.VMEM((length, columns), jnp.float32),
                pltpu.VMEM((length, columns), jnp.float32),
                pltpu.VMEM((length, block), jnp.float32),
                pltpu.VMEM((chips, HEAD, block), jnp.bfloat16),
                pltpu.VMEM((HEAD, columns), jnp.float32),
                pltpu.VMEM((length, HEAD), jnp.float32),
                pltpu.VMEM((length, HEAD), jnp.float32),
            ],
        ),
        out_shape=[
            jax.ShapeDtypeStruct((2 * block, heads * HEAD), jnp.bfloat16),
            jax.ShapeDtypeStruct((length, 2 * HEAD), jnp.bfloat16),
        ],
        compiler_params=pltpu.CompilerParams(
            dimension_semantics=("arbitrary",), vmem_limit_bytes=40 * 1024 * 1024
        ),
        cost_estimate=pl.CostEstimate(
            flops=8 * flops, bytes_accessed=8 * 1024 * 1024, transcendentals=0
        ),
        name="attention",
    )(where, *parts, *parts, kv, kv)


VMEM = pl.BlockSpec(memory_space=pltpu.VMEM)
SMEM = pl.BlockSpec(memory_space=pltpu.SMEM)


def pack_keys(keys, values, starts, devices):
    tokens = keys.shape[0]

    def kernel(k_ref, v_ref, s_ref, out_ref):
        start = s_ref[...]
        high = jnp.right_shift(start, 6).astype(jnp.float32)
        low = jnp.bitwise_and(start, 63).astype(jnp.float32)
        row = jnp.concatenate([high, low], axis=1)
        first = lax.broadcasted_iota(jnp.int32, (16, 2 * tokens), 0) == 0
        extra = jnp.where(first, row, 0.0).astype(jnp.bfloat16)
        for n in range(devices):
            h = 2 * (n % 2) + (n >= devices // 2)
            out_ref[n, :tokens, :HEAD] = k_ref[:, h * HEAD : (h + 1) * HEAD]
            out_ref[n, :tokens, HEAD:] = v_ref[:, h * HEAD : (h + 1) * HEAD]
            out_ref[n, tokens:, :] = extra

    return pl.pallas_call(
        kernel,
        out_shape=jax.ShapeDtypeStruct((devices, tokens + 16, 2 * HEAD), jnp.bfloat16),
        in_specs=[VMEM] * 3,
        out_specs=VMEM,
        name="pack_keys",
    )(keys, values, starts)


def pack_queries(heads, queries, d_out, group):
    tokens = queries.shape[0]

    def kernel(h_ref, q_ref, g_ref, *outs):
        for n, out in enumerate(outs):
            span = pl.ds(pl.multiple_of(h_ref[n] * group, group), group)
            out[:, :group] = q_ref[:, span]
            out[:, group:] = g_ref[:, span]

    return pl.pallas_call(
        kernel,
        out_shape=[jax.ShapeDtypeStruct((tokens, 2 * group), jnp.bfloat16)] * 4,
        in_specs=[SMEM, VMEM, VMEM],
        out_specs=[VMEM] * 4,
        name="pack_queries",
    )(heads, queries, d_out)


def unpack_queries(heads, parts, group):
    tokens = parts[0].shape[0]

    def kernel(h_ref, *refs):
        for n in range(4):
            span = pl.ds(pl.multiple_of(h_ref[n] * group, group), group)
            refs[4][:, span] = refs[n][...]

    return pl.pallas_call(
        kernel,
        out_shape=jax.ShapeDtypeStruct((tokens, 4 * group), jnp.bfloat16),
        in_specs=[SMEM] + [VMEM] * 4,
        out_specs=VMEM,
        name="unpack_queries",
    )(heads, *parts)


def gradient(where, turned, mine, theirs, error):
    devices, rows, tokens = turned.shape
    width = mine.shape[2]

    def kernel(at, f_ref, m_ref, t_ref, e_ref, out_ref, low_ref):
        core = at[0]
        total = e_ref[...]
        for c in range(devices // 2):
            total = total + jnp.dot(
                f_ref[2 * c + core], m_ref[c], preferred_element_type=jnp.float32
            )
            total = total + jnp.dot(
                f_ref[2 * c + 1 - core], t_ref[c], preferred_element_type=jnp.float32
            )
        out_ref[...] = total
        low_ref[...] = total.astype(jnp.bfloat16)

    return pl.pallas_call(
        kernel,
        out_shape=[
            jax.ShapeDtypeStruct((rows, width), jnp.float32),
            jax.ShapeDtypeStruct((rows, width), jnp.bfloat16),
        ],
        in_specs=[SMEM] + [VMEM] * 4,
        out_specs=[VMEM] * 2,
        compiler_params=pltpu.CompilerParams(vmem_limit_bytes=32 * 1024 * 1024),
        name="gradient",
    )(where, turned, mine, theirs, error)


def finish(where, p_sum, mine, theirs, combined, replicas):
    rows, width = combined.shape
    size = p_sum.shape[1]
    half, part = width // 2, size // 2
    tiles = size // 8
    shape = (8, size)

    def kernel(at, p_ref, m_ref, t_ref, c_ref, comp_ref, q_ref, new_ref, gram_ref, inv_ref, all_ref):
        core = at[0]
        for x, who in ((m_ref, core), (t_ref, 1 - core)):
            all_ref[pl.ds(pl.multiple_of(who * half, half), half), :] = x[:half, :]
            gram_ref[pl.ds(pl.multiple_of(who * part, part), part), :] = (
                x[half : half + part, :]
                + x[half + part : half + 2 * part, :]
                + x[half + 2 * part :, :]
            )
        lane = lax.broadcasted_iota(jnp.int32, shape, 1)
        sub = lax.broadcasted_iota(jnp.int32, shape, 0)
        left = [gram_ref[8 * t : 8 * t + 8, :] for t in range(tiles)]
        right = [jnp.where(lane == sub + 8 * t, 1.0, 0.0) for t in range(tiles)]
        def row(x, r):
            return jnp.broadcast_to(x[r : r + 1, :], shape)

        for p in range(tiles):
            spread = [
                [
                    jnp.broadcast_to(left[t][:, 8 * p + k : 8 * p + k + 1], shape)
                    for k in range(8)
                ]
                for t in range(p, tiles)
            ]
            for k in range(8):
                pivot = spread[0][k]
                root = lax.rsqrt(row(pivot, k))
                row_l = row(left[p], k) * root
                row_r = row(right[p], k) * root
                inv_ref[8 * p + k : 8 * p + k + 1, :] = row_r[0:1]
                factors = [row(pivot, m) * root for m in range(k + 1, 8)]
                for t in range(p, tiles):
                    x = spread[t - p][k] * root
                    for m in range(k + 1, 8):
                        spread[t - p][m] = spread[t - p][m] - x * factors[m - k - 1]
                    left[t] = left[t] - x * row_l
                    right[t] = right[t] - x * row_r

        def product(x, y):
            return lax.dot_general(
                x, y, NT, precision=HIGHEST, preferred_element_type=jnp.float32
            )

        inv = inv_ref[...]
        q = product(all_ref[...], inv) * (1.0 / replicas)
        q_ref[...] = q
        out = product(product(p_ref[...], inv), q)
        comp_ref[...] = out
        new_ref[0] = c_ref[...] - out

    return pl.pallas_call(
        kernel,
        out_shape=[
            jax.ShapeDtypeStruct((rows, width), jnp.float32),
            jax.ShapeDtypeStruct((width, size), jnp.float32),
            jax.ShapeDtypeStruct((1, rows, width), jnp.float32),
        ],
        in_specs=[SMEM] + [VMEM] * 4,
        out_specs=[VMEM] * 3,
        scratch_shapes=[
            pltpu.VMEM((size, size), jnp.float32),
            pltpu.VMEM((size, size), jnp.float32),
            pltpu.VMEM((width, size), jnp.float32),
        ],
        compiler_params=pltpu.CompilerParams(vmem_limit_bytes=32 * 1024 * 1024),
        name="finish",
    )(where, p_sum, mine, theirs, combined)


def body(queries, keys, values, d_out, features, doc_start, error, q_init):
    tokens = queries.shape[0]
    width_kv = keys.shape[1]
    group = queries.shape[1] // (width_kv // HEAD)
    chips = lax.axis_size("chip")
    devices = 2 * chips
    replicas = lax.axis_size("dp")
    core = lax.axis_index("core")
    chip = lax.axis_index("chip")
    upper = (chip >= chips // 2).astype(jnp.int32)
    f32, bf16 = jnp.float32, jnp.bfloat16
    ctx = ("chip", "core")

    def swap(x):
        return lax.ppermute(x, "core", [(0, 1), (1, 0)])

    def piece(x, size, index, axis=1):
        return lax.dynamic_slice_in_dim(x, index * size, size, axis)

    def move(x, cross, turn):
        pairs = []
        for c in range(chips):
            for h in range(2):
                to = (chips - 1 - c if cross else c) * 2 + (1 - h if turn else h)
                pairs.append((2 * c + h, to))
        return lax.ppermute(x, ctx, pairs)

    def exchange(x, axis):
        return lax.all_to_all(x, axis, 0, 0)

    def spread(x, axis, size):
        return exchange(jnp.broadcast_to(x[None], (size,) + x.shape), axis)

    def head_of(cross, turn):
        return 2 * (1 - core if turn else core) + (1 - upper if cross else upper)

    ways = [(False, False), (False, True), (True, False), (True, True)]
    heads = jnp.stack([head_of(*way) for way in ways]).astype(jnp.int32)
    kv = exchange(pack_keys(keys, values, doc_start[None, :], devices), ctx)
    parts = pack_queries(heads, queries, d_out, group)
    parts = [parts[0]] + [move(x, *way) for x, way in zip(parts[1:], ways[1:])]

    rows = features.shape[1] // devices
    feat = jnp.transpose(features).reshape(devices, rows, tokens)
    kv, feat = lax.optimization_barrier((kv, feat))
    feat = exchange(feat, ctx)

    where = jnp.stack([core, chip, chips - 1 - chip]).astype(jnp.int32)
    dq, dkv = attention(where, parts, kv)
    dkv, feat = lax.optimization_barrier((dkv, feat))

    home = exchange(dkv.reshape(devices, tokens, 2 * HEAD), ctx)
    home = home.reshape(2, chips // 2, 2, tokens, 2 * HEAD).astype(f32)
    home = jnp.sum(home, axis=1).astype(bf16)
    home = [home[0, 0], home[1, 0], home[0, 1], home[1, 1]]
    d_key = jnp.concatenate([x[:, :HEAD] for x in home], axis=1)
    d_value = jnp.concatenate([x[:, HEAD:] for x in home], axis=1)
    dk_mine = spread(d_key, "chip", chips)
    dk_theirs = swap(dk_mine)
    combined, low = gradient(where, feat, dk_mine, dk_theirs, error.reshape(rows, width_kv))

    low, dq = lax.optimization_barrier((low, dq))
    shares = exchange(low.reshape(replicas, rows // replicas, width_kv), "dp")
    back = [dq[:tokens]] + [
        move(dq[n * tokens : (n + 1) * tokens], *ways[n]) for n in range(1, 4)
    ]
    share = jnp.sum(shares.astype(f32), axis=0).astype(bf16)
    total = spread(share, "dp", replicas).reshape(rows, width_kv)

    total = total.astype(f32)
    p_sum = jnp.dot(total, q_init, precision=HIGHEST)
    gram = lax.dot_general(p_sum, p_sum, TN, precision=HIGHEST)
    moment = lax.dot_general(total, p_sum, TN, precision=HIGHEST)
    half, part = width_kv // 2, q_init.shape[1] // 2

    def share_of(who):
        return jnp.concatenate([piece(moment, half, who, 0), piece(gram, part, who, 0)], axis=0)

    sums = share_of(core) + swap(share_of(1 - core))
    gram = sums[half:]
    high = lax.reduce_precision(gram, 8, 7)
    mid = lax.reduce_precision(gram - high, 8, 7)
    low = gram - high - mid
    sums = jnp.concatenate([sums[:half], high, mid, low], axis=0).astype(bf16)
    sums, *back = lax.optimization_barrier((sums, *back))
    sums = spread(sums, "chip", chips)
    d_query = unpack_queries(heads, back, group)
    sums, d_query, d_value = lax.optimization_barrier((sums, d_query, d_value))
    sums = jnp.sum(sums.astype(f32), axis=0)
    compressed, q_factor, new_error = finish(where, p_sum, sums, swap(sums), combined, replicas)
    return (d_query, d_key, d_value, compressed, q_factor, new_error)


def solution(mesh):
    replicas, ctx = mesh.devices.shape
    parts = Mesh(mesh.devices.reshape(replicas, ctx // 2, 2), ("dp", "chip", "core"))
    everywhere = ("dp", "chip", "core")
    tokens = P(everywhere, None)
    in_specs = (
        tokens, tokens, tokens, tokens, tokens, P(everywhere), P("dp", ("chip", "core"), None), P(),
    )
    out_specs = (
        tokens, tokens, tokens, P(("chip", "core"), None), P(), P("dp", ("chip", "core"), None),
    )
    return jax.shard_map(body, mesh=parts, in_specs=in_specs, out_specs=out_specs, check_vma=False)
```

```python
import math

import jax
import jax.numpy as jnp
from jax import lax
from jax.experimental import pallas as pl
from jax.experimental.pallas import tpu as pltpu
from jax.sharding import Mesh
from jax.sharding import PartitionSpec as P

HEAD = 128
NEG_FILL = -1e30
LOG2E = 1.4426950408889634
HIGHEST = lax.Precision.HIGHEST
TN = (((0,), (0,)), ((), ()))
NT = (((1,), (1,)), ((), ()))
HEADS_AT_ONCE = 6


def attention(where, parts, kv):
    devices, padded, _ = kv.shape
    tokens = HEAD
    block = 2 * tokens
    chips = devices // 2
    length = devices * tokens
    heads = parts[0].shape[1] // (2 * HEAD)
    steps = heads // HEADS_AT_ONCE
    wide = HEADS_AT_ONCE * HEAD
    columns = HEADS_AT_ONCE * block
    scale = 1.0 / math.sqrt(HEAD)
    power = scale * LOG2E

    def kernel(
        at, q0, q1, q2, q3, g0, g1, g2, g3, k_ref, v_ref, dq_ref, dkv_ref,
        s_scr, d_scr, bias, k_turned, dq_acc, dk_acc, dv_acc,
    ):
        step = pl.program_id(0)
        core = at[0]
        chip = at[1 + step // steps]

        def place(index):
            return jnp.where(index < tokens, index + core * tokens, index - core * tokens)

        def starts(device):
            high = k_ref[device, tokens : tokens + 1, :].astype(jnp.float32)
            low = v_ref[device, tokens : tokens + 1, :].astype(jnp.float32)
            return high * 64.0 + low

        start = jnp.concatenate(
            [starts(2 * chip + core), starts(2 * chip + 1 - core)], axis=1
        )
        first = jnp.min(start).astype(jnp.int32) // block

        def span_of(j):
            return pl.ds(pl.multiple_of(j * block, block), block)

        def rows_of(ref, j):
            return ref[pl.ds(2 * j, 2), :tokens, :].reshape(block, HEAD)

        @pl.when(lax.rem(step, steps) == 0)
        def _():
            q_pos = chip * block + place(lax.broadcasted_iota(jnp.int32, (block, block), 1))
            k_off = lax.broadcasted_iota(jnp.int32, (block, block), 0)
            begin = start.astype(jnp.int32)

            def fill(j, _):
                k_pos = j * block + k_off
                ok = (k_pos <= q_pos) & (k_pos >= begin)
                bias[span_of(j), :] = jnp.where(ok, 0.0, NEG_FILL)
                return 0

            lax.fori_loop(first, chip + 1, fill, 0)

        @pl.when(step == 0)
        def _():
            dk_acc[...] = jnp.zeros_like(dk_acc)
            dv_acc[...] = jnp.zeros_like(dv_acc)
            for j in range(chips):
                k_turned[j] = (
                    k_ref[2 * j : 2 * j + 2, :tokens, :].reshape(block, HEAD).astype(jnp.float32).T
                ).astype(jnp.bfloat16)

        def stacked(a, b, c, d):
            x = jnp.where(step < steps, a[...], c[...])
            y = jnp.where(step < steps, b[...], d[...])
            rows = []
            for n in range(HEADS_AT_ONCE):
                rows += [x[:, n * HEAD : (n + 1) * HEAD], y[:, n * HEAD : (n + 1) * HEAD]]
            return jnp.concatenate(rows, axis=0)

        q = stacked(q0, q1, q2, q3)
        g = stacked(g0, g1, g2, g3)

        def fold(x):
            return x.reshape(block // 8, 8, columns)

        def score_step(j, top):
            s = lax.dot_general(rows_of(k_ref, j), q, NT, preferred_element_type=jnp.float32)
            b = bias[span_of(j), :]
            s = s + jnp.concatenate([b] * HEADS_AT_ONCE, axis=1)
            s_scr[span_of(j), :] = s
            return jnp.maximum(top, jnp.max(fold(s), axis=0))

        top = lax.fori_loop(
            first, chip + 1, score_step, jnp.full((8, columns), NEG_FILL, jnp.float32)
        )
        top = jnp.max(top, axis=0, keepdims=True)

        def prob_step(j, carry):
            total, mix = carry
            span = span_of(j)
            p = jnp.exp2((s_scr[span, :] - top) * power)
            d = lax.dot_general(rows_of(v_ref, j), g, NT, preferred_element_type=jnp.float32)
            s_scr[span, :] = p
            d_scr[span, :] = d
            return (total + jnp.sum(fold(p), axis=0), mix + jnp.sum(fold(p * d), axis=0))

        zero = jnp.zeros((8, columns), jnp.float32)
        total, mix = lax.fori_loop(first, chip + 1, prob_step, (zero, zero))
        inverse = 1.0 / jnp.sum(total, axis=0, keepdims=True)
        mix = jnp.sum(mix, axis=0, keepdims=True) * inverse
        dq_acc[...] = jnp.zeros_like(dq_acc)

        def grad_step(j, _):
            span = span_of(j)
            p = s_scr[span, :] * inverse
            ds = (p * (d_scr[span, :] - mix)).astype(jnp.bfloat16)
            low = p.astype(jnp.bfloat16)
            dv_acc[span, :] += jnp.dot(low, g, preferred_element_type=jnp.float32)
            dk_acc[span, :] += jnp.dot(ds, q, preferred_element_type=jnp.float32)
            dq_acc[...] += jnp.dot(k_turned[j], ds, preferred_element_type=jnp.float32)
            return 0

        lax.fori_loop(first, chip + 1, grad_step, 0)
        dq = (dq_acc[...] * scale).T.astype(jnp.bfloat16)
        for n in range(HEADS_AT_ONCE):
            dq_ref[:, n * HEAD : (n + 1) * HEAD] = dq[n * block : (n + 1) * block]

        @pl.when(step == 2 * steps - 1)
        def _():
            dkv_ref[:, :HEAD] = (dk_acc[...] * scale).astype(jnp.bfloat16)
            dkv_ref[:, HEAD:] = dv_acc[...].astype(jnp.bfloat16)

    whole = pl.BlockSpec((length, 2 * HEAD), lambda s, at: (0, 0))
    queries_at = pl.BlockSpec((block, wide), lambda s, at: (s // steps, s % steps))
    flops = 5 * 2 * length * block * heads * HEAD
    return pl.pallas_call(
        kernel,
        grid_spec=pltpu.PrefetchScalarGridSpec(
            num_scalar_prefetch=1,
            grid=(2 * steps,),
            in_specs=[
                *[pl.BlockSpec((tokens, wide), lambda s, at: (0, s % steps))] * 4,
                *[pl.BlockSpec((tokens, wide), lambda s, at: (0, steps + s % steps))] * 4,
                pl.BlockSpec((devices, padded, HEAD), lambda s, at: (0, 0, 0)),
                pl.BlockSpec((devices, padded, HEAD), lambda s, at: (0, 0, 1)),
            ],
            out_specs=[queries_at, whole],
            scratch_shapes=[
                pltpu.VMEM((length, columns), jnp.float32),
                pltpu.VMEM((length, columns), jnp.float32),
                pltpu.VMEM((length, block), jnp.float32),
                pltpu.VMEM((chips, HEAD, block), jnp.bfloat16),
                pltpu.VMEM((HEAD, columns), jnp.float32),
                pltpu.VMEM((length, HEAD), jnp.float32),
                pltpu.VMEM((length, HEAD), jnp.float32),
            ],
        ),
        out_shape=[
            jax.ShapeDtypeStruct((2 * block, heads * HEAD), jnp.bfloat16),
            jax.ShapeDtypeStruct((length, 2 * HEAD), jnp.bfloat16),
        ],
        compiler_params=pltpu.CompilerParams(
            dimension_semantics=("arbitrary",), vmem_limit_bytes=40 * 1024 * 1024
        ),
        cost_estimate=pl.CostEstimate(
            flops=8 * flops, bytes_accessed=8 * 1024 * 1024, transcendentals=0
        ),
        name="attention",
    )(where, *parts, *parts, kv, kv)


VMEM = pl.BlockSpec(memory_space=pltpu.VMEM)
SMEM = pl.BlockSpec(memory_space=pltpu.SMEM)


def pack_keys(keys, values, starts, devices):
    tokens = keys.shape[0]

    def kernel(k_ref, v_ref, s_ref, out_ref):
        start = s_ref[...]
        high = jnp.right_shift(start, 6).astype(jnp.float32)
        low = jnp.bitwise_and(start, 63).astype(jnp.float32)
        row = jnp.concatenate([high, low], axis=1)
        first = lax.broadcasted_iota(jnp.int32, (16, 2 * tokens), 0) == 0
        extra = jnp.where(first, row, 0.0).astype(jnp.bfloat16)
        for n in range(devices):
            h = 2 * (n % 2) + (n >= devices // 2)
            out_ref[n, :tokens, :HEAD] = k_ref[:, h * HEAD : (h + 1) * HEAD]
            out_ref[n, :tokens, HEAD:] = v_ref[:, h * HEAD : (h + 1) * HEAD]
            out_ref[n, tokens:, :] = extra

    return pl.pallas_call(
        kernel,
        out_shape=jax.ShapeDtypeStruct((devices, tokens + 16, 2 * HEAD), jnp.bfloat16),
        in_specs=[VMEM] * 3,
        out_specs=VMEM,
        name="pack_keys",
    )(keys, values, starts)


def pack_queries(heads, queries, d_out, group):
    tokens = queries.shape[0]

    def kernel(h_ref, q_ref, g_ref, *outs):
        for n, out in enumerate(outs):
            span = pl.ds(pl.multiple_of(h_ref[n] * group, group), group)
            out[:, :group] = q_ref[:, span]
            out[:, group:] = g_ref[:, span]

    return pl.pallas_call(
        kernel,
        out_shape=[jax.ShapeDtypeStruct((tokens, 2 * group), jnp.bfloat16)] * 4,
        in_specs=[SMEM, VMEM, VMEM],
        out_specs=[VMEM] * 4,
        name="pack_queries",
    )(heads, queries, d_out)


def unpack_queries(heads, parts, group):
    tokens = parts[0].shape[0]

    def kernel(h_ref, *refs):
        for n in range(4):
            span = pl.ds(pl.multiple_of(h_ref[n] * group, group), group)
            refs[4][:, span] = refs[n][...]

    return pl.pallas_call(
        kernel,
        out_shape=jax.ShapeDtypeStruct((tokens, 4 * group), jnp.bfloat16),
        in_specs=[SMEM] + [VMEM] * 4,
        out_specs=VMEM,
        name="unpack_queries",
    )(heads, *parts)


def gradient(where, turned, mine, theirs, error):
    devices, rows, tokens = turned.shape
    width = mine.shape[2]

    def kernel(at, f_ref, m_ref, t_ref, e_ref, out_ref, low_ref):
        core = at[0]
        total = e_ref[...]
        for c in range(devices // 2):
            total = total + jnp.dot(
                f_ref[2 * c + core], m_ref[c], preferred_element_type=jnp.float32
            )
            total = total + jnp.dot(
                f_ref[2 * c + 1 - core], t_ref[c], preferred_element_type=jnp.float32
            )
        out_ref[...] = total
        low_ref[...] = total.astype(jnp.bfloat16)

    return pl.pallas_call(
        kernel,
        out_shape=[
            jax.ShapeDtypeStruct((rows, width), jnp.float32),
            jax.ShapeDtypeStruct((rows, width), jnp.bfloat16),
        ],
        in_specs=[SMEM] + [VMEM] * 4,
        out_specs=[VMEM] * 2,
        compiler_params=pltpu.CompilerParams(vmem_limit_bytes=32 * 1024 * 1024),
        name="gradient",
    )(where, turned, mine, theirs, error)


def finish(where, p_sum, mine, theirs, combined, replicas):
    rows, width = combined.shape
    size = p_sum.shape[1]
    half, part = width // 2, size // 2
    tiles = size // 8
    shape = (8, size)

    def kernel(at, p_ref, m_ref, t_ref, c_ref, comp_ref, q_ref, new_ref, gram_ref, inv_ref, all_ref):
        core = at[0]
        for x, who in ((m_ref, core), (t_ref, 1 - core)):
            all_ref[pl.ds(pl.multiple_of(who * half, half), half), :] = x[:half, :]
            gram_ref[pl.ds(pl.multiple_of(who * part, part), part), :] = (
                x[half : half + part, :]
                + x[half + part : half + 2 * part, :]
                + x[half + 2 * part :, :]
            )
        lane = lax.broadcasted_iota(jnp.int32, shape, 1)
        sub = lax.broadcasted_iota(jnp.int32, shape, 0)
        left = [gram_ref[8 * t : 8 * t + 8, :] for t in range(tiles)]
        right = [jnp.where(lane == sub + 8 * t, 1.0, 0.0) for t in range(tiles)]
        def row(x, r):
            return jnp.broadcast_to(x[r : r + 1, :], shape)

        for p in range(tiles):
            spread = [
                [
                    jnp.broadcast_to(left[t][:, 8 * p + k : 8 * p + k + 1], shape)
                    for k in range(8)
                ]
                for t in range(p, tiles)
            ]
            for k in range(8):
                pivot = spread[0][k]
                root = lax.rsqrt(row(pivot, k))
                row_l = row(left[p], k) * root
                row_r = row(right[p], k) * root
                inv_ref[8 * p + k : 8 * p + k + 1, :] = row_r[0:1]
                factors = [row(pivot, m) * root for m in range(k + 1, 8)]
                for t in range(p, tiles):
                    x = spread[t - p][k] * root
                    for m in range(k + 1, 8):
                        spread[t - p][m] = spread[t - p][m] - x * factors[m - k - 1]
                    left[t] = left[t] - x * row_l
                    right[t] = right[t] - x * row_r

        def product(x, y):
            return lax.dot_general(
                x, y, NT, precision=HIGHEST, preferred_element_type=jnp.float32
            )

        inv = inv_ref[...]
        q = product(all_ref[...], inv) * (1.0 / replicas)
        q_ref[...] = q
        out = product(product(p_ref[...], inv), q)
        comp_ref[...] = out
        new_ref[0] = c_ref[...] - out

    return pl.pallas_call(
        kernel,
        out_shape=[
            jax.ShapeDtypeStruct((rows, width), jnp.float32),
            jax.ShapeDtypeStruct((width, size), jnp.float32),
            jax.ShapeDtypeStruct((1, rows, width), jnp.float32),
        ],
        in_specs=[SMEM] + [VMEM] * 4,
        out_specs=[VMEM] * 3,
        scratch_shapes=[
            pltpu.VMEM((size, size), jnp.float32),
            pltpu.VMEM((size, size), jnp.float32),
            pltpu.VMEM((width, size), jnp.float32),
        ],
        compiler_params=pltpu.CompilerParams(vmem_limit_bytes=32 * 1024 * 1024),
        name="finish",
    )(where, p_sum, mine, theirs, combined)


def body(queries, keys, values, d_out, features, doc_start, error, q_init):
    tokens = queries.shape[0]
    width_kv = keys.shape[1]
    group = queries.shape[1] // (width_kv // HEAD)
    chips = lax.axis_size("chip")
    devices = 2 * chips
    replicas = lax.axis_size("dp")
    core = lax.axis_index("core")
    chip = lax.axis_index("chip")
    upper = (chip >= chips // 2).astype(jnp.int32)
    f32, bf16 = jnp.float32, jnp.bfloat16
    ctx = ("chip", "core")

    def swap(x):
        return lax.ppermute(x, "core", [(0, 1), (1, 0)])

    def piece(x, size, index, axis=1):
        return lax.dynamic_slice_in_dim(x, index * size, size, axis)

    def move(x, cross, turn):
        pairs = []
        for c in range(chips):
            for h in range(2):
                to = (chips - 1 - c if cross else c) * 2 + (1 - h if turn else h)
                pairs.append((2 * c + h, to))
        return lax.ppermute(x, ctx, pairs)

    def exchange(x, axis):
        return lax.all_to_all(x, axis, 0, 0)

    def spread(x, axis, size):
        return exchange(jnp.broadcast_to(x[None], (size,) + x.shape), axis)

    def head_of(cross, turn):
        return 2 * (1 - core if turn else core) + (1 - upper if cross else upper)

    ways = [(False, False), (False, True), (True, False), (True, True)]
    heads = jnp.stack([head_of(*way) for way in ways]).astype(jnp.int32)
    kv = exchange(pack_keys(keys, values, doc_start[None, :], devices), ctx)
    parts = pack_queries(heads, queries, d_out, group)
    parts = [parts[0]] + [move(x, *way) for x, way in zip(parts[1:], ways[1:])]

    rows = features.shape[1] // devices
    feat = jnp.transpose(features).reshape(devices, rows, tokens)
    kv, feat = lax.optimization_barrier((kv, feat))
    feat = exchange(feat, ctx)

    where = jnp.stack([core, chip, chips - 1 - chip]).astype(jnp.int32)
    dq, dkv = attention(where, parts, kv)
    dkv, feat = lax.optimization_barrier((dkv, feat))

    home = exchange(dkv.reshape(devices, tokens, 2 * HEAD), ctx)
    home = home.reshape(2, chips // 2, 2, tokens, 2 * HEAD).astype(f32)
    home = jnp.sum(home, axis=1).astype(bf16)
    home = [home[0, 0], home[1, 0], home[0, 1], home[1, 1]]
    d_key = jnp.concatenate([x[:, :HEAD] for x in home], axis=1)
    d_value = jnp.concatenate([x[:, HEAD:] for x in home], axis=1)
    dk_mine = spread(d_key, "chip", chips)
    dk_theirs = swap(dk_mine)
    combined, low = gradient(where, feat, dk_mine, dk_theirs, error.reshape(rows, width_kv))

    low, dq = lax.optimization_barrier((low, dq))
    shares = exchange(low.reshape(replicas, rows // replicas, width_kv), "dp")
    near = [move(dq[n * tokens : (n + 1) * tokens], *ways[n]) for n in (1, 2)]
    share = jnp.sum(shares.astype(f32), axis=0).astype(bf16)
    share, last, *near = lax.optimization_barrier((share, dq[3 * tokens :], *near))
    total = spread(share, "dp", replicas).reshape(rows, width_kv)
    last = move(last, *ways[3])
    total, last = lax.optimization_barrier((total, last))
    back = [dq[:tokens], *near, last]

    total = total.astype(f32)
    p_sum = jnp.dot(total, q_init, precision=HIGHEST)
    gram = lax.dot_general(p_sum, p_sum, TN, precision=HIGHEST)
    moment = lax.dot_general(total, p_sum, TN, precision=HIGHEST)
    half, part = width_kv // 2, q_init.shape[1] // 2

    def share_of(who):
        return jnp.concatenate([piece(moment, half, who, 0), piece(gram, part, who, 0)], axis=0)

    sums = share_of(core) + swap(share_of(1 - core))
    gram = sums[half:]
    high = lax.reduce_precision(gram, 8, 7)
    mid = lax.reduce_precision(gram - high, 8, 7)
    low = gram - high - mid
    sums = jnp.concatenate([sums[:half], high, mid, low], axis=0).astype(bf16)
    sums = spread(sums, "chip", chips)
    d_query = unpack_queries(heads, back, group)
    sums, d_query, d_value = lax.optimization_barrier((sums, d_query, d_value))
    sums = jnp.sum(sums.astype(f32), axis=0)
    compressed, q_factor, new_error = finish(where, p_sum, sums, swap(sums), combined, replicas)
    return (d_query, d_key, d_value, compressed, q_factor, new_error)


def solution(mesh):
    replicas, ctx = mesh.devices.shape
    parts = Mesh(mesh.devices.reshape(replicas, ctx // 2, 2), ("dp", "chip", "core"))
    everywhere = ("dp", "chip", "core")
    tokens = P(everywhere, None)
    in_specs = (
        tokens, tokens, tokens, tokens, tokens, P(everywhere), P("dp", ("chip", "core"), None), P(),
    )
    out_specs = (
        tokens, tokens, tokens, P(("chip", "core"), None), P(), P("dp", ("chip", "core"), None),
    )
    return jax.shard_map(body, mesh=parts, in_specs=in_specs, out_specs=out_specs, check_vma=False)
```
